32 devices in a mesh: batch: 8 (over y, x, core), ctx: 4 (over z).
Axes of the slice: x: 2, y: 2, z: 4, core: 2. Of those that a mesh axis runs over, the one named last changes fastest.
Arguments:
- tokens: bfloat16 [16, 1024, 1600], P('batch', 'ctx'), may hold values from -8 to 8
- teacher: bfloat16 [16, 1024, 1600], P('batch', 'ctx'), may hold values from -6 to 6
- cotangent: bfloat16 [16, 1024, 1600], P('batch', 'ctx'), may hold values from -6 to 6
- valid: int32 [16, 1024], P('batch', 'ctx'), may hold values from 0 to 1, as said below
- w_query: bfloat16 [1600, 1600], P('batch', 'ctx'), may hold values from -0.15625 to 0.15625
- w_key: bfloat16 [1600, 320], P('batch', 'ctx'), may hold values from -0.15625 to 0.15625
- w_value: bfloat16 [1600, 640], P('batch', 'ctx'), may hold values from -0.15625 to 0.15625
- w_mixer: bfloat16 [1600, 6400], P('batch', 'ctx'), may hold values from -0.15625 to 0.15625
- w_output: bfloat16 [3200, 1600], P('batch', 'ctx'), may hold values from -0.109375 to 0.109375
- w_gate: bfloat16 [1600, 5504], P('batch', 'ctx'), may hold values from -0.15625 to 0.15625
- w_up: bfloat16 [1600, 5504], P('batch', 'ctx'), may hold values from -0.15625 to 0.15625
- w_down: bfloat16 [5504, 1600], P('batch', 'ctx'), may hold values from -0.15625 to 0.15625
- w_select: bfloat16 [3200, 132], P('batch'), may hold values from -0.109375 to 0.109375
- w_step: bfloat16 [100, 3200], P(None, 'batch'), may hold values from -0.625 to 0.625
- log_decay: bfloat16 [16, 3200], P(None, 'batch'), may hold values from -6 to 1
- conv_taps: bfloat16 [4, 3200], P(None, 'batch'), may hold values from -3 to 3
- conv_bias: bfloat16 [3200], P('batch'), may hold values from -2 to 2
- step_bias: bfloat16 [3200], P('batch'), may hold values from -6 to -1
- skip_gain: bfloat16 [3200], P('batch'), may hold values from 0.29882812 to 1.1953125
- beta_attn: bfloat16 [3200], P('batch'), may hold values from 0.5 to 2
- beta_ssm: bfloat16 [3200], P('batch'), may hold values from 0.5 to 2
- gain_first: bfloat16 [1600], P('batch'), may hold values from 0.5 to 1.5
- gain_second: bfloat16 [1600], P('batch'), may hold values from 0.5 to 1.5
Outputs:
- output: bfloat16 [16, 1024, 1600], P('batch', 'ctx')
- distill_loss: float32 [], replicated
- tokens_grad: bfloat16 [16, 1024, 1600], P('batch', 'ctx')
- query_grad: float32 [1600, 1600], P('batch', 'ctx')
- key_grad: float32 [1600, 320], P('batch', 'ctx')
- value_grad: float32 [1600, 640], P('batch', 'ctx')
- mixer_grad: float32 [1600, 6400], P('batch', 'ctx')
- output_grad: float32 [3200, 1600], P('batch', 'ctx')
- gate_grad: float32 [1600, 5504], P('batch', 'ctx')
- up_grad: float32 [1600, 5504], P('batch', 'ctx')
- down_grad: float32 [5504, 1600], P('batch', 'ctx')
- select_grad: float32 [3200, 132], P('batch')
- step_grad: float32 [100, 3200], P(None, 'batch')
- decay_grad: float32 [16, 3200], P(None, 'batch')
- taps_grad: float32 [4, 3200], P(None, 'batch')
- conv_bias_grad: float32 [3200], P('batch')
- step_bias_grad: float32 [3200], P('batch')
- skip_grad: float32 [3200], P('batch')
- beta_attn_grad: float32 [3200], P('batch')
- beta_ssm_grad: float32 [3200], P('batch')
- gain_first_grad: float32 [1600], P('batch')
- gain_second_grad: float32 [1600], P('batch')
The draws below stay inside these ranges and needn't reach their ends.
Inputs may be any that keep to these rules, and one draw needn't show every extreme that they name: `valid`: every sequence's first position is 1.
All inputs are finite; a program needn't handle non-finite values.
Results may differ from the reference program's by a relative error of at most 0.017.
Values may be sent and summed in bfloat16 or wider, within the bound.
A program may use at most 576 MiB of HBM per device.

```python
import math
import jax
import jax.numpy as jnp
from jax import lax

D = 1600
HEADS = 25
KV = 5
HD = 64
INNER = 3200
STATE = 16
CONV = 4
RANK = 100
FF = 5504
WINDOW = 1024
LENGTH = 1024
SEQS = 16
TOKENS = 16384
SPAN = 256


def draw_tokens(key, part):
    key = jax.random.fold_in(key, 11)
    key_base, key_dirs, key_amps = jax.random.split(key, 3)
    blocks = LENGTH // SPAN
    base = jax.random.normal(key_base, (SEQS, blocks, SPAN, D), jnp.float32)
    dirs = jax.random.normal(key_dirs, (SEQS, blocks, 1, D), jnp.float32)
    amps = jax.random.uniform(key_amps, (SEQS, blocks, 1, 1), jnp.float32, 0.3, 1.5)
    values = jnp.clip(base + amps * dirs, -8.0, 8.0)
    return values.reshape(SEQS, LENGTH, D).astype(jnp.bfloat16)


def draw_valid(key, part):
    key = jax.random.fold_in(key, 12)
    ticket = jax.random.randint(key, (SEQS, LENGTH), 0, 1000)
    level = 150 + 750 * jnp.arange(SEQS, dtype=jnp.int32) // max(SEQS - 1, 1)
    marks = (ticket < level[:, None]).astype(jnp.int32)
    first = (jnp.arange(LENGTH, dtype=jnp.int32) == 0)[None, :]
    return jnp.where(first, 1, marks).astype(jnp.int32)


def block_scale(rng, shape, shards, smallest, high):
    def one(position, parts):
        steps = jax.random.uniform(jax.random.fold_in(jax.random.fold_in(rng, 6), position), (parts,), jnp.float32, smallest / len(shards), high / len(shards))
        return jnp.repeat(jnp.exp(steps), shape[position] // parts).reshape((-1,) + (1,) * (len(shape) - position - 1))

    loudness = one(*shards[0])
    for cut in shards[1:]:
        loudness = loudness * one(*cut)
    return loudness


def gaussian(own_key, shape, width, bound, pieces=(), kind=jnp.bfloat16):
    entries = width * jax.random.normal(own_key, shape, jnp.float32)
    if pieces:
        entries = entries * block_scale(own_key, shape, pieces, -0.22, 0.18)
    return jnp.clip(entries, -bound, bound).astype(kind)


def setup_inputs(seed: int = 0) -> dict:
    streams_of = jax.random.split(jax.random.key(seed), 24)
    tokens = draw_tokens(jax.random.fold_in(streams_of[23], 71), 0)
    teacher = gaussian(streams_of[1], (SEQS, LENGTH, D), 1.0, 6.0, ((0, 8), (1, 4)))
    cotangent = gaussian(streams_of[2], (SEQS, LENGTH, D), 1.0, 6.0, ((0, 8), (1, 4)))
    valid = draw_valid(jax.random.fold_in(streams_of[23], 71), 0)
    w_query = gaussian(streams_of[4], (D, HEADS * HD), D ** -0.5, 0.15625, ((0, 8), (1, 4)))
    w_key = gaussian(streams_of[5], (D, KV * HD), D ** -0.5, 0.15625, ((0, 8), (1, 4)))
    w_value = gaussian(streams_of[6], (D, KV * (INNER // HEADS)), D ** -0.5, 0.15625, ((0, 8), (1, 4)))
    w_mixer = gaussian(streams_of[7], (D, 2 * INNER), D ** -0.5, 0.15625, ((0, 8), (1, 4)))
    w_output = gaussian(streams_of[8], (INNER, D), INNER ** -0.5, 0.109375, ((0, 8), (1, 4)))
    w_gate = gaussian(streams_of[9], (D, FF), D ** -0.5, 0.15625, ((0, 8), (1, 4)))
    w_up = gaussian(streams_of[10], (D, FF), D ** -0.5, 0.15625, ((0, 8), (1, 4)))
    w_down = gaussian(streams_of[11], (FF, D), (FF // 4) ** -0.5, 0.15625, ((0, 8), (1, 4)))
    w_select = gaussian(streams_of[12], (INNER, RANK + 2 * STATE), INNER ** -0.5, 0.109375, ((0, 8),))
    w_step = gaussian(streams_of[13], (RANK, INNER), RANK ** -0.5, 0.625, ((1, 8),))
    log_decay = jnp.clip(-6.0 + 7.0 * jax.random.uniform(streams_of[14], (STATE, INNER), jnp.float32) ** block_scale(streams_of[14], (STATE, INNER), ((1, 8),), -0.2, 0.2), -6.0, 1.0).astype(jnp.bfloat16)
    conv_taps = gaussian(streams_of[15], (CONV, INNER), CONV ** -0.5, 3.0, ((1, 8),))
    conv_bias = gaussian(streams_of[16], (INNER,), 0.3, 2.0, ((0, 8),))
    step_bias = jnp.clip(-6.0 + 5.0 * jax.random.uniform(streams_of[17], (INNER,), jnp.float32) ** block_scale(streams_of[17], (INNER,), ((0, 8),), -0.2, 0.2), -6.0, -1.0).astype(jnp.bfloat16)
    skip_gain = jnp.clip(0.29882812 + 0.8964844 * jax.random.uniform(streams_of[18], (INNER,), jnp.float32) ** block_scale(streams_of[18], (INNER,), ((0, 8),), -0.2, 0.2), 0.29882812, 1.1953125).astype(jnp.bfloat16)
    beta_attn = jnp.clip(jnp.exp(math.log(2.0) - 1.3862944 * jax.random.uniform(streams_of[19], (INNER,), jnp.float32) ** block_scale(streams_of[19], (INNER,), ((0, 8),), -0.2, 0.2)), 0.5, 2.0).astype(jnp.bfloat16)
    beta_ssm = jnp.clip(jnp.exp(math.log(2.0) - 1.3862944 * jax.random.uniform(streams_of[20], (INNER,), jnp.float32) ** block_scale(streams_of[20], (INNER,), ((0, 8),), -0.2, 0.2)), 0.5, 2.0).astype(jnp.bfloat16)
    gain_first = jnp.clip(1.0 + 0.1 * jax.random.normal(streams_of[21], (D,), jnp.float32), 0.5, 1.5).astype(jnp.bfloat16)
    gain_second = jnp.clip(1.0 + 0.1 * jax.random.normal(streams_of[22], (D,), jnp.float32), 0.5, 1.5).astype(jnp.bfloat16)
    return {"tokens": tokens, "teacher": teacher, "cotangent": cotangent, "valid": valid, "w_query": w_query, "w_key": w_key, "w_value": w_value, "w_mixer": w_mixer, "w_output": w_output, "w_gate": w_gate, "w_up": w_up, "w_down": w_down, "w_select": w_select, "w_step": w_step, "log_decay": log_decay, "conv_taps": conv_taps, "conv_bias": conv_bias, "step_bias": step_bias, "skip_gain": skip_gain, "beta_attn": beta_attn, "beta_ssm": beta_ssm, "gain_first": gain_first, "gain_second": gain_second}


EPS = 1e-05
HIGH = lax.Precision.HIGHEST

@jax.custom_vjp
def low(v):
    return lax.optimization_barrier(v.astype(jnp.bfloat16)).astype(jnp.float32)

@jax.custom_vjp
def low_back(v):
    return v

def low_keep(v):
    return (low(v), None)

def low_pass(kept, grad):
    return (grad,)

def back_keep(v):
    return (v, None)

def back_low(kept, grad):
    return (low(grad),)
low.defvjp(low_keep, low_pass)
low_back.defvjp(back_keep, back_low)

def einsum_high(form, left, right):
    return jnp.einsum(form, left, right, precision=HIGH)

def rms_scale(value):
    return lax.rsqrt(lax.optimization_barrier(jnp.mean(value * value, axis=-1, keepdims=True)) + EPS)

def silu(value):
    return value * jax.nn.sigmoid(value)

def attend(queries, keys, values):
    q_heads = queries.reshape(LENGTH, KV, HEADS // KV, HD)
    k_heads = keys.reshape(LENGTH, KV, HD)
    v_heads = values.reshape(LENGTH, KV, INNER // HEADS)
    scores = low_back(einsum_high('lgqd,mgd->gqlm', q_heads, k_heads) / math.sqrt(HD))
    places = jnp.arange(LENGTH)
    allowed = (places[None, :] <= places[:, None]) & (places[None, :] > places[:, None] - WINDOW)
    scores = jnp.where(allowed, scores, -1e+30)
    probs = jax.nn.softmax(scores, axis=-1)
    mixed = einsum_high('gqlm,mgv->lgqv', low(probs), v_heads)
    return mixed.reshape(LENGTH, INNER)

def ssm_block(state, block, decay):

    def advance(carry, item):
        steps, drive, b_coef, c_coef = item
        carry = jnp.exp(steps[:, None, :] * decay) * carry + (steps * drive)[:, None, :] * b_coef[:, :, None]
        return (carry, lax.optimization_barrier(jnp.sum(c_coef[:, :, None] * carry, axis=1)))
    return lax.scan(advance, state, block)

def run_ssm(steps, drive, b_coef, c_coef, decay):
    seqs = steps.shape[0]
    block = math.gcd(LENGTH, 64)
    turns = LENGTH // block

    def cut(value):
        return value.reshape(seqs, turns, block, value.shape[-1]).transpose(1, 2, 0, 3)
    checked = jax.checkpoint(ssm_block)
    start = jnp.zeros((seqs, STATE, INNER), steps.dtype)
    _, outs = lax.scan(lambda state, item: checked(state, item, decay), start, (cut(steps), cut(drive), cut(b_coef), cut(c_coef)))
    return outs.transpose(2, 0, 1, 3).reshape(seqs, LENGTH, INNER)

def layer(tokens, target, weight_rows, count, w_query, w_key, w_value, w_mixer, w_output, w_gate, w_up, w_down, w_select, w_step, log_decay, conv_taps, conv_bias, step_bias, skip_gain, beta_attn, beta_ssm, gain_first, gain_second):
    normed1 = low(tokens * rms_scale(tokens) * gain_first)
    queries = low(low_back(einsum_high('bld,de->ble', normed1, w_query)))
    keys = low(low_back(einsum_high('bld,de->ble', normed1, w_key)))
    values = low(low_back(einsum_high('bld,de->ble', normed1, w_value)))
    attn = low_back(lax.map(jax.checkpoint(lambda item: attend(*item)), (queries, keys, values)))
    mixer = low_back(einsum_high('bld,de->ble', normed1, w_mixer))
    conv_in = low(mixer[..., :INNER])
    gate_z = mixer[..., INNER:]
    padded = jnp.pad(conv_in, ((0, 0), (CONV - 1, 0), (0, 0)))
    pre_conv = conv_bias
    for tap in range(CONV):
        pre_conv = pre_conv + conv_taps[tap] * padded[:, tap:tap + LENGTH]
    conv_out = silu(pre_conv)
    proj = low_back(einsum_high('ble,ef->blf', low(conv_out), w_select))
    rank_low = low(proj[..., :RANK])
    b_coef = proj[..., RANK:RANK + STATE]
    c_coef = proj[..., RANK + STATE:]
    steps = jax.nn.softplus(low_back(einsum_high('blr,re->ble', rank_low, w_step)) + step_bias)
    decay = -jnp.exp(log_decay)
    scan_out = run_ssm(steps, conv_out, b_coef, c_coef, decay)
    ssm = (scan_out + skip_gain * conv_out) * silu(gate_z)
    merged = low(0.5 * (attn * rms_scale(attn) * beta_attn + ssm * rms_scale(ssm) * beta_ssm))
    hidden1 = tokens + low_back(einsum_high('ble,ed->bld', merged, w_output))
    normed2 = low(hidden1 * rms_scale(hidden1) * gain_second)
    gate = low_back(einsum_high('bld,df->blf', normed2, w_gate))
    upper = low_back(einsum_high('bld,df->blf', normed2, w_up))
    hidden = low(silu(gate) * upper)
    hidden2 = hidden1 + low_back(einsum_high('blf,fd->bld', hidden, w_down))
    diff = hidden2 - target
    distill = 0.5 * TOKENS / count * jnp.sum(weight_rows[..., None] * diff * diff)
    return (hidden2, distill)

def reference(tokens, teacher, cotangent, valid, w_query, w_key, w_value, w_mixer, w_output, w_gate, w_up, w_down, w_select, w_step, log_decay, conv_taps, conv_bias, step_bias, skip_gain, beta_attn, beta_ssm, gain_first, gain_second):
    weights = tuple((item.astype(jnp.float32) for item in (w_query, w_key, w_value, w_mixer, w_output, w_gate, w_up, w_down, w_select, w_step, log_decay, conv_taps, conv_bias, step_bias, skip_gain, beta_attn, beta_ssm, gain_first, gain_second)))
    count = jnp.sum(valid.astype(jnp.float32))
    group = math.gcd(SEQS, 4)

    def split(value):
        return value.reshape((SEQS // group, group) + value.shape[1:])

    def run_group(carry, item):
        sums, loss_sum = carry
        x_grp, t_grp, c_grp, v_grp = item
        x_grp = x_grp.astype(jnp.float32)
        t_grp = t_grp.astype(jnp.float32)
        c_grp = c_grp.astype(jnp.float32)
        m_grp = v_grp.astype(jnp.float32)

        def objective(inputs, *params):
            return layer(inputs, t_grp, m_grp, count, *params)
        (hidden2, distill), pull = jax.vjp(objective, x_grp, *weights)
        grads = pull((c_grp, jnp.ones_like(distill)))
        sums = tuple((left + right for left, right in zip(sums, grads[1:])))
        diff = hidden2 - t_grp
        loss_sum = loss_sum + jnp.sum(m_grp[..., None] * diff * diff)
        return ((sums, loss_sum), (hidden2.astype(jnp.bfloat16), grads[0].astype(jnp.bfloat16)))
    zeros = tuple((jnp.zeros(item.shape, jnp.float32) for item in weights))
    (sums, loss_sum), (outs, dtok) = lax.scan(run_group, (zeros, jnp.zeros((), jnp.float32)), (split(tokens), split(teacher), split(cotangent), split(valid)))
    g_query, g_key, g_value, g_mixer, g_output, g_gate, g_up, g_down, g_select, g_step, g_decay, g_taps, g_conv_bias, g_step_bias, g_skip, g_beta_attn, g_beta_ssm, g_gain_first, g_gain_second = sums
    return (outs.reshape(tokens.shape), loss_sum / (count * D), dtok.reshape(tokens.shape), g_query, g_key, g_value, g_mixer, g_output, g_gate, g_up, g_down, g_select, g_step, g_decay, g_taps, g_conv_bias, g_step_bias, g_skip, g_beta_attn, g_beta_ssm, g_gain_first, g_gain_second)
```

```python
import functools
import math

import jax
import jax.numpy as jnp
from jax import lax
from jax.experimental import pallas as pl
from jax.experimental.pallas import tpu as pltpu
from jax.sharding import PartitionSpec as P

D = 1600
HEADS = 25
KV = 5
HD = 64
INNER = 3200
STATE = 16
CONV = 4
RANK = 100
WINDOW = 1024
GROUP = HEADS // KV
VHEAD = INNER // HEADS
LANE = 128

EPS = 1e-05
F32 = jnp.float32
BF16 = jnp.bfloat16
LOG2E = math.log2(math.e)
LN2 = math.log(2.0)
MESH = pl.DeviceIdType.MESH


def permute_bit(value, axis, bit):
    count = lax.axis_size(axis)
    return lax.ppermute(value, axis, [(i, i ^ bit) for i in range(count)])


def shift(value, axis, steps, wrap):
    count = lax.axis_size(axis)
    pairs = [(i, (i + steps) % count) for i in range(count) if wrap or 0 <= i + steps < count]
    return lax.ppermute(value, axis, pairs)


def bits_of(axis):
    count = lax.axis_size(axis)
    return [1 << k for k in range(count.bit_length() - 1)]


def total_over(value, axes):
    for axis in axes:
        for bit in bits_of(axis):
            value = value + permute_bit(value, axis, bit)
    return value


def from_ctx(blocks):
    count, mine = lax.axis_size("ctx"), lax.axis_index("ctx")
    out = []
    for at in range(count):
        block = blocks[0]
        for r in range(1, count):
            block = jnp.where(mine ^ r == at, blocks[r], block)
        out.append(block)
    return out


def gather_columns(shard):
    return lax.all_gather(shard, "ctx", axis=0)


def gather_rows(block):
    return lax.all_gather(block, "batch", axis=0, tiled=True)


def copy_rows(rows, copy):
    whole = rows // 16 * 16

    def body(i, _):
        copy(pl.multiple_of(i * 16, 16), 16)
        return 0

    lax.fori_loop(0, whole // 16, body, 0)
    if whole < rows:
        copy(whole, rows - whole)


def pieces_of(part, n, places, at=0, group=0, wide=0):
    out = []
    for i, place in enumerate(places):
        lo = 0
        while lo < n:
            col = i * n + lo
            hi, target = n, at + col
            if group:
                hi = min(n, (col // group + 1) * group - i * n)
                target = at + col // group * wide + col % group
            out.append((part, place, lo, hi, target))
            lo = hi
    return tuple(out)


def gather_kernel(n_parts, items, program, *refs):
    plain = [i for i, (pieces, _) in enumerate(items) if not pieces]
    shards, refs = refs[:n_parts], refs[n_parts:]
    direct, refs = dict(zip(plain, refs)), refs[len(plain) :]
    wholes, refs = refs[: len(items)], refs[len(items) :]
    parts, refs = refs[:n_parts], refs[n_parts:]
    blocks, sems = refs[: len(items)], refs[len(items) :]
    z_own, z_send, z_recv, b_send, b_recv, b_own = sems
    b, c = lax.axis_index("batch"), lax.axis_index("ctx")
    bits = bits_of("ctx")[::-1]

    barrier = pltpu.get_barrier_semaphore()
    peers = [{"ctx": c ^ bit} for bit in bits] + [{"batch": b ^ bit} for bit in (1, 2, 4)]
    for device in peers:
        pl.semaphore_signal(barrier, inc=1, device_id=device, device_id_type=MESH)
    pl.semaphore_wait(barrier, len(peers))

    started, stores = [], []

    def remote(source, target, send_sem, recv_sem, device):
        copy = pltpu.make_async_remote_copy(
            src_ref=source,
            dst_ref=target,
            send_sem=send_sem,
            recv_sem=recv_sem,
            device_id=device,
            device_id_type=MESH,
        )
        copy.start()
        started.append(copy)
        return copy

    come, reached = {}, {}

    def columns(part):
        shard, slot = shards[part], parts[part]
        stage = reached.get(part, 0)
        bit = bits[stage]
        if stage == 0:
            own = pltpu.make_async_copy(shard, slot.at[c], z_own.at[part])
            own.start()
            come[part] = {0: own.wait}
        for r in sorted(come[part]):
            if r:
                come[part][r]()
                come[part][r] = lambda: None
            copy = remote(
                slot.at[c ^ r] if r else shard,
                slot.at[c ^ r],
                z_send.at[part, r ^ bit],
                z_recv.at[part, r ^ bit],
                {"ctx": c ^ bit},
            )
            come[part][r ^ bit] = copy.wait_recv
        reached[part] = stage + 1

    flights = {}

    def send(item, slot, source, target, bit):
        return remote(
            source, target, b_send.at[item, slot], b_recv.at[item, slot], {"batch": b ^ bit}
        )

    def keep(item, slot, r):
        there = wholes[item].at[b ^ r]
        store = pltpu.make_async_copy(blocks[item].at[slot], there, b_own.at[item, slot])
        store.start()
        stores.append(store)
        return send(item, 4 + slot, blocks[item].at[slot], there, 1)

    def launch(item):
        pieces, rows = items[item]
        block = blocks[item]
        if pieces:
            for part in sorted({piece[0] for piece in pieces}):
                for r in come[part]:
                    come[part][r]()
                    come[part][r] = lambda: None
            ends = sorted((at, at + hi - lo) for _, _, lo, hi, at in pieces)
            ends.append((block.shape[2], 0))
            gaps = [(end, ends[i + 1][0]) for i, (_, end) in enumerate(ends[:-1])]

            def relay(start, count):
                for part, place, lo, hi, at in pieces:
                    block[0, pl.ds(start, count), at : at + hi - lo] = parts[part][
                        place, pl.ds(start, count), lo:hi
                    ]
                for lo, hi in gaps:
                    if lo < hi:
                        block[0, pl.ds(start, count), lo:hi] = jnp.zeros((count, hi - lo), block.dtype)

            copy_rows(block.shape[1], relay)
        else:
            own = pltpu.make_async_copy(direct[item], block.at[0], b_own.at[item, 4])
            own.start()
            own.wait()
        if rows:
            flights[item] = [
                send(item, 1, block.at[0], block.at[1], 2),
                send(item, 2, block.at[0], block.at[2], 4),
            ]
            flights[item].append(keep(item, 0, 0))
        else:
            store = pltpu.make_async_copy(block.at[0], wholes[item], b_own.at[item, 0])
            store.start()
            stores.append(store)

    def forward(item):
        block, flight = blocks[item], flights[item]
        n = block.shape[2]
        half = n // 2 // LANE * LANE
        flight[0].wait_recv()
        left, right = (slice(None), slice(0, half)), (slice(None), slice(half, n))
        flight.append(send(item, 3, block.at[1, *left], block.at[3, *left], 4))
        flight.append(keep(item, 1, 2))
        flight[1].wait_recv()
        flight.append(send(item, 0, block.at[2, *right], block.at[3, *right], 2))
        flight.append(keep(item, 2, 4))

    def last(item):
        flight = flights[item]
        flight[3].wait_recv()
        flight[5].wait_recv()
        flight.append(keep(item, 3, 6))

    acts = {"columns": columns, "launch": launch, "forward": forward, "last": last}
    for act, which in program:
        acts[act](which)
    for flight in flights.values():
        for key in (2, 4, 6, 7):
            flight[key].wait_recv()
    for copy in stores:
        copy.wait()
    for copy in started:
        copy.wait_send()


def gather_all(shards, items, program, collective_id):
    count, nbatch = lax.axis_size("ctx"), lax.axis_size("batch")
    if nbatch != 8:
        found, out = [gather_columns(shard) for shard in shards], []
        for item in items:
            if not isinstance(item, tuple):
                out.append(gather_rows(item).reshape(nbatch, *item.shape))
                continue
            pieces, n, rows = item
            block = jnp.zeros((found[pieces[0][0]].shape[1], n), shards[pieces[0][0]].dtype)
            for part, place, lo, hi, at in pieces:
                block = block.at[:, at : at + hi - lo].set(found[part][place, :, lo:hi])
            out.append(gather_rows(block).reshape(nbatch, *block.shape) if rows else block)
        return out
    flat, kinds, shapes, blocks = list(shards), [], [], []
    for item in items:
        if isinstance(item, tuple):
            pieces, n, rows = item
            k, dtype = shards[pieces[0][0]].shape[0], shards[pieces[0][0]].dtype
        else:
            (k, n), pieces, rows, dtype = item.shape, (), True, item.dtype
            flat.append(item)
        kinds.append((pieces, rows))
        blocks.append(pltpu.VMEM((4 if rows else 1, k, n), dtype))
        shapes.append(jax.ShapeDtypeStruct((nbatch, k, n) if rows else (k, n), dtype))
    dma = pltpu.SemaphoreType.DMA
    hbm = pl.BlockSpec(memory_space=pl.ANY)
    return pl.pallas_call(
        functools.partial(gather_kernel, len(shards), tuple(kinds), program),
        in_specs=[hbm] * len(flat),
        out_specs=[hbm] * len(shapes),
        out_shape=shapes,
        scratch_shapes=[pltpu.VMEM((count,) + w.shape, w.dtype) for w in shards]
        + blocks
        + [dma((len(shards),)), dma((len(shards), count)), dma((len(shards), count))]
        + [dma((len(shapes), 8)), dma((len(shapes), 8)), dma((len(shapes), 5))],
        compiler_params=pltpu.CompilerParams(
            collective_id=collective_id, has_side_effects=True, vmem_limit_bytes=56 << 20
        ),
        name="gather_weights",
    )(*flat)


class Staged:
    def __init__(self, live):
        self.live = live
        self.fresh = list(live)
        self.stage = 0

    def fly(self, key, value):
        self.live[key] = value
        self.fresh.append(key)


def hold(staged, *values):
    flying = [[item.live[key] for key in item.fresh] for item in staged]
    flying, values = lax.optimization_barrier((flying, values))
    for item, arrived in zip(staged, flying):
        item.live.update(zip(item.fresh, arrived))
        item.fresh = []
    return values[0] if len(values) == 1 else values


class FromCtx(Staged):
    def __init__(self, value):
        super().__init__({0: value[None]})
        self.orders = [[0]]

    def step(self):
        bits = bits_of("ctx")[::-1]
        if self.stage < len(bits):
            bit = bits[self.stage]
            sent = list(self.live.values())
            sent = jnp.concatenate(sent, axis=0) if len(sent) > 1 else sent[0]
            self.orders.append([r ^ bit for order in self.orders for r in order])
            self.fly(self.stage + 1, permute_bit(sent, "ctx", bit))
        self.stage += 1

    def finish(self):
        while self.stage < len(bits_of("ctx")):
            self.step()
        return {
            r: self.live[i][j] for i, order in enumerate(self.orders) for j, r in enumerate(order)
        }


class ToCtx(Staged):
    def __init__(self, blocks):
        super().__init__({(r, 0): block for r, block in blocks.items()})

    def total(self, r):
        terms = [v.astype(F32) for key, v in self.live.items() if key[0] == r]
        return functools.reduce(jnp.add, terms)

    def step(self):
        bits = bits_of("ctx")
        if self.stage < len(bits):
            bit = bits[self.stage]
            which = sorted({key[0] for key in self.live if key[0] & bit})
            sent = jnp.stack([self.total(r).astype(BF16) for r in which])
            got = permute_bit(sent, "ctx", bit)
            self.live = {key: v for key, v in self.live.items() if not key[0] & bit}
            self.fresh = [key for key in self.fresh if key in self.live]
            for i, r in enumerate(which):
                self.fly((r ^ bit, self.stage + 1), got[i])
        self.stage += 1

    def result(self):
        while self.stage < len(bits_of("ctx")):
            self.step()
        return self.total(0)


def assemble_kernel(names, cuts, *refs):
    parts, wholes = refs[: len(names)], refs[len(names) : len(names) + len(cuts)]
    held, sems_in, sems_out, send_sems, recv_sems = refs[-5:]
    b = lax.axis_index("batch")
    other = {"batch": b ^ 1}
    ins = {}
    for i, (part, (r, lo)) in enumerate(zip(parts, names)):
        n = part.shape[1]
        slot = held.at[r // 2] if n == held.shape[2] else held.at[r // 2, :, lo : lo + n]
        ins.setdefault(r, []).append(pltpu.make_async_copy(part, slot, sems_in.at[i]))
        ins[r][-1].start()
    barrier = pltpu.get_barrier_semaphore()
    pl.semaphore_signal(barrier, inc=1, device_id=other, device_id_type=MESH)
    pl.semaphore_wait(barrier, 1)
    waits = []
    for r, copies in ins.items():
        for copy in copies:
            copy.wait()
        for i, (whole, (lo, hi)) in enumerate(zip(wholes, cuts)):
            slot = held.at[r // 2] if len(cuts) == 1 else held.at[r // 2, :, lo:hi]
            goes = pltpu.make_async_remote_copy(
                src_ref=slot,
                dst_ref=whole.at[b ^ r],
                send_sem=send_sems.at[i, r // 2],
                recv_sem=recv_sems.at[i, r // 2],
                device_id=other,
                device_id_type=MESH,
            )
            stays = pltpu.make_async_copy(slot, whole.at[b ^ r], sems_out.at[i, r // 2])
            goes.start()
            stays.start()
            waits += [goes, stays]
    for copy in waits:
        copy.wait()


def assemble(parts, widths, collective_id):
    names = tuple(parts)
    k, n = parts[(0, 0)].shape
    cuts = tuple((sum(widths[:i]), sum(widths[: i + 1])) for i in range(len(widths)))
    hbm = pl.BlockSpec(memory_space=pl.ANY)
    dma = pltpu.SemaphoreType.DMA
    wholes = pl.pallas_call(
        functools.partial(assemble_kernel, names, cuts),
        in_specs=[hbm] * len(names),
        out_specs=[hbm] * len(cuts),
        out_shape=[jax.ShapeDtypeStruct((8, k, width), BF16) for width in widths],
        scratch_shapes=[pltpu.VMEM((4, k, n), BF16), dma((len(names),)), dma((len(cuts), 4))]
        + [dma((len(cuts), 4)), dma((len(cuts), 4))],
        compiler_params=pltpu.CompilerParams(
            collective_id=collective_id, has_side_effects=True, vmem_limit_bytes=40 << 20
        ),
        cost_estimate=pl.CostEstimate(flops=0, bytes_accessed=32 * k * n, transcendentals=0),
        name="assemble",
    )(*[parts[name] for name in names])
    return [whole.reshape(8 * k, -1) for whole in wholes]


class Gather(Staged):
    def __init__(self, block, shard=None):
        self.block, self.shard = block, shard
        self.columns = None if shard is None else FromCtx(shard)
        super().__init__({(0, 0): block} if shard is None else self.columns.live)

    def step(self):
        if lax.axis_size("batch") != 8:
            return
        if self.columns:
            if self.columns.stage < len(bits_of("ctx")):
                self.columns.live, self.columns.fresh = self.live, []
                self.columns.step()
                self.live, self.fresh = self.columns.live, self.columns.fresh
                return
            self.columns.live = self.live
            self.live = {(0, 0): jnp.concatenate(from_ctx(self.columns.finish()), axis=1)}
            self.columns, self.fresh = None, []
        live, block = self.live, self.live[(0, 0)]
        if self.stage == 0:
            for bit in (2, 4):
                self.fly((bit, 0), permute_bit(block, "batch", bit))
        elif self.stage == 1:
            n = block.shape[1]
            half = n // 2 // LANE * LANE
            self.fly((6, 0), permute_bit(live[(2, 0)][:, :half], "batch", 4))
            self.fly((6, half), permute_bit(live[(4, 0)][:, half:], "batch", 2))
        self.stage += 1

    def whole(self, collective_id, *widths):
        if lax.axis_size("batch") == 8:
            return assemble(self.live, widths, collective_id)
        block = self.block
        if self.shard is not None:
            block = jnp.concatenate(list(gather_columns(self.shard)), axis=1)
        whole = gather_rows(block)
        return jnp.split(whole, [sum(widths[:i]) for i in range(1, len(widths))], axis=1)


def ctx_terms(own, columns):
    nctx, mine = lax.axis_size("ctx"), lax.axis_index("ctx")
    at, cuts = 0, []
    for n in columns:
        cuts.append([own[:, at + c * n : at + (c + 1) * n] for c in range(nctx)])
        at += nctx * n
    parts = [jnp.concatenate(cut, axis=1) if len(cut) > 1 else cut[0] for cut in zip(*cuts)]
    blocks = {}
    for r in range(nctx):
        blocks[r] = parts[0]
        for c in range(1, nctx):
            blocks[r] = jnp.where(mine ^ r == c, parts[c], blocks[r])
    return ToCtx(blocks)


class Scatter(Staged):
    def __init__(self, left, right, *columns, trim=None):
        count = lax.axis_size("batch")
        super().__init__({})
        self.columns, self.trim = columns, trim
        self.tall, self.right = left.T.reshape(count, -1, left.shape[0]), right
        self.arrived = {}
        self.spread = None

    def rows_of(self, which):
        mine = lax.axis_index("batch")
        return jnp.concatenate(
            [lax.dynamic_index_in_dim(self.tall, mine ^ r, 0, keepdims=False) for r in which], axis=0
        )

    def part(self, which, lo, hi):
        k = self.tall.shape[1]
        own = matmul(self.rows_of(which), self.right[:, lo:hi])
        for key, order in self.arrived.items():
            if key[0] in (lo, -1):
                off = lo if key[0] == -1 else 0
                pieces = [
                    self.live[key][
                        order.index(r) * k : (order.index(r) + 1) * k, off : off + hi - lo
                    ]
                    for r in which
                ]
                own = own + jnp.concatenate(pieces, axis=0).astype(F32)
        return own

    def step(self):
        stage = self.stage
        self.stage += 1
        count, bits = lax.axis_size("batch"), bits_of("batch")
        n = self.right.shape[1]
        cut = n // 2 // LANE * LANE
        halves = ((0, cut, bits[1:]), (cut, n, bits[:0:-1]))
        if self.stage > len(bits) + 1 and not self.spread:
            return
        if count != 8 and stage <= len(bits):
            self.stage = len(bits) + 1
            whole = matmul(self.tall.reshape(-1, self.tall.shape[2]), self.right).astype(BF16)
            own = lax.psum_scatter(whole, "batch", scatter_dimension=0, tiled=True)
            self.live = {"own": self.trim(own) if self.trim else own}
            if self.columns:
                self.to_ctx(self.live["own"])
        elif stage == 0:
            odd = [r for r in range(count) if r & 1]
            sent = matmul(self.rows_of(odd), self.right).astype(BF16)
            self.fly((-1, 0), permute_bit(sent, "batch", 1))
            self.arrived[(-1, 0)] = [r ^ 1 for r in odd]
        elif stage < len(bits):
            fresh = {}
            for lo, hi, order in halves:
                gone, bit = sum(order[: stage - 1]), order[stage - 1]
                which = [r for r in range(count) if not r & (gone | 1) and r & bit]
                fresh[(lo, stage)] = permute_bit(self.part(which, lo, hi).astype(BF16), "batch", bit)
                self.arrived[(lo, stage)] = [r ^ bit for r in which]
            for key, value in fresh.items():
                self.fly(key, value)
        elif stage == len(bits):
            own = jnp.concatenate([self.part([0], lo, hi) for lo, hi, _ in halves], axis=1)
            own = own.astype(BF16)
            self.live, self.fresh = {"own": self.trim(own) if self.trim else own}, []
            if self.columns:
                self.to_ctx(self.live["own"])
                self.step()
        elif self.spread:
            self.spread.live, self.spread.fresh = self.live, []
            self.spread.step()
            self.live, self.fresh = self.spread.live, self.spread.fresh

    def to_ctx(self, own):
        self.spread = ctx_terms(own, self.columns)
        self.live, self.fresh = self.spread.live, []

    def finished(self):
        while self.stage <= len(bits_of("batch")):
            self.step()
        return self.live["own"]

    def result(self):
        while self.stage <= len(bits_of("batch")) or not self.spread:
            self.step()
        self.spread.live = self.live
        total, out = self.spread.result(), []
        for n in self.columns:
            at = sum(v.shape[1] for v in out)
            out.append(total[:, at : at + n])
        return out


def reduce_kernel(n_parts, items, program, *refs):
    n = len(items)
    plain = [i for i, pieces in enumerate(items) if not pieces]
    terms, refs = refs[:n], refs[n:]
    outs, refs = refs[: n_parts + len(plain)], refs[n_parts + len(plain) :]
    accs, refs = refs[:n], refs[n:]
    firsts, refs = refs[:n], refs[n:]
    seconds, refs = refs[:n], refs[n:]
    thirds, refs = refs[:n], refs[n:]
    parts, refs = refs[:n_parts], refs[n_parts:]
    lands, sems = refs[: n_parts + len(plain)], refs[n_parts + len(plain) :]
    load, b_send, b_recv, z_send, z_recv = sems
    nctx = lax.axis_size("ctx")
    b, c = lax.axis_index("batch"), lax.axis_index("ctx")

    barrier = pltpu.get_barrier_semaphore()
    peers = [{"ctx": c ^ r} for r in range(1, nctx)] + [{"batch": b ^ bit} for bit in (1, 2, 4)]
    for device in peers:
        pl.semaphore_signal(barrier, inc=1, device_id=device, device_id_type=MESH)
    pl.semaphore_wait(barrier, len(peers))

    started = []

    def remote(source, target, send_sem, recv_sem, device):
        copy = pltpu.make_async_remote_copy(
            src_ref=source,
            dst_ref=target,
            send_sem=send_sem,
            recv_sem=recv_sem,
            device_id=device,
            device_id_type=MESH,
        )
        copy.start()
        started.append(copy)
        return copy

    def send(item, slot, source, target, bit):
        return remote(
            source, target, b_send.at[item, slot], b_recv.at[item, slot], {"batch": b ^ bit}
        )

    def halves(item):
        width = accs[item].shape[2]
        cut = width // 2 // LANE * LANE
        return (0, cut), (cut, width)

    def add(to, j, other, i, lo, hi):
        def rows(start, count):
            at = pl.ds(start, count)
            total = to[j, at, lo:hi].astype(F32) + other[i, at, lo:hi].astype(F32)
            to[j, at, lo:hi] = total.astype(BF16)

        copy_rows(to.shape[1], rows)

    flights, z_flights = {}, {}

    def begin(item):
        copies = []
        for j in range(4):
            own = pltpu.make_async_copy(terms[item].at[b ^ (2 * j)], accs[item].at[j], load.at[item, j])
            own.start()
            copies.append(own)
        for j in range(4):
            copies.append(send(item, j, terms[item].at[b ^ (2 * j + 1)], firsts[item].at[j], 1))
        flights[item] = copies

    def sub(ref, j, span):
        return ref.at[j, :, span[0] : span[1]]

    def first(item):
        acc, flight = accs[item], flights[item]
        left, right = halves(item)
        for j in (3, 1, 2, 0):
            flight[j].wait()
            flight[4 + j].wait_recv()
            add(acc, j, firsts[item], j, 0, acc.shape[2])
            if j == 1:
                after = [
                    send(item, 4, sub(acc, 1, left), sub(seconds[item], 0, left), 2),
                    send(item, 5, sub(acc, 3, left), sub(seconds[item], 1, left), 2),
                ]
            if j == 2:
                after += [
                    send(item, 6, sub(acc, 2, right), sub(seconds[item], 0, right), 4),
                    send(item, 7, sub(acc, 3, right), sub(seconds[item], 1, right), 4),
                ]
        flights[item] = after

    def second(item):
        acc, flight = accs[item], flights[item]
        left, right = halves(item)
        flight[1].wait_recv()
        add(acc, 2, seconds[item], 1, *left)
        after = [send(item, 8, sub(acc, 2, left), sub(thirds[item], 0, left), 4)]
        flight[3].wait_recv()
        add(acc, 1, seconds[item], 1, *right)
        after.append(send(item, 9, sub(acc, 1, right), sub(thirds[item], 0, right), 2))
        flight[0].wait_recv()
        flight[2].wait_recv()
        add(acc, 0, seconds[item], 0, 0, acc.shape[2])
        flights[item] = after

    def third(item):
        acc = accs[item]
        for copy in flights[item]:
            copy.wait_recv()
        add(acc, 0, thirds[item], 0, 0, acc.shape[2])
        if items[item]:

            def relay(start, count):
                at = pl.ds(start, count)
                for part, place, lo, hi, col in items[item]:
                    parts[part][place, at, lo:hi] = acc[0, at, col : col + hi - lo]

            copy_rows(acc.shape[1], relay)
        else:
            slot = n_parts + plain.index(item)
            land = lands[slot]

            def keep(start, count):
                land[c, pl.ds(start, count), :] = acc[0, pl.ds(start, count), :]

            copy_rows(acc.shape[1], keep)
            z_flights[slot] = [
                remote(
                    acc.at[0], land.at[c], z_send.at[slot, r], z_recv.at[slot, r], {"ctx": c ^ r}
                )
                for r in range(1, nctx)
            ]

    def spread(part):
        z_flights[part] = [
            remote(
                parts[part].at[c ^ r],
                lands[part].at[r],
                z_send.at[part, r],
                z_recv.at[part, r],
                {"ctx": c ^ r},
            )
            for r in range(1, nctx)
        ]

    def finish(slot):
        land, out = lands[slot], outs[slot]
        for copy in z_flights[slot]:
            copy.wait_recv()

        def rows(start, count):
            at = pl.ds(start, count)
            first = parts[slot][c, at, :] if slot < n_parts else land[0, at, :]
            total = first.astype(F32)
            for r in range(1, nctx):
                total = total + land[r, at, :].astype(F32)
            out[at, :] = total

        copy_rows(out.shape[0], rows)

    acts = {"b": begin, "f": first, "s": second, "t": third, "p": spread, "e": finish}
    for act, which in program:
        acts[act](which)
    for copy in started:
        copy.wait_send()


def reduce_all(terms, items, widths, program, collective_id):
    nctx, nbatch = lax.axis_size("ctx"), lax.axis_size("batch")
    plain = [i for i, pieces in enumerate(items) if not pieces]
    rows = {piece[0]: terms[i].shape[0] // nbatch for i, ps in enumerate(items) for piece in ps}
    if nbatch != 8:
        sums = [lax.psum_scatter(t, "batch", scatter_dimension=0, tiled=True) for t in terms]
        out = []
        for part, n in enumerate(widths):
            whole = jnp.zeros((rows[part], nctx, n), BF16)
            for i, pieces in enumerate(items):
                for at_part, place, lo, hi, col in pieces:
                    if at_part == part:
                        whole = whole.at[:, place, lo:hi].set(sums[i][:, col : col + hi - lo])
            out.append(lax.psum_scatter(whole, "ctx", scatter_dimension=1).astype(F32))
        return out + [lax.psum(sums[i], "ctx").astype(F32) for i in plain]
    terms = [t.reshape(nbatch, -1, t.shape[1]) for t in terms]
    sizes = [t.shape[1:] for t in terms]
    shapes = [(rows[part], n) for part, n in enumerate(widths)] + [sizes[i] for i in plain]
    dma = pltpu.SemaphoreType.DMA
    return pl.pallas_call(
        functools.partial(reduce_kernel, len(widths), tuple(items), program),
        in_specs=[pl.BlockSpec(memory_space=pl.ANY)] * len(terms),
        out_specs=[pl.BlockSpec(memory_space=pltpu.VMEM)] * len(shapes),
        out_shape=[jax.ShapeDtypeStruct(shape, F32) for shape in shapes],
        scratch_shapes=[pltpu.VMEM((count,) + size, BF16) for count in (4, 4, 2, 1) for size in sizes]
        + [pltpu.VMEM((nctx,) + shape, BF16) for shape in shapes[: len(widths)]]
        + [pltpu.VMEM((nctx,) + shape, BF16) for shape in shapes]
        + [dma((len(terms), 4)), dma((len(terms), 10)), dma((len(terms), 10))]
        + [dma((len(shapes), nctx)), dma((len(shapes), nctx))],
        compiler_params=pltpu.CompilerParams(
            collective_id=collective_id, has_side_effects=True, vmem_limit_bytes=62 << 20
        ),
        name="reduce_gradients",
    )(*terms)


def wide(tile, width):
    return jnp.concatenate([tile] * (width // LANE), axis=1)


def fold(value):
    parts = [value[:, at : at + LANE] for at in range(0, value.shape[1], LANE)]
    return functools.reduce(jnp.add, parts)


SCAN_WIDTH = 640
SCAN_PART = 384
UNROLL = 8


def scan_parts(width):
    return [(lo, min(width, lo + SCAN_PART)) for lo in range(0, width, SCAN_PART)]


def scan_specs(seqs, span, chan):
    pos = pl.BlockSpec((1, span, SCAN_WIDTH), lambda s, e: (s, 0, e))
    coef = pl.BlockSpec((1, span, STATE, LANE), lambda s, e: (s, 0, 0, 0))
    dec = pl.BlockSpec((STATE, SCAN_WIDTH), lambda s, e: (0, e))
    state = pl.BlockSpec((1, STATE, SCAN_WIDTH), lambda s, e: (s, 0, e))
    return pos, coef, dec, state


def scan_params():
    return pltpu.CompilerParams(vmem_limit_bytes=56 << 20)


def scan_cost(seqs, span, chan, ops):
    cells = seqs * span * chan * STATE
    return pl.CostEstimate(flops=cells * ops, bytes_accessed=seqs * span * chan * 16, transcendentals=cells)


def final_kernel(step_ref, xc_ref, b_ref, dec_ref, fin_ref, drive):
    span, width = step_ref.shape[1:]
    drive[...] = step_ref[0] * xc_ref[0]
    for lo, hi in scan_parts(width):
        dec = dec_ref[:, lo:hi]

        def body(i, h):
            for j in range(UNROLL):
                t = i * UNROLL + j
                f = jnp.exp2(step_ref[0, pl.ds(t, 1), lo:hi] * dec)
                h = f * h + drive[pl.ds(t, 1), lo:hi] * wide(b_ref[0, t], hi - lo)
            return h

        fin_ref[0, :, lo:hi] = lax.fori_loop(
            0, span // UNROLL, body, jnp.zeros((STATE, hi - lo), F32)
        )


def scan_final(steps, xc, bb, dec):
    seqs, span, chan = steps.shape
    pos, coef, decs, state = scan_specs(seqs, span, chan)
    return pl.pallas_call(
        final_kernel,
        grid=(seqs, chan // SCAN_WIDTH),
        in_specs=[pos, pos, coef, decs],
        out_specs=state,
        out_shape=jax.ShapeDtypeStruct((seqs, STATE, chan), F32),
        scratch_shapes=[pltpu.VMEM((span, SCAN_WIDTH), F32)],
        compiler_params=scan_params(),
        cost_estimate=scan_cost(seqs, span, chan, 6),
        name="scan_final",
    )(steps, xc, bb, dec)


def out_kernel(step_ref, xc_ref, b_ref, c_ref, dec_ref, entry_ref, y_ref, drive):
    span, width = step_ref.shape[1:]
    drive[...] = step_ref[0] * xc_ref[0]
    for lo, hi in scan_parts(width):
        dec = dec_ref[:, lo:hi]

        def body(i, h):
            rows = []
            for j in range(UNROLL):
                t = i * UNROLL + j
                f = jnp.exp2(step_ref[0, pl.ds(t, 1), lo:hi] * dec)
                h = f * h + drive[pl.ds(t, 1), lo:hi] * wide(b_ref[0, t], hi - lo)
                rows.append(jnp.sum(h * wide(c_ref[0, t], hi - lo), axis=0, keepdims=True))
            at = pl.multiple_of(i * UNROLL, UNROLL)
            y_ref[0, pl.ds(at, UNROLL), lo:hi] = jnp.concatenate(rows, axis=0)
            return h

        lax.fori_loop(0, span // UNROLL, body, entry_ref[0, :, lo:hi])


def scan_out_of(steps, xc, bb, cc, dec, entry):
    seqs, span, chan = steps.shape
    pos, coef, decs, state = scan_specs(seqs, span, chan)
    return pl.pallas_call(
        out_kernel,
        grid=(seqs, chan // SCAN_WIDTH),
        in_specs=[pos, pos, coef, coef, decs, state],
        out_specs=pos,
        out_shape=jax.ShapeDtypeStruct((seqs, span, chan), F32),
        scratch_shapes=[pltpu.VMEM((span, SCAN_WIDTH), F32)],
        compiler_params=scan_params(),
        cost_estimate=scan_cost(seqs, span, chan, 10),
        name="scan_out",
    )(steps, xc, bb, cc, dec, entry)


def adjoint_kernel(step_ref, gy_ref, c_ref, dec_ref, out_ref):
    span, width = step_ref.shape[1:]
    for lo, hi in scan_parts(width):
        dec = dec_ref[:, lo:hi]

        def body(i, g):
            for j in range(UNROLL):
                t = span - 1 - (i * UNROLL + j)
                f = jnp.exp2(step_ref[0, pl.ds(t, 1), lo:hi] * dec)
                g = f * (g + gy_ref[0, pl.ds(t, 1), lo:hi] * wide(c_ref[0, t], hi - lo))
            return g

        out_ref[0, :, lo:hi] = lax.fori_loop(
            0, span // UNROLL, body, jnp.zeros((STATE, hi - lo), F32)
        )


def scan_adjoint(steps, gy, cc, dec):
    seqs, span, chan = steps.shape
    pos, coef, decs, state = scan_specs(seqs, span, chan)
    return pl.pallas_call(
        adjoint_kernel,
        grid=(seqs, chan // SCAN_WIDTH),
        in_specs=[pos, pos, coef, decs],
        out_specs=state,
        out_shape=jax.ShapeDtypeStruct((seqs, STATE, chan), F32),
        compiler_params=scan_params(),
        cost_estimate=scan_cost(seqs, span, chan, 6),
        name="scan_adjoint",
    )(steps, gy, cc, dec)


def back_kernel(
    step_ref, xc_ref, gy_ref, b_ref, c_ref, dec_ref, entry_ref, arrive_ref,
    dxc_ref, dstep_ref, db_ref, dc_ref, ddec_ref, drive, hs, fs,
):
    span, width = step_ref.shape[1:]
    drive[...] = step_ref[0] * xc_ref[0]

    @pl.when(pl.program_id(1) == 0)
    def _():
        db_ref[...] = jnp.zeros_like(db_ref)
        dc_ref[...] = jnp.zeros_like(dc_ref)

    for lo, hi in scan_parts(width):
        n = hi - lo
        dec = dec_ref[:, lo:hi]

        def ahead(i, h):
            for j in range(UNROLL):
                t = i * UNROLL + j
                f = jnp.exp2(step_ref[0, pl.ds(t, 1), lo:hi] * dec)
                hs[t, :, :n] = h
                fs[t, :, :n] = f
                h = f * h + drive[pl.ds(t, 1), lo:hi] * wide(b_ref[0, t], n)
            return h

        last = lax.fori_loop(0, span // UNROLL, ahead, entry_ref[0, :, lo:hi])

        def back(i, carry):
            g, h, ddec = carry
            weighted, along = [], []
            for j in range(UNROLL):
                t = span - 1 - (i * UNROLL + j)
                gy = gy_ref[0, pl.ds(t, 1), lo:hi]
                g = g + gy * wide(c_ref[0, t], n)
                dc_ref[0, t] += fold(gy * h)
                db_ref[0, t] += fold(g * drive[pl.ds(t, 1), lo:hi])
                weighted.append(jnp.sum(g * wide(b_ref[0, t], n), axis=0, keepdims=True))
                g = g * fs[t, :, :n]
                h = hs[t, :, :n]
                m = g * h
                along.append(jnp.sum(m * dec, axis=0, keepdims=True))
                ddec = ddec + m * step_ref[0, pl.ds(t, 1), lo:hi]
            at = pl.multiple_of(span - (i + 1) * UNROLL, UNROLL)
            w8 = jnp.concatenate(weighted[::-1], axis=0)
            m8 = jnp.concatenate(along[::-1], axis=0)
            dxc_ref[0, pl.ds(at, UNROLL), lo:hi] = w8 * step_ref[0, pl.ds(at, UNROLL), lo:hi]
            dstep_ref[0, pl.ds(at, UNROLL), lo:hi] = (
                m8 * LN2 + w8 * xc_ref[0, pl.ds(at, UNROLL), lo:hi]
            )
            return g, h, ddec

        start = (arrive_ref[0, :, lo:hi], last, jnp.zeros((STATE, n), F32))
        ddec_ref[0, :, lo:hi] = lax.fori_loop(0, span // UNROLL, back, start)[2]


def scan_back(steps, xc, gy, bb, cc, dec, entry, arrive):
    seqs, span, chan = steps.shape
    pos, coef, decs, state = scan_specs(seqs, span, chan)
    by_pos = jax.ShapeDtypeStruct((seqs, span, chan), F32)
    by_coef = jax.ShapeDtypeStruct((seqs, span, STATE, LANE), F32)
    return pl.pallas_call(
        back_kernel,
        grid=(seqs, chan // SCAN_WIDTH),
        in_specs=[pos, pos, pos, coef, coef, decs, state, state],
        out_specs=[pos, pos, coef, coef, state],
        out_shape=[by_pos, by_pos, by_coef, by_coef, jax.ShapeDtypeStruct((seqs, STATE, chan), F32)],
        scratch_shapes=[pltpu.VMEM((span, SCAN_WIDTH), F32)]
        + [pltpu.VMEM((span, STATE, SCAN_PART), F32)] * 2,
        compiler_params=scan_params(),
        cost_estimate=scan_cost(seqs, span, chan, 24),
        name="scan_back",
    )(steps, xc, gy, bb, cc, dec, entry, arrive)


def attend_mask(place_ref, mask):
    span = mask.shape[0]
    row = lax.broadcasted_iota(jnp.int32, (span, span), 0) + place_ref[0]
    col = lax.broadcasted_iota(jnp.int32, (span, span), 1)
    for at in range(mask.shape[1] // span):
        apart = row - (col + place_ref[at])
        allowed = (apart >= 0) & (apart < WINDOW)
        mask[:, at * span : (at + 1) * span] = jnp.where(allowed, 0.0, -1e30)


def first_step():
    return (pl.program_id(0) == 0) & (pl.program_id(1) == 0)


def scores_of(q, k):
    return lax.dot_general(q, k, (((1,), (1,)), ((), ())), preferred_element_type=F32)


QWIDE = -(-GROUP * HD // LANE) * LANE
KWIDE = -(-KV * HD // LANE) * LANE


def heads_in(k_refs, v_refs, k_all, v_all):
    span, at = v_refs[0].shape[2], 0
    for k_ref, v_ref in zip(k_refs, v_refs):
        for i in range(v_ref.shape[0]):
            v_all[at : at + span, :] = v_ref[i, 0]
            for h in range(KV):

                @pl.when(pl.program_id(1) == h)
                def _(k_ref=k_ref, i=i, at=at, h=h):
                    k_all[at : at + span, :] = k_ref[i, 0, :, h * HD : (h + 1) * HD]

            at += span


def attend_kernel(n, place_ref, q_ref, *refs):
    k_refs, v_refs, (out_ref, mask, k_all, v_all) = refs[:n], refs[n : 2 * n], refs[2 * n :]
    pl.when(first_step())(lambda: attend_mask(place_ref, mask))
    heads_in(k_refs, v_refs, k_all, v_all)
    for g in range(GROUP):
        s = scores_of(q_ref[0, :, g * HD : (g + 1) * HD], k_all[...]) + mask[...]
        e = jnp.exp(s - jnp.max(s, axis=-1, keepdims=True))
        total = jnp.sum(e, axis=-1, keepdims=True)
        mixed = jnp.dot(e.astype(BF16), v_all[...], preferred_element_type=F32)
        out_ref[0, :, g * VHEAD : (g + 1) * VHEAD] = mixed / total


def attend_specs(span, kvs):
    q = pl.BlockSpec((1, span, QWIDE), lambda s, h: (s, 0, h))
    ks = [pl.BlockSpec((kv.shape[0], 1, span, KWIDE), lambda s, h: (0, s, 0, 0)) for kv in kvs]
    vs = [
        pl.BlockSpec((kv.shape[0], 1, span, VHEAD), lambda s, h: (0, s, 0, KWIDE // VHEAD + h))
        for kv in kvs
    ]
    out = pl.BlockSpec((1, span, GROUP * VHEAD), lambda s, h: (s, 0, h))
    length = span * sum(kv.shape[0] for kv in kvs)
    held = [
        pltpu.VMEM((span, length), F32),
        pltpu.VMEM((length, HD), BF16),
        pltpu.VMEM((length, VHEAD), BF16),
    ]
    return [pl.BlockSpec(memory_space=pltpu.SMEM), q] + ks + vs, q, out, length, held


def attend(place_of, q, kvs):
    seqs, span, _ = q.shape
    ins, _, out, length, held = attend_specs(span, kvs)
    cells = seqs * HEADS * span * length
    return pl.pallas_call(
        functools.partial(attend_kernel, len(kvs)),
        grid=(seqs, KV),
        in_specs=ins,
        out_specs=out,
        out_shape=jax.ShapeDtypeStruct((seqs, span, INNER), F32),
        scratch_shapes=held,
        compiler_params=pltpu.CompilerParams(vmem_limit_bytes=50 << 20),
        cost_estimate=pl.CostEstimate(
            flops=cells * 2 * (HD + VHEAD), bytes_accessed=cells, transcendentals=cells
        ),
        name="attend",
    )(place_of, q, *kvs, *kvs)


def attend_back_kernel(n, place_ref, q_ref, *refs):
    k_refs, v_refs, refs = refs[:n], refs[n : 2 * n], refs[2 * n :]
    o_ref, do_ref, dq_ref, dk_ref, dv_ref, mask, k_all, v_all, dk_sum, dv_sum = refs
    pl.when(first_step())(lambda: attend_mask(place_ref, mask))
    heads_in(k_refs, v_refs, k_all, v_all)
    k, v = k_all[...], v_all[...]
    for g in range(GROUP):
        q = q_ref[0, :, g * HD : (g + 1) * HD]
        do = do_ref[0, :, g * VHEAD : (g + 1) * VHEAD]
        o = o_ref[0, :, g * VHEAD : (g + 1) * VHEAD]
        s = scores_of(q, k) + mask[...]
        e = jnp.exp(s - jnp.max(s, axis=-1, keepdims=True))
        p = e * (1.0 / jnp.sum(e, axis=-1, keepdims=True))
        dp = scores_of(do, v)
        ds = (p * (dp - jnp.sum(do.astype(F32) * o, axis=-1, keepdims=True))).astype(BF16)
        dq = jnp.dot(ds, k, preferred_element_type=F32).astype(BF16)
        dq_ref[0, :, g * HD : (g + 1) * HD] = dq * jnp.asarray(HD**-0.5, BF16)
        dv = lax.dot_general(do, p.astype(BF16), (((0,), (0,)), ((), ())), preferred_element_type=F32)
        dk = lax.dot_general(q, ds, (((0,), (0,)), ((), ())), preferred_element_type=F32)
        if g == 0:
            dk_sum[...] = dk
            dv_sum[...] = dv
        else:
            dk_sum[...] += dk
            dv_sum[...] += dv
    if QWIDE > GROUP * HD:
        dq_ref[0, :, GROUP * HD :] = jnp.zeros((dq_ref.shape[1], QWIDE - GROUP * HD), BF16)
    dv_ref[0] = dv_sum[...].T.astype(BF16)
    dk = dk_sum[...].T.astype(BF16)

    @pl.when(pl.program_id(1) == 0)
    def _():
        dk_ref[...] = jnp.zeros_like(dk_ref)

    for h in range(KV):

        @pl.when(pl.program_id(1) == h)
        def _(h=h):
            dk_ref[0, :, h * HD : (h + 1) * HD] = dk


def attend_back(place_of, q, kvs, o, do):
    seqs, span, _ = q.shape
    ins, qs, out, length, held = attend_specs(span, kvs)
    cells = seqs * HEADS * span * length
    return pl.pallas_call(
        functools.partial(attend_back_kernel, len(kvs)),
        grid=(seqs, KV),
        in_specs=ins + [out, out],
        out_specs=[
            qs,
            pl.BlockSpec((1, length, KWIDE), lambda s, h: (s, 0, 0)),
            pl.BlockSpec((1, length, VHEAD), lambda s, h: (s, 0, h)),
        ],
        out_shape=[
            jax.ShapeDtypeStruct(q.shape, BF16),
            jax.ShapeDtypeStruct((seqs, length, KWIDE), BF16),
            jax.ShapeDtypeStruct((seqs, length, KV * VHEAD), BF16),
        ],
        scratch_shapes=held + [pltpu.VMEM((HD, length), F32), pltpu.VMEM((VHEAD, length), F32)],
        compiler_params=pltpu.CompilerParams(vmem_limit_bytes=50 << 20),
        cost_estimate=pl.CostEstimate(
            flops=cells * 2 * (3 * HD + 2 * VHEAD), bytes_accessed=cells, transcendentals=cells
        ),
        name="attend_back",
    )(place_of, q, *kvs, *kvs, o, do)


def rms_scale(value):
    return lax.rsqrt(jnp.mean(value * value, axis=-1, keepdims=True) + EPS)


def norm_back(value, scale, upstream):
    return scale * upstream - value * scale**3 * jnp.mean(upstream * value, axis=-1, keepdims=True)


def silu_pair(value):
    sigma = jax.nn.sigmoid(value)
    return (value * sigma, sigma * (1.0 + value * (1.0 - sigma)))


def matmul(left, right):
    return jnp.dot(left, right, preferred_element_type=F32)


def matmul_back(left, right):
    return lax.dot_general(left, right, (((1,), (1,)), ((), ())), preferred_element_type=F32)


def outer_sum(left, right):
    return lax.dot_general(left, right, (((0,), (0,)), ((), ())), preferred_element_type=F32)


def carried(states, sums, dec, later):
    mine = lax.axis_index("ctx")
    total = jnp.zeros(states[0].shape, F32)
    for r in range(1, lax.axis_size("ctx")):
        far = mine ^ r
        passed = jnp.zeros(sums[0].shape, F32)
        for q in range(1, lax.axis_size("ctx")):
            at = mine ^ q
            between = (at > mine) & (at < far) if later else (at < mine) & (at > far)
            passed = passed + jnp.where(between, sums[q], 0.0)
        reaches = far > mine if later else far < mine
        total = total + jnp.where(reaches, jnp.exp2(dec * passed) * states[r].astype(F32), 0.0)
    return total


def per_device(
    tokens,
    teacher,
    cotangent,
    valid,
    w_query,
    w_key,
    w_value,
    w_mixer,
    w_output,
    w_gate,
    w_up,
    w_down,
    w_select,
    w_step,
    log_decay,
    conv_taps,
    conv_bias,
    step_bias,
    skip_gain,
    beta_attn,
    beta_ssm,
    gain_first,
    gain_second,
):
    seqs, span, width = tokens.shape
    nctx, nbatch = lax.axis_size("ctx"), lax.axis_size("batch")
    rows = seqs * span
    scale = 1.0 / math.sqrt(HD)
    all_tokens = rows * nbatch * nctx
    order = [0]
    for bit in bits_of("ctx")[::-1]:
        order += [r ^ bit for r in order]
    place_of = jnp.stack([(lax.axis_index("ctx") ^ r) * span for r in order]).astype(jnp.int32)

    lines = jnp.concatenate(
        [w_step, log_decay, conv_taps]
        + [v[None] for v in (conv_bias, step_bias, skip_gain, beta_attn, beta_ssm)]
        + [w_select.T],
        axis=0,
    )
    n_lines, chan = lines.shape
    gains = jnp.stack([gain_first, gain_second])
    packed = jnp.concatenate(
        [lines, jnp.pad(gains, ((0, 0), (0, chan - gains.shape[1])))], axis=0
    )
    packed = jnp.pad(packed, ((0, -packed.shape[0] % 16), (0, -chan % (2 * LANE))))
    n_q, n_k, n_v, n_mixer = [w.shape[1] for w in (w_query, w_key, w_value, w_mixer)]
    ff = nctx * w_gate.shape[1]
    every, half = range(nctx), nctx // 2
    here = jnp.full((8, LANE), jnp.sum(valid.astype(F32)))
    shards = [w_query, w_key, w_value, w_mixer, w_output, w_gate, w_up, here]
    in_kv = pieces_of(1, n_k, every) + pieces_of(2, n_v, every, KWIDE)
    items = [
        packed,
        (in_kv, KWIDE + KV * VHEAD, True),
        (pieces_of(0, n_q, every, 0, GROUP * HD, QWIDE), KV * QWIDE, True),
        (pieces_of(3, n_mixer, range(half)), INNER, True),
        (pieces_of(3, n_mixer, range(half, nctx)), INNER, True),
        (pieces_of(4, w_output.shape[1], every), D, False),
        (
            pieces_of(5, w_gate.shape[1], every) + pieces_of(6, w_up.shape[1], every, ff),
            2 * ff,
            False,
        ),
        (pieces_of(7, LANE, every), nctx * LANE, True),
    ]
    program = (
        "c1 c2 c0 c7 l0 c1 c2 l1 c0 c7 c3 l2 l7 c5 c3 f0 c6 l3 l4 f1 f2 f7 e0 c5 c4 f3 c6 e1 e2 "
        "e7 c4 l6 f4 l5 e3 e4"
    )
    acts = {"c": "columns", "l": "launch", "f": "forward", "e": "last"}
    program = tuple((acts[word[0]], int(word[1:])) for word in program.split())
    f_packed, f_kv, f_q, f_conv, f_z, row_output, row_gate_up, counts = gather_all(
        shards, items, program, 0
    )
    f_kv, f_q, f_conv, f_z = [v.reshape(-1, v.shape[2]) for v in (f_kv, f_q, f_conv, f_z)]
    count = jnp.sum(counts[:, 0, ::LANE])
    get_output, get_gate_up = Gather(row_output), Gather(row_gate_up)
    get_down = Gather(None, w_down)
    f_conv = hold([get_down], f_conv)
    f_vectors = f_packed[:, :n_lines, :chan].transpose(1, 0, 2).reshape(n_lines, nbatch * chan)
    f_select = f_vectors[RANK + STATE + CONV + 5 :].T
    f_gains = f_packed[:, n_lines : n_lines + 2, : gains.shape[1]]
    f_gains = f_gains.transpose(1, 0, 2).reshape(2, -1)

    f_step = f_vectors[:RANK]
    f_decay = f_vectors[RANK : RANK + STATE].astype(F32)
    taps = f_vectors[RANK + STATE : RANK + STATE + CONV].astype(F32)
    f_conv_bias, f_step_bias, skip, beta_a, beta_s = [
        f_vectors[RANK + STATE + CONV + i].astype(F32) for i in range(5)
    ]
    gain_one, gain_two = f_gains[0].astype(F32), f_gains[1].astype(F32)
    decay = -jnp.exp(f_decay)
    dec = decay * LOG2E

    get_gate_up.step()
    x_flat = tokens.reshape(rows, D).astype(F32)
    scale1 = rms_scale(x_flat)
    normed1 = (x_flat * scale1 * gain_one).astype(BF16)
    conv_in = matmul(normed1, f_conv).astype(BF16).reshape(seqs, span, INNER)
    rim = shift(conv_in[:, span - (CONV - 1) :], "ctx", 1, False)
    conv_in, then1 = hold([], conv_in, normed1)
    kv_own = matmul(then1, f_kv).astype(BF16).reshape(seqs, span, KWIDE + KV * VHEAD)
    get_kv = FromCtx(kv_own)
    get_kv.step()
    q_heads = (matmul(then1, f_q) * scale).astype(BF16).reshape(seqs, span, KV * QWIDE)
    gate_z = matmul(then1, f_z).reshape(seqs, span, INNER)
    extended = jnp.concatenate([rim, conv_in], axis=1).astype(F32)
    pre_conv = f_conv_bias + sum((taps[tap] * extended[:, tap : tap + span] for tap in range(CONV)))
    conv_out, conv_slope = silu_pair(pre_conv)
    conv_out = hold([get_gate_up, get_kv], conv_out)

    get_kv.step()
    get_gate_up.step()
    get_output.step()
    get_down.step()
    conv_low = conv_out.reshape(rows, INNER).astype(BF16)
    projected = matmul(conv_low, f_select)
    rank_low = projected[:, :RANK].astype(BF16)
    coefs = projected[:, RANK:].reshape(seqs, span, 2, STATE, 1)
    bb = jnp.broadcast_to(coefs[:, :, 0], (seqs, span, STATE, LANE))
    cc = jnp.broadcast_to(coefs[:, :, 1], (seqs, span, STATE, LANE))
    step_pre = matmul(rank_low, f_step) + f_step_bias
    steps = jax.nn.softplus(step_pre).reshape(seqs, span, INNER)
    step_sums = jnp.sum(steps, axis=1, keepdims=True)
    final = scan_final(steps, conv_out, bb, dec)
    final = hold([get_output, get_kv, get_gate_up, get_down], final)

    sums_high = step_sums.astype(BF16)
    sums_low = (step_sums - sums_high.astype(F32)).astype(BF16)
    get_state = FromCtx(jnp.concatenate([final.astype(BF16), sums_high, sums_low], axis=1))
    get_state.step()
    get_output.step()
    get_down.step()
    get_kv.finish()
    kvs = list(get_kv.live.values())
    attn = attend(place_of, q_heads, kvs).reshape(rows, INNER)
    attn = hold([get_state, get_output, get_down], attn)
    get_state.step()
    get_down.step()
    f_gate, f_up = hold([get_state], *get_gate_up.whole(2, ff, ff))

    states = get_state.finish()
    all_sums = {
        r: v[:, STATE : STATE + 1].astype(F32) + v[:, STATE + 1 :].astype(F32)
        for r, v in states.items()
    }
    entry = carried({r: v[:, :STATE] for r, v in states.items()}, all_sums, dec, False)
    scan_out = scan_out_of(steps, conv_out, bb, cc, dec, entry)
    (f_output,) = get_output.whole(1, D)
    scan_out, f_output = hold([get_down], scan_out, f_output)
    get_down.step()

    gate_act, gate_slope = silu_pair(gate_z)
    pre_gate = scan_out + skip * conv_out
    ssm_flat = (pre_gate * gate_act).reshape(rows, INNER)
    attn_scale = rms_scale(attn)
    attn_norm = attn * attn_scale
    ssm_scale = rms_scale(ssm_flat)
    ssm_norm = ssm_flat * ssm_scale
    merged = (0.5 * (attn_norm * beta_a + ssm_norm * beta_s)).astype(BF16)
    hidden1 = x_flat + matmul(merged, f_output)

    scale2 = rms_scale(hidden1)
    normed2 = (hidden1 * scale2 * gain_two).astype(BF16)
    gate_pre = matmul(normed2, f_gate)
    up_pre = matmul(normed2, f_up)
    gate_act2, gate_slope2 = silu_pair(gate_pre)
    inner_ff = (gate_act2 * up_pre).astype(BF16)
    (f_down,) = get_down.whole(3, D)
    hidden2 = hidden1 + matmul(inner_ff, f_down)
    output = hidden2.astype(BF16).reshape(seqs, span, D)
    weight_rows = valid.reshape(rows, 1).astype(F32)
    diff = hidden2 - teacher.reshape(rows, D).astype(F32)
    loss_local = jnp.sum(weight_rows * diff * diff)
    loss_sum = total_over(jnp.full((8, LANE), loss_local), ("batch", "ctx"))[0, 0]

    seed = cotangent.reshape(rows, D).astype(F32) + all_tokens / count * weight_rows * diff
    seed_low = seed.astype(BF16)
    put_down = Scatter(inner_ff, seed_low, w_down.shape[1])
    put_down.step()
    d_inner = matmul_back(seed_low, f_down)
    d_gate = (d_inner * up_pre * gate_slope2).astype(BF16)
    d_up = (d_inner * gate_act2).astype(BF16)
    d_gate, d_up = hold([put_down], d_gate, d_up)

    put_down.step()
    put_gate = Scatter(normed2, d_gate, w_gate.shape[1])
    put_gate.step()
    put_up = Scatter(normed2, d_up, w_up.shape[1])
    put_up.step()
    d_norm2 = matmul_back(d_gate, f_gate) + matmul_back(d_up, f_up)
    g_gain_second = jnp.sum(d_norm2 * hidden1 * scale2, axis=0, keepdims=True)
    d_hidden1 = seed + norm_back(hidden1, scale2, d_norm2 * gain_two)
    d_hidden1 = hold([put_down, put_gate, put_up], d_hidden1)

    put_down.step()
    put_gate.step()
    d_branch = d_hidden1.astype(BF16)
    put_output = Scatter(merged, d_branch, w_output.shape[1])
    put_output.step()
    d_merged = matmul_back(d_branch, f_output)
    g_beta_attn = jnp.sum(0.5 * d_merged * attn_norm, axis=0, keepdims=True)
    g_beta_ssm = jnp.sum(0.5 * d_merged * ssm_norm, axis=0, keepdims=True)
    d_attn = norm_back(attn, attn_scale, 0.5 * d_merged * beta_a).astype(BF16)
    d_ssm = norm_back(ssm_flat, ssm_scale, 0.5 * d_merged * beta_s).reshape(seqs, span, INNER)
    d_pre_gate = d_ssm * gate_act
    d_gate_z = (d_ssm * pre_gate * gate_slope).reshape(rows, INNER).astype(BF16)
    g_skip = jnp.sum(d_pre_gate * conv_out, axis=(0, 1))[None]
    adjoint = scan_adjoint(steps, d_pre_gate, cc, dec)
    d_attn, d_pre_gate, d_gate_z, adjoint = hold(
        [put_down, put_gate, put_output], d_attn, d_pre_gate, d_gate_z, adjoint
    )

    put_down.step()
    put_gate.step()
    put_up.step()
    get_adjoint = FromCtx(adjoint.astype(BF16))
    get_adjoint.step()
    dq, dk, dv = attend_back(
        place_of, q_heads, kvs, attn.reshape(seqs, span, INNER), d_attn.reshape(seqs, span, INNER)
    )
    dq, dk, dv = hold([put_down, put_gate, put_up, get_adjoint], dq, dk, dv)
    get_adjoint.step()
    put_down.step()
    put_gate.step()
    put_up.step()
    put_output.step()
    dq = dq.reshape(rows, KV * QWIDE)
    g_q = outer_sum(normed1, dq).astype(BF16)
    g_z = outer_sum(normed1, d_gate_z).astype(BF16)
    d_norm1 = matmul_back(dq, f_q) + matmul_back(d_gate_z, f_z)
    d_norm1, g_q, g_z = hold(
        [get_adjoint, put_down, put_gate, put_up, put_output], d_norm1, g_q, g_z
    )

    d_kv = jnp.concatenate([dk, dv], axis=-1).reshape(seqs, nctx, span, KWIDE + KV * VHEAD)
    put_kv = ToCtx({r: d_kv[:, i] for i, r in enumerate(order)})
    put_kv.step()
    put_gate.step()
    put_up.step()
    put_output.step()
    arrive = carried(get_adjoint.finish(), all_sums, dec, True)
    g_drive, g_steps, g_b, g_c, grad_decay = scan_back(
        steps, conv_out, d_pre_gate, bb, cc, dec, entry, arrive
    )
    g_drive, g_steps, g_b, g_c = hold(
        [put_gate, put_up, put_output, put_kv], g_drive, g_steps, g_b, g_c
    )

    put_kv.step()
    put_up.step()
    put_output.step()
    d_step_pre = g_steps.reshape(rows, INNER) * jax.nn.sigmoid(step_pre)
    g_step_bias = jnp.sum(d_step_pre, axis=0, keepdims=True)
    d_step_low = d_step_pre.astype(BF16)
    d_rank = matmul_back(d_step_low, f_step)
    d_projected = jnp.concatenate(
        [d_rank] + [jnp.sum(g, axis=-1).reshape(rows, STATE) for g in (g_b, g_c)], axis=1
    ).astype(BF16)
    d_conv = (
        g_drive
        + d_pre_gate * skip
        + matmul_back(d_projected, f_select).reshape(seqs, span, INNER)
    )
    d_pre_conv = hold([put_kv], d_conv * conv_slope)
    g_conv_bias = jnp.sum(d_pre_conv, axis=(0, 1))[None]
    g_taps = [
        jnp.sum(d_pre_conv * extended[:, tap : tap + span], axis=(0, 1))[None]
        for tap in range(CONV)
    ]
    d_extended = sum(
        (
            jnp.pad(taps[tap] * d_pre_conv, ((0, 0), (tap, CONV - 1 - tap), (0, 0)))
            for tap in range(CONV)
        )
    )
    back_rim = shift(d_extended[:, : CONV - 1].astype(BF16), "ctx", -1, False)
    d_conv_in = d_extended[:, CONV - 1 :].at[:, span - (CONV - 1) :].add(back_rim.astype(F32))
    d_conv_in = d_conv_in.reshape(rows, INNER).astype(BF16)
    d_conv_in = hold([put_output, put_up], d_conv_in)

    put_output.step()
    d_kv_own = put_kv.result().astype(BF16).reshape(rows, KWIDE + KV * VHEAD)
    d_norm1 = d_norm1 + matmul_back(d_kv_own, f_kv) + matmul_back(d_conv_in, f_conv)
    g_gain_first = jnp.sum(d_norm1 * x_flat * scale1, axis=0, keepdims=True)
    d_tokens = d_hidden1 + norm_back(x_flat, scale1, d_norm1 * gain_one)
    tokens_grad = d_tokens.astype(BF16).reshape(seqs, span, D)
    g_conv = outer_sum(normed1, d_conv_in).astype(BF16)
    g_kv = outer_sum(normed1, d_kv_own).astype(BF16)

    pad_rank, pad_sel = -RANK % 8, -(RANK + 2 * STATE) % 8
    g_step = outer_sum(jnp.pad(rank_low, ((0, 0), (0, pad_rank))), d_step_low)
    g_select = outer_sum(jnp.pad(d_projected, ((0, 0), (0, pad_sel))), conv_low)
    own_gain = D // nbatch
    gains_wide = [
        jnp.pad(g.reshape(nbatch, own_gain), ((0, 0), (0, chan - own_gain))).reshape(1, INNER)
        for g in (g_gain_first, g_gain_second)
    ]
    few = g_taps + [g_conv_bias, g_step_bias, g_skip, g_beta_attn, g_beta_ssm] + gains_wide
    few.append(jnp.zeros((-len(few) % 8, INNER), F32))
    at_sel = RANK + pad_rank
    at_dec = at_sel + RANK + 2 * STATE + pad_sel
    at_few = at_dec + STATE

    small = jnp.concatenate(
        [g_step, g_select, jnp.sum(grad_decay, axis=0) * decay] + few, axis=0
    ).astype(BF16)
    small = small.reshape(small.shape[0], nbatch, chan).transpose(1, 0, 2)
    small = jnp.pad(small, ((0, 0), (0, -small.shape[1] % 16), (0, -chan % (2 * LANE))))
    small = small.reshape(-1, small.shape[2])
    small = hold([put_output], small)
    terms = [g_conv, g_z, g_q, g_kv, small]
    items = [items[3][0], items[4][0], items[2][0], items[1][0], ()]
    program = "b4 b3 b2 b1 b0 f4 f3 f2 f1 s4 f0 s3 t4 s2 t3 p1 p2 t2 p0 s1 e4 t1 s0 t0 p3 e1 e2 e0 e3"
    program = tuple((word[0], int(word[1:])) for word in program.split())
    (r_down,), (r_gate,), (r_up,), (r_output,) = [
        put.result() for put in (put_down, put_gate, put_up, put_output)
    ]
    r_query, r_key, r_value, r_mixer, small = reduce_all(
        terms, items, (n_q, n_k, n_v, n_mixer), program, 4
    )
    small = small[:, :chan]
    return (
        output,
        loss_sum / (count * D),
        tokens_grad,
        r_query,
        r_key,
        r_value,
        r_mixer,
        r_output,
        r_gate,
        r_up,
        r_down,
        small[at_sel : at_sel + RANK + 2 * STATE].T,
        small[:RANK],
        small[at_dec:at_few],
        small[at_few : at_few + CONV],
        *[small[at_few + CONV + i] for i in range(5)],
        *[small[at_few + CONV + 5 + i, :own_gain] for i in range(2)],
    )


def solution(mesh):
    by_pos = P("batch", "ctx", None)
    by_both = P("batch", "ctx")
    by_row, by_col, by_one = P("batch", None), P(None, "batch"), P("batch")
    weights = (by_both,) * 8 + (by_row,) + (by_col,) * 3 + (by_one,) * 7
    return jax.shard_map(
        per_device,
        mesh=mesh,
        in_specs=(by_pos, by_pos, by_pos, by_both) + weights,
        out_specs=(by_pos, P(), by_pos) + weights,
        check_vma=False,
    )
```

```python
import functools
import math

import jax
import jax.numpy as jnp
from jax import lax
from jax.experimental import pallas as pl
from jax.experimental.pallas import tpu as pltpu
from jax.sharding import PartitionSpec as P

D = 1600
HEADS = 25
KV = 5
HD = 64
INNER = 3200
STATE = 16
CONV = 4
RANK = 100
WINDOW = 1024
GROUP = HEADS // KV
VHEAD = INNER // HEADS
LANE = 128

EPS = 1e-05
F32 = jnp.float32
BF16 = jnp.bfloat16
LOG2E = math.log2(math.e)
LN2 = math.log(2.0)
MESH = pl.DeviceIdType.MESH


def permute_bit(value, axis, bit):
    count = lax.axis_size(axis)
    return lax.ppermute(value, axis, [(i, i ^ bit) for i in range(count)])


def shift(value, axis, steps, wrap):
    count = lax.axis_size(axis)
    pairs = [(i, (i + steps) % count) for i in range(count) if wrap or 0 <= i + steps < count]
    return lax.ppermute(value, axis, pairs)


def bits_of(axis):
    count = lax.axis_size(axis)
    return [1 << k for k in range(count.bit_length() - 1)]


def from_ctx(blocks):
    count, mine = lax.axis_size("ctx"), lax.axis_index("ctx")
    out = []
    for at in range(count):
        block = blocks[0]
        for r in range(1, count):
            block = jnp.where(mine ^ r == at, blocks[r], block)
        out.append(block)
    return out


def gather_columns(shard):
    return lax.all_gather(shard, "ctx", axis=0)


def gather_rows(block):
    return lax.all_gather(block, "batch", axis=0, tiled=True)


def copy_rows(rows, copy):
    whole = rows // 16 * 16

    def body(i, _):
        copy(pl.multiple_of(i * 16, 16), 16)
        return 0

    lax.fori_loop(0, whole // 16, body, 0)
    if whole < rows:
        copy(whole, rows - whole)


def pieces_of(part, n, places, at=0, group=0, wide=0):
    out = []
    for i, place in enumerate(places):
        lo = 0
        while lo < n:
            col = i * n + lo
            hi, target = n, at + col
            if group:
                hi = min(n, (col // group + 1) * group - i * n)
                target = at + col // group * wide + col % group
            out.append((part, place, lo, hi, target))
            lo = hi
    return tuple(out)


def gather_kernel(n_parts, items, program, *refs):
    plain = [i for i, (pieces, _) in enumerate(items) if not pieces]
    shards, refs = refs[:n_parts], refs[n_parts:]
    direct, refs = dict(zip(plain, refs)), refs[len(plain) :]
    wholes, refs = refs[: len(items)], refs[len(items) :]
    parts, refs = refs[:n_parts], refs[n_parts:]
    blocks, sems = refs[: len(items)], refs[len(items) :]
    z_own, z_send, z_recv, b_send, b_recv, b_own = sems
    b, c = lax.axis_index("batch"), lax.axis_index("ctx")
    bits = bits_of("ctx")[::-1]

    barrier = pltpu.get_barrier_semaphore()
    peers = [{"ctx": c ^ bit} for bit in bits] + [{"batch": b ^ bit} for bit in (1, 2, 4)]
    for device in peers:
        pl.semaphore_signal(barrier, inc=1, device_id=device, device_id_type=MESH)
    pl.semaphore_wait(barrier, len(peers))

    started, stores = [], []

    def remote(source, target, send_sem, recv_sem, device):
        copy = pltpu.make_async_remote_copy(
            src_ref=source,
            dst_ref=target,
            send_sem=send_sem,
            recv_sem=recv_sem,
            device_id=device,
            device_id_type=MESH,
        )
        copy.start()
        started.append(copy)
        return copy

    come, reached = {}, {}

    def columns(part):
        shard, slot = shards[part], parts[part]
        stage = reached.get(part, 0)
        bit = bits[stage]
        if stage == 0:
            own = pltpu.make_async_copy(shard, slot.at[c], z_own.at[part])
            own.start()
            come[part] = {0: own.wait}
        for r in sorted(come[part]):
            if r:
                come[part][r]()
                come[part][r] = lambda: None
            copy = remote(
                slot.at[c ^ r] if r else shard,
                slot.at[c ^ r],
                z_send.at[part, r ^ bit],
                z_recv.at[part, r ^ bit],
                {"ctx": c ^ bit},
            )
            come[part][r ^ bit] = copy.wait_recv
        reached[part] = stage + 1

    flights = {}

    def send(item, slot, source, target, bit):
        return remote(
            source, target, b_send.at[item, slot], b_recv.at[item, slot], {"batch": b ^ bit}
        )

    def keep(item, slot, r):
        there = wholes[item].at[b ^ r]
        store = pltpu.make_async_copy(blocks[item].at[slot], there, b_own.at[item, slot])
        store.start()
        stores.append(store)
        return send(item, 4 + slot, blocks[item].at[slot], there, 1)

    def launch(item):
        pieces, rows = items[item]
        block = blocks[item]
        if pieces:
            for part in sorted({piece[0] for piece in pieces}):
                for r in come[part]:
                    come[part][r]()
                    come[part][r] = lambda: None
            ends = sorted((at, at + hi - lo) for _, _, lo, hi, at in pieces)
            ends.append((block.shape[2], 0))
            gaps = [(end, ends[i + 1][0]) for i, (_, end) in enumerate(ends[:-1])]

            def relay(start, count):
                for part, place, lo, hi, at in pieces:
                    block[0, pl.ds(start, count), at : at + hi - lo] = parts[part][
                        place, pl.ds(start, count), lo:hi
                    ]
                for lo, hi in gaps:
                    if lo < hi:
                        block[0, pl.ds(start, count), lo:hi] = jnp.zeros((count, hi - lo), block.dtype)

            copy_rows(block.shape[1], relay)
        else:
            own = pltpu.make_async_copy(direct[item], block.at[0], b_own.at[item, 4])
            own.start()
            own.wait()
        if rows:
            flights[item] = [
                send(item, 1, block.at[0], block.at[1], 2),
                send(item, 2, block.at[0], block.at[2], 4),
            ]
            flights[item].append(keep(item, 0, 0))
        else:
            store = pltpu.make_async_copy(block.at[0], wholes[item], b_own.at[item, 0])
            store.start()
            stores.append(store)

    def forward(item):
        block, flight = blocks[item], flights[item]
        n = block.shape[2]
        half = n // 2 // LANE * LANE
        flight[0].wait_recv()
        left, right = (slice(None), slice(0, half)), (slice(None), slice(half, n))
        flight.append(send(item, 3, block.at[1, *left], block.at[3, *left], 4))
        flight.append(keep(item, 1, 2))
        flight[1].wait_recv()
        flight.append(send(item, 0, block.at[2, *right], block.at[3, *right], 2))
        flight.append(keep(item, 2, 4))

    def last(item):
        flight = flights[item]
        flight[3].wait_recv()
        flight[5].wait_recv()
        flight.append(keep(item, 3, 6))

    acts = {"columns": columns, "launch": launch, "forward": forward, "last": last}
    for act, which in program:
        acts[act](which)
    for flight in flights.values():
        for key in (2, 4, 6, 7):
            flight[key].wait_recv()
    for copy in stores:
        copy.wait()
    for copy in started:
        copy.wait_send()


def gather_all(shards, items, program, collective_id):
    count, nbatch = lax.axis_size("ctx"), lax.axis_size("batch")
    if nbatch != 8:
        found, out = [gather_columns(shard) for shard in shards], []
        for item in items:
            if not isinstance(item, tuple):
                out.append(gather_rows(item).reshape(nbatch, *item.shape))
                continue
            pieces, n, rows = item
            block = jnp.zeros((found[pieces[0][0]].shape[1], n), shards[pieces[0][0]].dtype)
            for part, place, lo, hi, at in pieces:
                block = block.at[:, at : at + hi - lo].set(found[part][place, :, lo:hi])
            out.append(gather_rows(block).reshape(nbatch, *block.shape) if rows else block)
        return out
    flat, kinds, shapes, blocks = list(shards), [], [], []
    for item in items:
        if isinstance(item, tuple):
            pieces, n, rows = item
            k, dtype = shards[pieces[0][0]].shape[0], shards[pieces[0][0]].dtype
        else:
            (k, n), pieces, rows, dtype = item.shape, (), True, item.dtype
            flat.append(item)
        kinds.append((pieces, rows))
        blocks.append(pltpu.VMEM((4 if rows else 1, k, n), dtype))
        shapes.append(jax.ShapeDtypeStruct((nbatch, k, n) if rows else (k, n), dtype))
    dma = pltpu.SemaphoreType.DMA
    hbm = pl.BlockSpec(memory_space=pl.ANY)
    return pl.pallas_call(
        functools.partial(gather_kernel, len(shards), tuple(kinds), program),
        in_specs=[hbm] * len(flat),
        out_specs=[hbm] * len(shapes),
        out_shape=shapes,
        scratch_shapes=[pltpu.VMEM((count,) + w.shape, w.dtype) for w in shards]
        + blocks
        + [dma((len(shards),)), dma((len(shards), count)), dma((len(shards), count))]
        + [dma((len(shapes), 8)), dma((len(shapes), 8)), dma((len(shapes), 5))],
        compiler_params=pltpu.CompilerParams(
            collective_id=collective_id, has_side_effects=True, vmem_limit_bytes=56 << 20
        ),
        name="gather_weights",
    )(*flat)


class Staged:
    def __init__(self, live):
        self.live = live
        self.fresh = list(live)
        self.stage = 0

    def fly(self, key, value):
        self.live[key] = value
        self.fresh.append(key)


def hold(staged, *values):
    flying = [[item.live[key] for key in item.fresh] for item in staged]
    flying, values = lax.optimization_barrier((flying, values))
    for item, arrived in zip(staged, flying):
        item.live.update(zip(item.fresh, arrived))
        item.fresh = []
    return values[0] if len(values) == 1 else values


class FromCtx(Staged):
    def __init__(self, value):
        super().__init__({0: value[None]})
        self.orders = [[0]]

    def step(self):
        bits = bits_of("ctx")[::-1]
        if self.stage < len(bits):
            bit = bits[self.stage]
            sent = list(self.live.values())
            sent = jnp.concatenate(sent, axis=0) if len(sent) > 1 else sent[0]
            self.orders.append([r ^ bit for order in self.orders for r in order])
            self.fly(self.stage + 1, permute_bit(sent, "ctx", bit))
        self.stage += 1

    def finish(self):
        while self.stage < len(bits_of("ctx")):
            self.step()
        return {
            r: self.live[i][j] for i, order in enumerate(self.orders) for j, r in enumerate(order)
        }


class ToCtx(Staged):
    def __init__(self, blocks):
        super().__init__({(r, 0): block for r, block in blocks.items()})

    def total(self, r):
        terms = [v.astype(F32) for key, v in self.live.items() if key[0] == r]
        return functools.reduce(jnp.add, terms)

    def step(self):
        bits = bits_of("ctx")
        if self.stage < len(bits):
            bit = bits[self.stage]
            which = sorted({key[0] for key in self.live if key[0] & bit})
            sent = jnp.stack([self.total(r).astype(BF16) for r in which])
            got = permute_bit(sent, "ctx", bit)
            self.live = {key: v for key, v in self.live.items() if not key[0] & bit}
            self.fresh = [key for key in self.fresh if key in self.live]
            for i, r in enumerate(which):
                self.fly((r ^ bit, self.stage + 1), got[i])
        self.stage += 1

    def result(self):
        while self.stage < len(bits_of("ctx")):
            self.step()
        return self.total(0)


def assemble_kernel(names, cuts, *refs):
    parts, wholes = refs[: len(names)], refs[len(names) : len(names) + len(cuts)]
    held, sems_in, sems_out, send_sems, recv_sems = refs[-5:]
    b = lax.axis_index("batch")
    other = {"batch": b ^ 1}
    ins = {}
    for i, (part, (r, lo)) in enumerate(zip(parts, names)):
        n = part.shape[1]
        slot = held.at[r // 2] if n == held.shape[2] else held.at[r // 2, :, lo : lo + n]
        ins.setdefault(r, []).append(pltpu.make_async_copy(part, slot, sems_in.at[i]))
        ins[r][-1].start()
    barrier = pltpu.get_barrier_semaphore()
    pl.semaphore_signal(barrier, inc=1, device_id=other, device_id_type=MESH)
    pl.semaphore_wait(barrier, 1)
    waits = []
    for r, copies in ins.items():
        for copy in copies:
            copy.wait()
        for i, (whole, (lo, hi)) in enumerate(zip(wholes, cuts)):
            slot = held.at[r // 2] if len(cuts) == 1 else held.at[r // 2, :, lo:hi]
            goes = pltpu.make_async_remote_copy(
                src_ref=slot,
                dst_ref=whole.at[b ^ r],
                send_sem=send_sems.at[i, r // 2],
                recv_sem=recv_sems.at[i, r // 2],
                device_id=other,
                device_id_type=MESH,
            )
            stays = pltpu.make_async_copy(slot, whole.at[b ^ r], sems_out.at[i, r // 2])
            goes.start()
            stays.start()
            waits += [goes, stays]
    for copy in waits:
        copy.wait()


def assemble(parts, widths, collective_id):
    names = tuple(parts)
    k, n = parts[(0, 0)].shape
    cuts = tuple((sum(widths[:i]), sum(widths[: i + 1])) for i in range(len(widths)))
    hbm = pl.BlockSpec(memory_space=pl.ANY)
    dma = pltpu.SemaphoreType.DMA
    wholes = pl.pallas_call(
        functools.partial(assemble_kernel, names, cuts),
        in_specs=[hbm] * len(names),
        out_specs=[hbm] * len(cuts),
        out_shape=[jax.ShapeDtypeStruct((8, k, width), BF16) for width in widths],
        scratch_shapes=[pltpu.VMEM((4, k, n), BF16), dma((len(names),)), dma((len(cuts), 4))]
        + [dma((len(cuts), 4)), dma((len(cuts), 4))],
        compiler_params=pltpu.CompilerParams(
            collective_id=collective_id, has_side_effects=True, vmem_limit_bytes=40 << 20
        ),
        cost_estimate=pl.CostEstimate(flops=0, bytes_accessed=32 * k * n, transcendentals=0),
        name="assemble",
    )(*[parts[name] for name in names])
    return [whole.reshape(8 * k, -1) for whole in wholes]


class Gather(Staged):
    def __init__(self, block, shard=None):
        self.block, self.shard = block, shard
        self.columns = None if shard is None else FromCtx(shard)
        super().__init__({(0, 0): block} if shard is None else self.columns.live)

    def step(self):
        if lax.axis_size("batch") != 8:
            return
        if self.columns:
            if self.columns.stage < len(bits_of("ctx")):
                self.columns.live, self.columns.fresh = self.live, []
                self.columns.step()
                self.live, self.fresh = self.columns.live, self.columns.fresh
                return
            self.columns.live = self.live
            self.live = {(0, 0): jnp.concatenate(from_ctx(self.columns.finish()), axis=1)}
            self.columns, self.fresh = None, []
        live, block = self.live, self.live[(0, 0)]
        if self.stage == 0:
            for bit in (2, 4):
                self.fly((bit, 0), permute_bit(block, "batch", bit))
        elif self.stage == 1:
            n = block.shape[1]
            half = n // 2 // LANE * LANE
            self.fly((6, 0), permute_bit(live[(2, 0)][:, :half], "batch", 4))
            self.fly((6, half), permute_bit(live[(4, 0)][:, half:], "batch", 2))
        self.stage += 1

    def whole(self, collective_id, *widths):
        if lax.axis_size("batch") == 8:
            return assemble(self.live, widths, collective_id)
        block = self.block
        if self.shard is not None:
            block = jnp.concatenate(list(gather_columns(self.shard)), axis=1)
        whole = gather_rows(block)
        return jnp.split(whole, [sum(widths[:i]) for i in range(1, len(widths))], axis=1)


def ctx_terms(own, columns):
    nctx, mine = lax.axis_size("ctx"), lax.axis_index("ctx")
    at, cuts = 0, []
    for n in columns:
        cuts.append([own[:, at + c * n : at + (c + 1) * n] for c in range(nctx)])
        at += nctx * n
    parts = [jnp.concatenate(cut, axis=1) if len(cut) > 1 else cut[0] for cut in zip(*cuts)]
    blocks = {}
    for r in range(nctx):
        blocks[r] = parts[0]
        for c in range(1, nctx):
            blocks[r] = jnp.where(mine ^ r == c, parts[c], blocks[r])
    return ToCtx(blocks)


class Scatter(Staged):
    def __init__(self, left, right, *columns, trim=None):
        count = lax.axis_size("batch")
        super().__init__({})
        self.columns, self.trim = columns, trim
        self.tall, self.right = left.T.reshape(count, -1, left.shape[0]), right
        self.arrived = {}
        self.spread = None

    def rows_of(self, which):
        mine = lax.axis_index("batch")
        return jnp.concatenate(
            [lax.dynamic_index_in_dim(self.tall, mine ^ r, 0, keepdims=False) for r in which], axis=0
        )

    def part(self, which, lo, hi):
        k = self.tall.shape[1]
        own = matmul(self.rows_of(which), self.right[:, lo:hi])
        for key, order in self.arrived.items():
            if key[0] in (lo, -1):
                off = lo if key[0] == -1 else 0
                pieces = [
                    self.live[key][
                        order.index(r) * k : (order.index(r) + 1) * k, off : off + hi - lo
                    ]
                    for r in which
                ]
                own = own + jnp.concatenate(pieces, axis=0).astype(F32)
        return own

    def step(self):
        stage = self.stage
        self.stage += 1
        count, bits = lax.axis_size("batch"), bits_of("batch")
        n = self.right.shape[1]
        cut = n // 2 // LANE * LANE
        halves = ((0, cut, bits[1:]), (cut, n, bits[:0:-1]))
        if self.stage > len(bits) + 1 and not self.spread:
            return
        if count != 8 and stage <= len(bits):
            self.stage = len(bits) + 1
            whole = matmul(self.tall.reshape(-1, self.tall.shape[2]), self.right).astype(BF16)
            own = lax.psum_scatter(whole, "batch", scatter_dimension=0, tiled=True)
            self.live = {"own": self.trim(own) if self.trim else own}
            if self.columns:
                self.to_ctx(self.live["own"])
        elif stage == 0:
            odd = [r for r in range(count) if r & 1]
            sent = matmul(self.rows_of(odd), self.right).astype(BF16)
            self.fly((-1, 0), permute_bit(sent, "batch", 1))
            self.arrived[(-1, 0)] = [r ^ 1 for r in odd]
        elif stage < len(bits):
            fresh = {}
            for lo, hi, order in halves:
                gone, bit = sum(order[: stage - 1]), order[stage - 1]
                which = [r for r in range(count) if not r & (gone | 1) and r & bit]
                fresh[(lo, stage)] = permute_bit(self.part(which, lo, hi).astype(BF16), "batch", bit)
                self.arrived[(lo, stage)] = [r ^ bit for r in which]
            for key, value in fresh.items():
                self.fly(key, value)
        elif stage == len(bits):
            own = jnp.concatenate([self.part([0], lo, hi) for lo, hi, _ in halves], axis=1)
            own = own.astype(BF16)
            self.live, self.fresh = {"own": self.trim(own) if self.trim else own}, []
            if self.columns:
                self.to_ctx(self.live["own"])
                self.step()
        elif self.spread:
            self.spread.live, self.spread.fresh = self.live, []
            self.spread.step()
            self.live, self.fresh = self.spread.live, self.spread.fresh

    def to_ctx(self, own):
        self.spread = ctx_terms(own, self.columns)
        self.live, self.fresh = self.spread.live, []

    def blocks(self, *columns):
        while self.stage <= len(bits_of("batch")):
            self.step()
        terms = ctx_terms(self.live["own"], columns).live
        return {key[0]: block for key, block in terms.items()}

    def result(self):
        while self.stage <= len(bits_of("batch")) or not self.spread:
            self.step()
        self.spread.live = self.live
        total, out = self.spread.result(), []
        for n in self.columns:
            at = sum(v.shape[1] for v in out)
            out.append(total[:, at : at + n])
        return out


def reduce_kernel(n_parts, n_late, items, program, *refs):
    n = len(items)
    plain = [i for i, pieces in enumerate(items) if not pieces]
    nctx = lax.axis_size("ctx")
    n_slots = n_parts + len(plain) + n_late
    terms, tile, refs = refs[:n], refs[n], refs[n + 1 :]
    lates, refs = refs[: n_late * nctx], refs[n_late * nctx :]
    outs, refs = refs[:n_slots], refs[n_slots:]
    tile_out, refs = refs[0], refs[1:]
    accs, refs = refs[:n], refs[n:]
    firsts, refs = refs[:n], refs[n:]
    seconds, refs = refs[:n], refs[n:]
    thirds, refs = refs[:n], refs[n:]
    parts, refs = refs[:n_parts], refs[n_parts:]
    lands, refs = refs[:n_slots], refs[n_slots:]
    load, b_send, b_recv, z_send, z_recv, held, came, m_send, m_recv = refs
    b, c = lax.axis_index("batch"), lax.axis_index("ctx")

    barrier = pltpu.get_barrier_semaphore()
    peers = [{"ctx": c ^ r} for r in range(1, nctx)] + [{"batch": b ^ bit} for bit in (1, 2, 4)]
    for device in peers:
        pl.semaphore_signal(barrier, inc=1, device_id=device, device_id_type=MESH)
    pl.semaphore_wait(barrier, len(peers))

    started = []

    def remote(source, target, send_sem, recv_sem, device):
        copy = pltpu.make_async_remote_copy(
            src_ref=source,
            dst_ref=target,
            send_sem=send_sem,
            recv_sem=recv_sem,
            device_id=device,
            device_id_type=MESH,
        )
        copy.start()
        started.append(copy)
        return copy

    def send(item, slot, source, target, bit):
        return remote(
            source, target, b_send.at[item, slot], b_recv.at[item, slot], {"batch": b ^ bit}
        )

    def halves(item):
        width = accs[item].shape[2]
        cut = width // 2 // LANE * LANE
        return (0, cut), (cut, width)

    def add(to, j, other, i, lo, hi):
        def rows(start, count):
            at = pl.ds(start, count)
            total = to[j, at, lo:hi].astype(F32) + other[i, at, lo:hi].astype(F32)
            to[j, at, lo:hi] = total.astype(BF16)

        copy_rows(to.shape[1], rows)

    flights, z_flights, owns = {}, {}, {}

    def begin(item):
        copies = []
        for j in range(4):
            own = pltpu.make_async_copy(terms[item].at[b ^ (2 * j)], accs[item].at[j], load.at[item, j])
            own.start()
            copies.append(own)
        for j in range(4):
            copies.append(send(item, j, terms[item].at[b ^ (2 * j + 1)], firsts[item].at[j], 1))
        flights[item] = copies

    def sub(ref, j, span):
        return ref.at[j, :, span[0] : span[1]]

    def first(item):
        acc, flight = accs[item], flights[item]
        left, right = halves(item)
        for j in (3, 1, 2, 0):
            flight[j].wait()
            flight[4 + j].wait_recv()
            add(acc, j, firsts[item], j, 0, acc.shape[2])
            if j == 1:
                after = [
                    send(item, 4, sub(acc, 1, left), sub(seconds[item], 0, left), 2),
                    send(item, 5, sub(acc, 3, left), sub(seconds[item], 1, left), 2),
                ]
            if j == 2:
                after += [
                    send(item, 6, sub(acc, 2, right), sub(seconds[item], 0, right), 4),
                    send(item, 7, sub(acc, 3, right), sub(seconds[item], 1, right), 4),
                ]
        flights[item] = after

    def second(item):
        acc, flight = accs[item], flights[item]
        left, right = halves(item)
        flight[1].wait_recv()
        add(acc, 2, seconds[item], 1, *left)
        after = [send(item, 8, sub(acc, 2, left), sub(thirds[item], 0, left), 4)]
        flight[3].wait_recv()
        add(acc, 1, seconds[item], 1, *right)
        after.append(send(item, 9, sub(acc, 1, right), sub(thirds[item], 0, right), 2))
        flight[0].wait_recv()
        flight[2].wait_recv()
        add(acc, 0, seconds[item], 0, 0, acc.shape[2])
        flights[item] = after

    def third(item):
        acc = accs[item]
        for copy in flights[item]:
            copy.wait_recv()
        add(acc, 0, thirds[item], 0, 0, acc.shape[2])
        if items[item]:

            def relay(start, count):
                at = pl.ds(start, count)
                for part, place, lo, hi, col in items[item]:
                    parts[part][place, at, lo:hi] = acc[0, at, col : col + hi - lo]

            copy_rows(acc.shape[1], relay)
        else:
            slot = n_parts + plain.index(item)
            land = lands[slot]

            def keep(start, count):
                land[c, pl.ds(start, count), :] = acc[0, pl.ds(start, count), :]

            copy_rows(acc.shape[1], keep)
            z_flights[slot] = [
                remote(
                    acc.at[0], land.at[c], z_send.at[slot, r], z_recv.at[slot, r], {"ctx": c ^ r}
                )
                for r in range(1, nctx)
            ]

    def spread(part):
        z_flights[part] = [
            remote(
                parts[part].at[c ^ r],
                lands[part].at[r],
                z_send.at[part, r],
                z_recv.at[part, r],
                {"ctx": c ^ r},
            )
            for r in range(1, nctx)
        ]

    def late(i):
        slot = n_slots - n_late + i
        own = pltpu.make_async_copy(lates[i * nctx], lands[slot].at[0], z_send.at[slot, 0])
        own.start()
        z_flights[slot] = [
            remote(
                lates[i * nctx + r],
                lands[slot].at[r],
                z_send.at[slot, r],
                z_recv.at[slot, r],
                {"ctx": c ^ r},
            )
            for r in range(1, nctx)
        ]
        owns[slot] = own

    def finish(slot):
        land, out = lands[slot], outs[slot]
        if slot in owns:
            owns[slot].wait()
        for copy in z_flights[slot]:
            copy.wait_recv()

        def rows(start, count):
            at = pl.ds(start, count)
            first = parts[slot][c, at, :] if slot < n_parts else land[0, at, :]
            total = first.astype(F32)
            for r in range(1, nctx):
                total = total + land[r, at, :].astype(F32)
            out[at, :] = total

        copy_rows(out.shape[0], rows)

    ways = [{"batch": b ^ bit} for bit in (1, 2, 4)] + [{"ctx": c ^ bit} for bit in bits_of("ctx")]
    swaps = []

    def swap(stage):
        if stage:
            swaps[-1].wait_recv()
            held[stage] = held[stage - 1] + came[stage - 1]
        else:
            held[0] = tile[...]
        if stage == len(ways):
            tile_out[...] = held[stage]
            return
        swaps.append(
            remote(held.at[stage], came.at[stage], m_send.at[stage], m_recv.at[stage], ways[stage])
        )

    acts = {"b": begin, "f": first, "s": second, "t": third, "p": spread, "e": finish, "m": swap, "l": late}
    for act, which in program:
        acts[act](which)
    for copy in started:
        copy.wait_send()


def reduce_all(terms, tile, lates, items, widths, program, collective_id):
    nctx, nbatch = lax.axis_size("ctx"), lax.axis_size("batch")
    plain = [i for i, pieces in enumerate(items) if not pieces]
    rows = {piece[0]: terms[i].shape[0] // nbatch for i, ps in enumerate(items) for piece in ps}
    if nbatch != 8:
        sums = [lax.psum_scatter(t, "batch", scatter_dimension=0, tiled=True) for t in terms]
        out = []
        for part, n in enumerate(widths):
            whole = jnp.zeros((rows[part], nctx, n), BF16)
            for i, pieces in enumerate(items):
                for at_part, place, lo, hi, col in pieces:
                    if at_part == part:
                        whole = whole.at[:, place, lo:hi].set(sums[i][:, col : col + hi - lo])
            out.append(lax.psum_scatter(whole, "ctx", scatter_dimension=1).astype(F32))
        out += [lax.psum(sums[i], "ctx").astype(F32) for i in plain]
        out += [ToCtx(blocks).result() for blocks in lates]
        return out + [lax.psum(tile, ("batch", "ctx"))]
    terms = [t.reshape(nbatch, -1, t.shape[1]) for t in terms]
    sizes = [t.shape[1:] for t in terms]
    shapes = [(rows[part], n) for part, n in enumerate(widths)] + [sizes[i] for i in plain]
    shapes += [blocks[0].shape for blocks in lates]
    late_blocks = [blocks[r] for blocks in lates for r in range(nctx)]
    hops = 3 + len(bits_of("ctx"))
    dma = pltpu.SemaphoreType.DMA
    return pl.pallas_call(
        functools.partial(reduce_kernel, len(widths), len(lates), tuple(items), program),
        in_specs=[pl.BlockSpec(memory_space=pl.ANY)] * len(terms)
        + [pl.BlockSpec(memory_space=pltpu.VMEM)]
        + [pl.BlockSpec(memory_space=pl.ANY)] * len(late_blocks),
        out_specs=[pl.BlockSpec(memory_space=pltpu.VMEM)] * (len(shapes) + 1),
        out_shape=[jax.ShapeDtypeStruct(shape, F32) for shape in shapes + [tile.shape]],
        scratch_shapes=[pltpu.VMEM((count,) + size, BF16) for count in (4, 4, 2, 1) for size in sizes]
        + [pltpu.VMEM((nctx,) + shape, BF16) for shape in shapes[: len(widths)]]
        + [pltpu.VMEM((nctx,) + shape, BF16) for shape in shapes]
        + [dma((len(terms), 4)), dma((len(terms), 10)), dma((len(terms), 10))]
        + [dma((len(shapes), nctx)), dma((len(shapes), nctx))]
        + [pltpu.VMEM((hops + 1,) + tile.shape, F32), pltpu.VMEM((hops,) + tile.shape, F32)]
        + [dma((hops,)), dma((hops,))],
        cost_estimate=pl.CostEstimate(flops=1, bytes_accessed=1, transcendentals=0),
        compiler_params=pltpu.CompilerParams(
            collective_id=collective_id, has_side_effects=True, vmem_limit_bytes=62 << 20
        ),
        name="reduce_gradients",
    )(*terms, tile, *late_blocks)


def pack_kernel(heights, n_rows, n_gains, *refs):
    blocks, refs = refs[: len(heights)], refs[len(heights) :]
    lines, gains, (out, few) = refs[:n_rows], refs[n_rows : n_rows + n_gains], refs[n_rows + n_gains :]
    owners, width = out.shape[0], few.shape[1]
    chan = width // owners
    out[...] = jnp.zeros_like(out)
    few[...] = jnp.zeros_like(few)
    for i, line in enumerate(lines):
        few[i : i + 1, :] = line[...]
    for i, gain in enumerate(gains):
        n = gain.shape[1] // owners
        for q in range(owners):
            few[n_rows + i : n_rows + i + 1, q * chan : q * chan + n] = gain[:, q * n : (q + 1) * n]
    at = 0
    for block in blocks + (few,):
        rows = block.shape[0]
        for q in range(owners):
            out[q, at : at + rows, :chan] = block[:, q * chan : (q + 1) * chan].astype(BF16)
        at += rows


def pack_small(blocks, lines, gains):
    nbatch = lax.axis_size("batch")
    heights = [block.shape[0] for block in blocks]
    total, chan = sum(heights) + 16, INNER // nbatch
    wide = -(-chan // (2 * LANE)) * 2 * LANE
    if nbatch != 8:
        own = D // nbatch
        gains = [
            jnp.pad(g.reshape(nbatch, own), ((0, 0), (0, chan - own))).reshape(1, INNER)
            for g in gains
        ]
        few = lines + gains
        few.append(jnp.zeros((16 - len(few), INNER), F32))
        packed = jnp.concatenate(blocks + few, axis=0).astype(BF16)
        packed = packed.reshape(total, nbatch, chan).transpose(1, 0, 2)
        packed = jnp.pad(packed, ((0, 0), (0, 0), (0, wide - chan)))
    else:
        vmem = pl.BlockSpec(memory_space=pltpu.VMEM)
        packed = pl.pallas_call(
            functools.partial(pack_kernel, tuple(heights), len(lines), len(gains)),
            in_specs=[vmem] * (len(blocks) + len(lines) + len(gains)),
            out_specs=vmem,
            out_shape=jax.ShapeDtypeStruct((nbatch, total, wide), BF16),
            scratch_shapes=[pltpu.VMEM((16, INNER), F32)],
            compiler_params=pltpu.CompilerParams(vmem_limit_bytes=40 << 20),
            name="pack_small",
        )(*blocks, *lines, *gains)
    return packed.reshape(nbatch * total, wide)


def wide(tile, width):
    return jnp.concatenate([tile] * (width // LANE), axis=1)


def fold(value):
    parts = [value[:, at : at + LANE] for at in range(0, value.shape[1], LANE)]
    return functools.reduce(jnp.add, parts)


SCAN_WIDTH = 640
SCAN_PART = 384
UNROLL = 16


def scan_parts(width):
    return [(lo, min(width, lo + SCAN_PART)) for lo in range(0, width, SCAN_PART)]


def scan_specs(seqs, span, chan):
    pos = pl.BlockSpec((1, span, SCAN_WIDTH), lambda s, e: (s, 0, e))
    coef = pl.BlockSpec((1, span, STATE, LANE), lambda s, e: (s, 0, 0, 0))
    dec = pl.BlockSpec((STATE, SCAN_WIDTH), lambda s, e: (0, e))
    state = pl.BlockSpec((1, STATE, SCAN_WIDTH), lambda s, e: (s, 0, e))
    return pos, coef, dec, state


def scan_params():
    return pltpu.CompilerParams(vmem_limit_bytes=56 << 20)


def scan_cost(seqs, span, chan, ops):
    return pl.CostEstimate(flops=ops, bytes_accessed=seqs * span * chan, transcendentals=0)


def final_kernel(step_ref, xc_ref, b_ref, dec_ref, fin_ref, drive):
    span, width = step_ref.shape[1:]
    drive[...] = step_ref[0] * xc_ref[0]
    for lo, hi in scan_parts(width):
        dec = dec_ref[:, lo:hi]

        def body(i, h):
            for j in range(UNROLL):
                t = i * UNROLL + j
                f = jnp.exp2(step_ref[0, pl.ds(t, 1), lo:hi] * dec)
                h = f * h + drive[pl.ds(t, 1), lo:hi] * wide(b_ref[0, t], hi - lo)
            return h

        fin_ref[0, :, lo:hi] = lax.fori_loop(
            0, span // UNROLL, body, jnp.zeros((STATE, hi - lo), F32)
        )


def scan_final(steps, xc, bb, dec):
    seqs, span, chan = steps.shape
    pos, coef, decs, state = scan_specs(seqs, span, chan)
    return pl.pallas_call(
        final_kernel,
        grid=(seqs, chan // SCAN_WIDTH),
        in_specs=[pos, pos, coef, decs],
        out_specs=state,
        out_shape=jax.ShapeDtypeStruct((seqs, STATE, chan), F32),
        scratch_shapes=[pltpu.VMEM((span, SCAN_WIDTH), F32)],
        compiler_params=scan_params(),
        cost_estimate=scan_cost(seqs, span, chan, 6),
        name="scan_final",
    )(steps, xc, bb, dec)


def out_kernel(step_ref, xc_ref, b_ref, c_ref, dec_ref, entry_ref, y_ref, drive):
    span, width = step_ref.shape[1:]
    drive[...] = step_ref[0] * xc_ref[0]
    for lo, hi in scan_parts(width):
        dec = dec_ref[:, lo:hi]

        def body(i, h):
            rows = []
            for j in range(UNROLL):
                t = i * UNROLL + j
                f = jnp.exp2(step_ref[0, pl.ds(t, 1), lo:hi] * dec)
                h = f * h + drive[pl.ds(t, 1), lo:hi] * wide(b_ref[0, t], hi - lo)
                rows.append(jnp.sum(h * wide(c_ref[0, t], hi - lo), axis=0, keepdims=True))
            at = pl.multiple_of(i * UNROLL, UNROLL)
            y_ref[0, pl.ds(at, UNROLL), lo:hi] = jnp.concatenate(rows, axis=0)
            return h

        lax.fori_loop(0, span // UNROLL, body, entry_ref[0, :, lo:hi])


def scan_out_of(steps, xc, bb, cc, dec, entry):
    seqs, span, chan = steps.shape
    pos, coef, decs, state = scan_specs(seqs, span, chan)
    return pl.pallas_call(
        out_kernel,
        grid=(seqs, chan // SCAN_WIDTH),
        in_specs=[pos, pos, coef, coef, decs, state],
        out_specs=pos,
        out_shape=jax.ShapeDtypeStruct((seqs, span, chan), F32),
        scratch_shapes=[pltpu.VMEM((span, SCAN_WIDTH), F32)],
        compiler_params=scan_params(),
        cost_estimate=scan_cost(seqs, span, chan, 10),
        name="scan_out",
    )(steps, xc, bb, cc, dec, entry)


def adjoint_kernel(step_ref, gy_ref, c_ref, dec_ref, out_ref):
    span, width = step_ref.shape[1:]
    for lo, hi in scan_parts(width):
        dec = dec_ref[:, lo:hi]

        def body(i, g):
            for j in range(UNROLL):
                t = span - 1 - (i * UNROLL + j)
                f = jnp.exp2(step_ref[0, pl.ds(t, 1), lo:hi] * dec)
                g = f * (g + gy_ref[0, pl.ds(t, 1), lo:hi] * wide(c_ref[0, t], hi - lo))
            return g

        out_ref[0, :, lo:hi] = lax.fori_loop(
            0, span // UNROLL, body, jnp.zeros((STATE, hi - lo), F32)
        )


def scan_adjoint(steps, gy, cc, dec):
    seqs, span, chan = steps.shape
    pos, coef, decs, state = scan_specs(seqs, span, chan)
    return pl.pallas_call(
        adjoint_kernel,
        grid=(seqs, chan // SCAN_WIDTH),
        in_specs=[pos, pos, coef, decs],
        out_specs=state,
        out_shape=jax.ShapeDtypeStruct((seqs, STATE, chan), F32),
        compiler_params=scan_params(),
        cost_estimate=scan_cost(seqs, span, chan, 6),
        name="scan_adjoint",
    )(steps, gy, cc, dec)


def back_kernel(
    step_ref, xc_ref, gy_ref, b_ref, c_ref, dec_ref, entry_ref, arrive_ref,
    dxc_ref, dstep_ref, db_ref, dc_ref, ddec_ref, drive, hs, fs,
):
    span, width = step_ref.shape[1:]
    drive[...] = step_ref[0] * xc_ref[0]

    @pl.when(pl.program_id(1) == 0)
    def _():
        db_ref[...] = jnp.zeros_like(db_ref)
        dc_ref[...] = jnp.zeros_like(dc_ref)

    for lo, hi in scan_parts(width):
        n = hi - lo
        dec = dec_ref[:, lo:hi]

        def ahead(i, h):
            for j in range(UNROLL):
                t = i * UNROLL + j
                f = jnp.exp2(step_ref[0, pl.ds(t, 1), lo:hi] * dec)
                hs[t, :, :n] = h
                fs[t, :, :n] = f
                h = f * h + drive[pl.ds(t, 1), lo:hi] * wide(b_ref[0, t], n)
            return h

        last = lax.fori_loop(0, span // UNROLL, ahead, entry_ref[0, :, lo:hi])

        def back(i, carry):
            g, h, ddec = carry
            weighted, along = [], []
            for j in range(UNROLL):
                t = span - 1 - (i * UNROLL + j)
                gy = gy_ref[0, pl.ds(t, 1), lo:hi]
                g = g + gy * wide(c_ref[0, t], n)
                dc_ref[0, t] += fold(gy * h)
                db_ref[0, t] += fold(g * drive[pl.ds(t, 1), lo:hi])
                weighted.append(jnp.sum(g * wide(b_ref[0, t], n), axis=0, keepdims=True))
                g = g * fs[t, :, :n]
                h = hs[t, :, :n]
                m = g * h
                along.append(jnp.sum(m * dec, axis=0, keepdims=True))
                ddec = ddec + m * step_ref[0, pl.ds(t, 1), lo:hi]
            at = pl.multiple_of(span - (i + 1) * UNROLL, UNROLL)
            w8 = jnp.concatenate(weighted[::-1], axis=0)
            m8 = jnp.concatenate(along[::-1], axis=0)
            dxc_ref[0, pl.ds(at, UNROLL), lo:hi] = w8 * step_ref[0, pl.ds(at, UNROLL), lo:hi]
            dstep_ref[0, pl.ds(at, UNROLL), lo:hi] = (
                m8 * LN2 + w8 * xc_ref[0, pl.ds(at, UNROLL), lo:hi]
            )
            return g, h, ddec

        start = (arrive_ref[0, :, lo:hi], last, jnp.zeros((STATE, n), F32))
        ddec_ref[0, :, lo:hi] = lax.fori_loop(0, span // UNROLL, back, start)[2]


def scan_back(steps, xc, gy, bb, cc, dec, entry, arrive):
    seqs, span, chan = steps.shape
    pos, coef, decs, state = scan_specs(seqs, span, chan)
    by_pos = jax.ShapeDtypeStruct((seqs, span, chan), F32)
    by_coef = jax.ShapeDtypeStruct((seqs, span, STATE, LANE), F32)
    return pl.pallas_call(
        back_kernel,
        grid=(seqs, chan // SCAN_WIDTH),
        in_specs=[pos, pos, pos, coef, coef, decs, state, state],
        out_specs=[pos, pos, coef, coef, state],
        out_shape=[by_pos, by_pos, by_coef, by_coef, jax.ShapeDtypeStruct((seqs, STATE, chan), F32)],
        scratch_shapes=[pltpu.VMEM((span, SCAN_WIDTH), F32)]
        + [pltpu.VMEM((span, STATE, SCAN_PART), F32)] * 2,
        compiler_params=scan_params(),
        cost_estimate=scan_cost(seqs, span, chan, 24),
        name="scan_back",
    )(steps, xc, gy, bb, cc, dec, entry, arrive)


def attend_mask(place_ref, mask):
    span = mask.shape[0]
    row = lax.broadcasted_iota(jnp.int32, (span, span), 0) + place_ref[0]
    col = lax.broadcasted_iota(jnp.int32, (span, span), 1)
    for at in range(mask.shape[1] // span):
        apart = row - (col + place_ref[at])
        allowed = (apart >= 0) & (apart < WINDOW)
        mask[:, at * span : (at + 1) * span] = jnp.where(allowed, 0.0, -1e30)


def first_step():
    return (pl.program_id(0) == 0) & (pl.program_id(1) == 0)


def scores_of(q, k):
    return lax.dot_general(q, k, (((1,), (1,)), ((), ())), preferred_element_type=F32)


QWIDE = -(-GROUP * HD // LANE) * LANE
KWIDE = -(-KV * HD // LANE) * LANE


def heads_in(k_refs, v_refs, k_all, v_all):
    span, at = v_refs[0].shape[2], 0
    for k_ref, v_ref in zip(k_refs, v_refs):
        for i in range(v_ref.shape[0]):
            v_all[at : at + span, :] = v_ref[i, 0]
            for h in range(KV):

                @pl.when(pl.program_id(1) == h)
                def _(k_ref=k_ref, i=i, at=at, h=h):
                    k_all[at : at + span, :] = k_ref[i, 0, :, h * HD : (h + 1) * HD]

            at += span


def attend_kernel(n, place_ref, q_ref, *refs):
    k_refs, v_refs, (out_ref, lse_ref, mask, k_all, v_all) = refs[:n], refs[n : 2 * n], refs[2 * n :]
    pl.when(first_step())(lambda: attend_mask(place_ref, mask))
    heads_in(k_refs, v_refs, k_all, v_all)
    for g in range(GROUP):
        s = scores_of(q_ref[0, :, g * HD : (g + 1) * HD], k_all[...]) + mask[...]
        peak = jnp.max(s, axis=-1, keepdims=True)
        e = jnp.exp(s - peak)
        total = jnp.sum(e, axis=-1, keepdims=True)
        lse_ref[0, :, g : g + 1] = peak + jnp.log(total)
        mixed = jnp.dot(e.astype(BF16), v_all[...], preferred_element_type=F32)
        out_ref[0, :, g * VHEAD : (g + 1) * VHEAD] = mixed / total


def attend_specs(span, kvs):
    q = pl.BlockSpec((1, span, QWIDE), lambda s, h: (s, 0, h))
    ks = [pl.BlockSpec((kv.shape[0], 1, span, KWIDE), lambda s, h: (0, s, 0, 0)) for kv in kvs]
    vs = [
        pl.BlockSpec((kv.shape[0], 1, span, VHEAD), lambda s, h: (0, s, 0, KWIDE // VHEAD + h))
        for kv in kvs
    ]
    out = pl.BlockSpec((1, span, GROUP * VHEAD), lambda s, h: (s, 0, h))
    lse = pl.BlockSpec((1, span, LANE), lambda s, h: (s, 0, h))
    length = span * sum(kv.shape[0] for kv in kvs)
    held = [
        pltpu.VMEM((span, length), F32),
        pltpu.VMEM((length, HD), BF16),
        pltpu.VMEM((length, VHEAD), BF16),
    ]
    return [pl.BlockSpec(memory_space=pltpu.SMEM), q] + ks + vs, q, out, lse, length, held


def attend(place_of, q, kvs):
    seqs, span, _ = q.shape
    ins, _, out, lse, length, held = attend_specs(span, kvs)
    cells = seqs * HEADS * span * length
    return pl.pallas_call(
        functools.partial(attend_kernel, len(kvs)),
        grid=(seqs, KV),
        in_specs=ins,
        out_specs=[out, lse],
        out_shape=[
            jax.ShapeDtypeStruct((seqs, span, INNER), F32),
            jax.ShapeDtypeStruct((seqs, span, KV * LANE), F32),
        ],
        scratch_shapes=held,
        compiler_params=pltpu.CompilerParams(vmem_limit_bytes=50 << 20),
        cost_estimate=pl.CostEstimate(flops=1, bytes_accessed=cells // 8, transcendentals=0),
        name="attend",
    )(place_of, q, *kvs, *kvs)


def attend_back_kernel(n, place_ref, q_ref, *refs):
    k_refs, v_refs, refs = refs[:n], refs[n : 2 * n], refs[2 * n :]
    lse_ref, o_ref, do_ref, dq_ref, dk_ref, dv_ref, mask, k_all, v_all, dk_sum, dv_sum = refs
    pl.when(first_step())(lambda: attend_mask(place_ref, mask))
    heads_in(k_refs, v_refs, k_all, v_all)
    k, v = k_all[...], v_all[...]
    for g in range(GROUP):
        q = q_ref[0, :, g * HD : (g + 1) * HD]
        do = do_ref[0, :, g * VHEAD : (g + 1) * VHEAD]
        o = o_ref[0, :, g * VHEAD : (g + 1) * VHEAD]
        s = scores_of(q, k) + mask[...]
        p = jnp.exp(s - lse_ref[0, :, g : g + 1])
        dp = scores_of(do, v)
        ds = (p * (dp - jnp.sum(do.astype(F32) * o, axis=-1, keepdims=True))).astype(BF16)
        dq = jnp.dot(ds, k, preferred_element_type=F32).astype(BF16)
        dq_ref[0, :, g * HD : (g + 1) * HD] = dq * jnp.asarray(HD**-0.5, BF16)
        dv = lax.dot_general(do, p.astype(BF16), (((0,), (0,)), ((), ())), preferred_element_type=F32)
        dk = lax.dot_general(q, ds, (((0,), (0,)), ((), ())), preferred_element_type=F32)
        if g == 0:
            dk_sum[...] = dk
            dv_sum[...] = dv
        else:
            dk_sum[...] += dk
            dv_sum[...] += dv
    if QWIDE > GROUP * HD:
        dq_ref[0, :, GROUP * HD :] = jnp.zeros((dq_ref.shape[1], QWIDE - GROUP * HD), BF16)
    dv_ref[0] = dv_sum[...].T.astype(BF16)
    dk = dk_sum[...].T.astype(BF16)

    @pl.when(pl.program_id(1) == 0)
    def _():
        dk_ref[...] = jnp.zeros_like(dk_ref)

    for h in range(KV):

        @pl.when(pl.program_id(1) == h)
        def _(h=h):
            dk_ref[0, :, h * HD : (h + 1) * HD] = dk


def attend_back(place_of, q, kvs, lse_in, o, do):
    seqs, span, _ = q.shape
    ins, qs, out, lse, length, held = attend_specs(span, kvs)
    cells = seqs * HEADS * span * length
    return pl.pallas_call(
        functools.partial(attend_back_kernel, len(kvs)),
        grid=(seqs, KV),
        in_specs=ins + [lse, out, out],
        out_specs=[
            qs,
            pl.BlockSpec((1, length, KWIDE), lambda s, h: (s, 0, 0)),
            pl.BlockSpec((1, length, VHEAD), lambda s, h: (s, 0, h)),
        ],
        out_shape=[
            jax.ShapeDtypeStruct(q.shape, BF16),
            jax.ShapeDtypeStruct((seqs, length, KWIDE), BF16),
            jax.ShapeDtypeStruct((seqs, length, KV * VHEAD), BF16),
        ],
        scratch_shapes=held + [pltpu.VMEM((HD, length), F32), pltpu.VMEM((VHEAD, length), F32)],
        compiler_params=pltpu.CompilerParams(vmem_limit_bytes=50 << 20),
        cost_estimate=pl.CostEstimate(flops=1, bytes_accessed=cells // 8, transcendentals=0),
        name="attend_back",
    )(place_of, q, *kvs, *kvs, lse_in, o, do)


def rms_scale(value):
    return lax.rsqrt(jnp.mean(value * value, axis=-1, keepdims=True) + EPS)


def norm_back(value, scale, upstream):
    return scale * upstream - value * scale**3 * jnp.mean(upstream * value, axis=-1, keepdims=True)


def silu_pair(value):
    sigma = jax.nn.sigmoid(value)
    return (value * sigma, sigma * (1.0 + value * (1.0 - sigma)))


def matmul(left, right):
    return jnp.dot(left, right, preferred_element_type=F32)


def matmul_back(left, right):
    return lax.dot_general(left, right, (((1,), (1,)), ((), ())), preferred_element_type=F32)


def outer_sum(left, right):
    return lax.dot_general(left, right, (((0,), (0,)), ((), ())), preferred_element_type=F32)


def carried(states, sums, dec, later):
    mine = lax.axis_index("ctx")
    total = jnp.zeros(states[0].shape, F32)
    for r in range(1, lax.axis_size("ctx")):
        far = mine ^ r
        passed = jnp.zeros(sums[0].shape, F32)
        for q in range(1, lax.axis_size("ctx")):
            at = mine ^ q
            between = (at > mine) & (at < far) if later else (at < mine) & (at > far)
            passed = passed + jnp.where(between, sums[q], 0.0)
        reaches = far > mine if later else far < mine
        total = total + jnp.where(reaches, jnp.exp2(dec * passed) * states[r].astype(F32), 0.0)
    return total


def per_device(
    tokens,
    teacher,
    cotangent,
    valid,
    w_query,
    w_key,
    w_value,
    w_mixer,
    w_output,
    w_gate,
    w_up,
    w_down,
    w_select,
    w_step,
    log_decay,
    conv_taps,
    conv_bias,
    step_bias,
    skip_gain,
    beta_attn,
    beta_ssm,
    gain_first,
    gain_second,
):
    seqs, span, width = tokens.shape
    nctx, nbatch = lax.axis_size("ctx"), lax.axis_size("batch")
    rows = seqs * span
    scale = 1.0 / math.sqrt(HD)
    all_tokens = rows * nbatch * nctx
    order = [0]
    for bit in bits_of("ctx")[::-1]:
        order += [r ^ bit for r in order]
    place_of = jnp.stack([(lax.axis_index("ctx") ^ r) * span for r in order]).astype(jnp.int32)

    lines = jnp.concatenate(
        [w_step, log_decay, conv_taps]
        + [v[None] for v in (conv_bias, step_bias, skip_gain, beta_attn, beta_ssm)]
        + [w_select.T],
        axis=0,
    )
    n_lines, chan = lines.shape
    gains = jnp.stack([gain_first, gain_second])
    packed = jnp.concatenate(
        [lines, jnp.pad(gains, ((0, 0), (0, chan - gains.shape[1])))], axis=0
    )
    packed = jnp.pad(packed, ((0, -packed.shape[0] % 16), (0, -chan % (2 * LANE))))
    n_q, n_k, n_v, n_mixer = [w.shape[1] for w in (w_query, w_key, w_value, w_mixer)]
    ff = nctx * w_gate.shape[1]
    every, half = range(nctx), nctx // 2
    here = jnp.full((8, LANE), jnp.sum(valid.astype(F32)))
    shards = [w_query, w_key, w_value, w_mixer, w_output, w_gate, w_up, here]
    in_kv = pieces_of(1, n_k, every) + pieces_of(2, n_v, every, KWIDE)
    items = [
        packed,
        (in_kv, KWIDE + KV * VHEAD, True),
        (pieces_of(0, n_q, every, 0, GROUP * HD, QWIDE), KV * QWIDE, True),
        (pieces_of(3, n_mixer, range(half)), INNER, True),
        (pieces_of(3, n_mixer, range(half, nctx)), INNER, True),
        (pieces_of(4, w_output.shape[1], every), D, False),
        (
            pieces_of(5, w_gate.shape[1], every) + pieces_of(6, w_up.shape[1], every, ff),
            2 * ff,
            False,
        ),
        (pieces_of(7, LANE, every), nctx * LANE, True),
    ]
    program = (
        "c1 c2 c0 c7 l0 c1 c2 l1 c0 c7 c3 l2 l7 c5 c3 f0 c6 l3 l4 f1 f2 f7 e0 c5 c4 f3 c6 e1 e2 "
        "e7 c4 l6 f4 l5 e3 e4"
    )
    acts = {"c": "columns", "l": "launch", "f": "forward", "e": "last"}
    program = tuple((acts[word[0]], int(word[1:])) for word in program.split())
    f_packed, f_kv, f_q, f_conv, f_z, row_output, row_gate_up, counts = gather_all(
        shards, items, program, 0
    )
    f_kv, f_q, f_conv, f_z = [v.reshape(-1, v.shape[2]) for v in (f_kv, f_q, f_conv, f_z)]
    count = jnp.sum(counts[:, 0, ::LANE])
    get_output, get_gate_up = Gather(row_output), Gather(row_gate_up)
    get_down = Gather(None, w_down)
    f_vectors = f_packed[:, :n_lines, :chan].transpose(1, 0, 2).reshape(n_lines, nbatch * chan)
    f_select = f_vectors[RANK + STATE + CONV + 5 :].T
    f_gains = f_packed[:, n_lines : n_lines + 2, : gains.shape[1]]
    f_gains = f_gains.transpose(1, 0, 2).reshape(2, -1)

    f_step = f_vectors[:RANK]
    f_decay = f_vectors[RANK : RANK + STATE].astype(F32)
    taps = f_vectors[RANK + STATE : RANK + STATE + CONV].astype(F32)
    f_conv_bias, f_step_bias, skip, beta_a, beta_s = [
        f_vectors[RANK + STATE + CONV + i].astype(F32) for i in range(5)
    ]
    gain_one, gain_two = f_gains[0].astype(F32), f_gains[1].astype(F32)
    decay = -jnp.exp(f_decay)
    dec = decay * LOG2E

    get_gate_up.step()
    x_flat = tokens.reshape(rows, D).astype(F32)
    scale1 = rms_scale(x_flat)
    normed1 = (x_flat * scale1 * gain_one).astype(BF16)
    conv_in = matmul(normed1, f_conv).astype(BF16).reshape(seqs, span, INNER)
    rim = shift(conv_in[:, span - (CONV - 1) :], "ctx", 1, False)
    conv_in, then1 = hold([], conv_in, normed1)
    kv_own = matmul(then1, f_kv).astype(BF16).reshape(seqs, span, KWIDE + KV * VHEAD)
    rim, kv_own, then1 = hold([], rim, kv_own, then1)
    get_kv = FromCtx(kv_own)
    get_kv.step()
    q_heads = (matmul(then1, f_q) * scale).astype(BF16).reshape(seqs, span, KV * QWIDE)
    gate_z = matmul(then1, f_z).reshape(seqs, span, INNER)
    extended = jnp.concatenate([rim, conv_in], axis=1).astype(F32)
    pre_conv = f_conv_bias + sum((taps[tap] * extended[:, tap : tap + span] for tap in range(CONV)))
    conv_out, conv_slope = silu_pair(pre_conv)

    conv_low = conv_out.reshape(rows, INNER).astype(BF16)
    projected = matmul(conv_low, f_select)
    rank_low = projected[:, :RANK].astype(BF16)
    coefs = projected[:, RANK:].reshape(seqs, span, 2, STATE, 1)
    bb = jnp.broadcast_to(coefs[:, :, 0], (seqs, span, STATE, LANE))
    cc = jnp.broadcast_to(coefs[:, :, 1], (seqs, span, STATE, LANE))
    step_pre = matmul(rank_low, f_step) + f_step_bias
    steps = jax.nn.softplus(step_pre).reshape(seqs, span, INNER)
    step_sums = jnp.sum(steps, axis=1, keepdims=True)
    steps, step_sums = hold([get_gate_up], steps, step_sums)
    get_gate_up.step()
    get_output.step()
    get_down.step()
    final = scan_final(steps, conv_out, bb, dec)
    final = hold([get_kv], final)
    get_kv.step()

    sums_high = step_sums.astype(BF16)
    sums_low = (step_sums - sums_high.astype(F32)).astype(BF16)
    get_state = FromCtx(jnp.concatenate([final.astype(BF16), sums_high, sums_low], axis=1))
    get_state.step()
    get_down.step()
    q_heads = hold([get_state, get_gate_up], q_heads)
    get_state.step()
    f_gate, f_up = hold([get_state, get_output, get_down], *get_gate_up.whole(2, ff, ff))
    get_output.step()
    get_down.step()

    states = get_state.finish()
    all_sums = {
        r: v[:, STATE : STATE + 1].astype(F32) + v[:, STATE + 1 :].astype(F32)
        for r, v in states.items()
    }
    entry = carried({r: v[:, :STATE] for r, v in states.items()}, all_sums, dec, False)
    scan_out = scan_out_of(steps, conv_out, bb, cc, dec, entry)
    scan_out = hold([get_kv, get_output, get_down], scan_out)
    get_down.step()
    get_kv.finish()
    kvs = list(get_kv.live.values())
    attn, lse = attend(place_of, q_heads, kvs)
    attn = attn.reshape(rows, INNER)
    attn = hold([get_down], attn)
    (f_output,) = get_output.whole(1, D)

    gate_act, gate_slope = silu_pair(gate_z)
    pre_gate = scan_out + skip * conv_out
    ssm_flat = (pre_gate * gate_act).reshape(rows, INNER)
    attn_scale = rms_scale(attn)
    attn_norm = attn * attn_scale
    ssm_scale = rms_scale(ssm_flat)
    ssm_norm = ssm_flat * ssm_scale
    merged = (0.5 * (attn_norm * beta_a + ssm_norm * beta_s)).astype(BF16)
    hidden1 = x_flat + matmul(merged, f_output)

    scale2 = rms_scale(hidden1)
    normed2 = (hidden1 * scale2 * gain_two).astype(BF16)
    gate_pre = matmul(normed2, f_gate)
    up_pre = matmul(normed2, f_up)
    gate_act2, gate_slope2 = silu_pair(gate_pre)
    inner_ff = (gate_act2 * up_pre).astype(BF16)
    (f_down,) = get_down.whole(3, D)
    hidden2 = hidden1 + matmul(inner_ff, f_down)
    output = hidden2.astype(BF16).reshape(seqs, span, D)
    weight_rows = valid.reshape(rows, 1).astype(F32)
    diff = hidden2 - teacher.reshape(rows, D).astype(F32)
    loss_local = jnp.sum(weight_rows * diff * diff)

    seed = cotangent.reshape(rows, D).astype(F32) + all_tokens / count * weight_rows * diff
    seed_low = seed.astype(BF16)
    put_down = Scatter(inner_ff, seed_low, w_down.shape[1])
    put_down.step()
    put_down.fresh.clear()
    d_inner = matmul_back(seed_low, f_down)
    d_gate = (d_inner * up_pre * gate_slope2).astype(BF16)
    d_up = (d_inner * gate_act2).astype(BF16)
    d_gate, d_up = hold([], d_gate, d_up)

    put_down.step()
    put_gate = Scatter(normed2, d_gate, w_gate.shape[1])
    put_gate.step()
    put_up = Scatter(normed2, d_up)
    put_up.step()
    d_norm2 = matmul_back(d_gate, f_gate) + matmul_back(d_up, f_up)
    g_gain_second = jnp.sum(d_norm2 * hidden1 * scale2, axis=0, keepdims=True)
    d_hidden1 = seed + norm_back(hidden1, scale2, d_norm2 * gain_two)
    d_hidden1 = hold([put_down, put_gate, put_up], d_hidden1)

    put_down.step()
    put_gate.step()
    d_branch = d_hidden1.astype(BF16)
    put_output = Scatter(merged, d_branch)
    put_output.step()
    d_merged = matmul_back(d_branch, f_output)
    g_beta_attn = jnp.sum(0.5 * d_merged * attn_norm, axis=0, keepdims=True)
    g_beta_ssm = jnp.sum(0.5 * d_merged * ssm_norm, axis=0, keepdims=True)
    d_attn = norm_back(attn, attn_scale, 0.5 * d_merged * beta_a).astype(BF16)
    d_ssm = norm_back(ssm_flat, ssm_scale, 0.5 * d_merged * beta_s).reshape(seqs, span, INNER)
    d_pre_gate = d_ssm * gate_act
    d_gate_z = (d_ssm * pre_gate * gate_slope).reshape(rows, INNER).astype(BF16)
    g_skip = jnp.sum(d_pre_gate * conv_out, axis=(0, 1))[None]
    adjoint = scan_adjoint(steps, d_pre_gate, cc, dec)
    d_attn, d_pre_gate, d_gate_z, adjoint = hold(
        [put_down, put_gate, put_output], d_attn, d_pre_gate, d_gate_z, adjoint
    )

    put_down.step()
    put_gate.step()
    put_up.step()
    get_adjoint = FromCtx(adjoint.astype(BF16))
    get_adjoint.step()
    dq, dk, dv = attend_back(
        place_of,
        q_heads,
        kvs,
        lse,
        attn.reshape(seqs, span, INNER),
        d_attn.reshape(seqs, span, INNER),
    )
    dq, dk, dv = hold([put_down, put_gate, put_up, get_adjoint], dq, dk, dv)
    get_adjoint.step()
    put_gate.step()
    put_up.step()
    put_output.step()
    dq = dq.reshape(rows, KV * QWIDE)
    g_q = outer_sum(normed1, dq).astype(BF16)
    g_z = outer_sum(normed1, d_gate_z).astype(BF16)
    d_norm1 = matmul_back(dq, f_q) + matmul_back(d_gate_z, f_z)
    d_norm1, g_q, g_z = hold([get_adjoint, put_up, put_output], d_norm1, g_q, g_z)

    d_kv = jnp.concatenate([dk, dv], axis=-1).reshape(seqs, nctx, span, KWIDE + KV * VHEAD)
    put_kv = ToCtx({r: d_kv[:, i] for i, r in enumerate(order)})
    put_kv.step()
    put_down.step()
    put_output.step()
    arrive = carried(get_adjoint.finish(), all_sums, dec, True)
    g_drive, g_steps, g_b, g_c, grad_decay = scan_back(
        steps, conv_out, d_pre_gate, bb, cc, dec, entry, arrive
    )
    g_drive, g_steps, g_b, g_c = hold(
        [put_down, put_gate, put_output, put_kv], g_drive, g_steps, g_b, g_c
    )

    put_kv.step()
    d_step_pre = g_steps.reshape(rows, INNER) * jax.nn.sigmoid(step_pre)
    g_step_bias = jnp.sum(d_step_pre, axis=0, keepdims=True)
    d_step_low = d_step_pre.astype(BF16)
    d_rank = matmul_back(d_step_low, f_step)
    d_projected = jnp.concatenate(
        [d_rank] + [jnp.sum(g, axis=-1).reshape(rows, STATE) for g in (g_b, g_c)], axis=1
    ).astype(BF16)
    d_conv = (
        g_drive
        + d_pre_gate * skip
        + matmul_back(d_projected, f_select).reshape(seqs, span, INNER)
    )
    d_pre_conv = hold([put_kv], d_conv * conv_slope)
    put_gate.step()
    g_conv_bias = jnp.sum(d_pre_conv, axis=(0, 1))[None]
    g_taps = [
        jnp.sum(d_pre_conv * extended[:, tap : tap + span], axis=(0, 1))[None]
        for tap in range(CONV)
    ]
    d_extended = sum(
        (
            jnp.pad(taps[tap] * d_pre_conv, ((0, 0), (tap, CONV - 1 - tap), (0, 0)))
            for tap in range(CONV)
        )
    )
    back_rim = shift(d_extended[:, : CONV - 1].astype(BF16), "ctx", -1, False)
    d_conv_in = d_extended[:, CONV - 1 :].at[:, span - (CONV - 1) :].add(back_rim.astype(F32))
    d_conv_in = hold([put_gate], d_conv_in.reshape(rows, INNER).astype(BF16))

    d_kv_own = put_kv.result().astype(BF16).reshape(rows, KWIDE + KV * VHEAD)
    d_norm1 = d_norm1 + matmul_back(d_kv_own, f_kv) + matmul_back(d_conv_in, f_conv)
    g_gain_first = jnp.sum(d_norm1 * x_flat * scale1, axis=0, keepdims=True)
    d_tokens = d_hidden1 + norm_back(x_flat, scale1, d_norm1 * gain_one)
    tokens_grad = d_tokens.astype(BF16).reshape(seqs, span, D)
    g_conv = outer_sum(normed1, d_conv_in).astype(BF16)
    g_kv = outer_sum(normed1, d_kv_own).astype(BF16)

    pad_rank, pad_sel = -RANK % 16, -(RANK + 2 * STATE) % 16
    g_step = outer_sum(jnp.pad(rank_low, ((0, 0), (0, pad_rank))), d_step_low)
    g_select = outer_sum(jnp.pad(d_projected, ((0, 0), (0, pad_sel))), conv_low)
    own_gain = D // nbatch
    at_sel = RANK + pad_rank
    at_dec = at_sel + RANK + 2 * STATE + pad_sel
    at_few = at_dec + STATE

    small = pack_small(
        [g_step, g_select, jnp.sum(grad_decay, axis=0) * decay],
        g_taps + [g_conv_bias, g_step_bias, g_skip, g_beta_attn, g_beta_ssm],
        [g_gain_first, g_gain_second],
    )
    lates = [put_output.blocks(w_output.shape[1]), put_up.blocks(w_up.shape[1])]
    terms = [g_conv, g_z, g_q, g_kv, small]
    items = [items[3][0], items[4][0], items[2][0], items[1][0], ()]
    program = "b4 b3 l0 l1 b2 b1 b0 m0 f4 f3 m1 f2 f1 s4 m2 f0 s3 t4 m3 s2 t3 p1 p2 m4 t2 p0 s1 e4 m5 t1 s0 "
    program += "t0 p3 e5 e6 e1 e2 e0 e3"
    program = tuple((word[0], int(word[1:])) for word in program.split())
    (r_down,), (r_gate,) = put_down.result(), put_gate.result()
    r_query, r_key, r_value, r_mixer, small, r_output, r_up, loss_sum = reduce_all(
        terms,
        jnp.full((8, LANE), loss_local),
        lates,
        items,
        (n_q, n_k, n_v, n_mixer),
        program,
        4,
    )
    loss_sum = loss_sum[0, 0]
    small = small[:, :chan]
    return (
        output,
        loss_sum / (count * D),
        tokens_grad,
        r_query,
        r_key,
        r_value,
        r_mixer,
        r_output,
        r_gate,
        r_up,
        r_down,
        small[at_sel : at_sel + RANK + 2 * STATE].T,
        small[:RANK],
        small[at_dec:at_few],
        small[at_few : at_few + CONV],
        *[small[at_few + CONV + i] for i in range(5)],
        *[small[at_few + CONV + 5 + i, :own_gain] for i in range(2)],
    )


def solution(mesh):
    by_pos = P("batch", "ctx", None)
    by_both = P("batch", "ctx")
    by_row, by_col, by_one = P("batch", None), P(None, "batch"), P("batch")
    weights = (by_both,) * 8 + (by_row,) + (by_col,) * 3 + (by_one,) * 7
    return jax.shard_map(
        per_device,
        mesh=mesh,
        in_specs=(by_pos, by_pos, by_pos, by_both) + weights,
        out_specs=(by_pos, P(), by_pos) + weights,
        check_vma=False,
    )
```

```python
import functools
import math

import jax
import jax.numpy as jnp
from jax import lax
from jax.experimental import pallas as pl
from jax.experimental.pallas import tpu as pltpu
from jax.sharding import PartitionSpec as P

D = 1600
HEADS = 25
KV = 5
HD = 64
INNER = 3200
STATE = 16
CONV = 4
RANK = 100
WINDOW = 1024
GROUP = HEADS // KV
VHEAD = INNER // HEADS
LANE = 128

EPS = 1e-05
F32 = jnp.float32
BF16 = jnp.bfloat16
LOG2E = math.log2(math.e)
LN2 = math.log(2.0)
MESH = pl.DeviceIdType.MESH


def permute_bit(value, axis, bit):
    count = lax.axis_size(axis)
    return lax.ppermute(value, axis, [(i, i ^ bit) for i in range(count)])


def shift(value, axis, steps, wrap):
    count = lax.axis_size(axis)
    pairs = [(i, (i + steps) % count) for i in range(count) if wrap or 0 <= i + steps < count]
    return lax.ppermute(value, axis, pairs)


def bits_of(axis):
    count = lax.axis_size(axis)
    return [1 << k for k in range(count.bit_length() - 1)]


def from_ctx(blocks):
    count, mine = lax.axis_size("ctx"), lax.axis_index("ctx")
    out = []
    for at in range(count):
        block = blocks[0]
        for r in range(1, count):
            block = jnp.where(mine ^ r == at, blocks[r], block)
        out.append(block)
    return out


def gather_columns(shard):
    return lax.all_gather(shard, "ctx", axis=0)


def gather_rows(block):
    return lax.all_gather(block, "batch", axis=0, tiled=True)


def copy_rows(rows, copy):
    whole = rows // 16 * 16

    def body(i, _):
        copy(pl.multiple_of(i * 16, 16), 16)
        return 0

    lax.fori_loop(0, whole // 16, body, 0)
    if whole < rows:
        copy(whole, rows - whole)


def pieces_of(part, n, places, at=0, group=0, wide=0):
    out = []
    for i, place in enumerate(places):
        lo = 0
        while lo < n:
            col = i * n + lo
            hi, target = n, at + col
            if group:
                hi = min(n, (col // group + 1) * group - i * n)
                target = at + col // group * wide + col % group
            out.append((part, place, lo, hi, target))
            lo = hi
    return tuple(out)


def gather_kernel(n_parts, items, program, *refs):
    plain = [i for i, (pieces, _) in enumerate(items) if not pieces]
    shards, refs = refs[:n_parts], refs[n_parts:]
    direct, refs = dict(zip(plain, refs)), refs[len(plain) :]
    wholes, refs = refs[: len(items)], refs[len(items) :]
    parts, refs = refs[:n_parts], refs[n_parts:]
    blocks, sems = refs[: len(items)], refs[len(items) :]
    z_own, z_send, z_recv, b_send, b_recv, b_own = sems
    b, c = lax.axis_index("batch"), lax.axis_index("ctx")
    bits = bits_of("ctx")[::-1]

    barrier = pltpu.get_barrier_semaphore()
    peers = [{"ctx": c ^ bit} for bit in bits] + [{"batch": b ^ bit} for bit in (1, 2, 4)]
    for device in peers:
        pl.semaphore_signal(barrier, inc=1, device_id=device, device_id_type=MESH)
    pl.semaphore_wait(barrier, len(peers))

    started, stores = [], []

    def remote(source, target, send_sem, recv_sem, device):
        copy = pltpu.make_async_remote_copy(
            src_ref=source,
            dst_ref=target,
            send_sem=send_sem,
            recv_sem=recv_sem,
            device_id=device,
            device_id_type=MESH,
        )
        copy.start()
        started.append(copy)
        return copy

    come, reached = {}, {}

    def columns(part):
        shard, slot = shards[part], parts[part]
        stage = reached.get(part, 0)
        bit = bits[stage]
        if stage == 0:
            own = pltpu.make_async_copy(shard, slot.at[c], z_own.at[part])
            own.start()
            come[part] = {0: own.wait}
        for r in sorted(come[part]):
            if r:
                come[part][r]()
                come[part][r] = lambda: None
            copy = remote(
                slot.at[c ^ r] if r else shard,
                slot.at[c ^ r],
                z_send.at[part, r ^ bit],
                z_recv.at[part, r ^ bit],
                {"ctx": c ^ bit},
            )
            come[part][r ^ bit] = copy.wait_recv
        reached[part] = stage + 1

    flights = {}

    def send(item, slot, source, target, bit):
        return remote(
            source, target, b_send.at[item, slot], b_recv.at[item, slot], {"batch": b ^ bit}
        )

    def keep(item, slot, r):
        there = wholes[item].at[b ^ r]
        store = pltpu.make_async_copy(blocks[item].at[slot], there, b_own.at[item, slot])
        store.start()
        stores.append(store)
        return send(item, 4 + slot, blocks[item].at[slot], there, 1)

    def launch(item):
        pieces, rows = items[item]
        block = blocks[item]
        if pieces:
            for part in sorted({piece[0] for piece in pieces}):
                for r in come[part]:
                    come[part][r]()
                    come[part][r] = lambda: None
            ends = sorted((at, at + hi - lo) for _, _, lo, hi, at in pieces)
            ends.append((block.shape[2], 0))
            gaps = [(end, ends[i + 1][0]) for i, (_, end) in enumerate(ends[:-1])]

            def relay(start, count):
                for part, place, lo, hi, at in pieces:
                    block[0, pl.ds(start, count), at : at + hi - lo] = parts[part][
                        place, pl.ds(start, count), lo:hi
                    ]
                for lo, hi in gaps:
                    if lo < hi:
                        block[0, pl.ds(start, count), lo:hi] = jnp.zeros((count, hi - lo), block.dtype)

            copy_rows(block.shape[1], relay)
        else:
            own = pltpu.make_async_copy(direct[item], block.at[0], b_own.at[item, 4])
            own.start()
            own.wait()
        if rows:
            flights[item] = [
                send(item, 1, block.at[0], block.at[1], 2),
                send(item, 2, block.at[0], block.at[2], 4),
            ]
            flights[item].append(keep(item, 0, 0))
        else:
            store = pltpu.make_async_copy(block.at[0], wholes[item], b_own.at[item, 0])
            store.start()
            stores.append(store)

    def forward(item):
        block, flight = blocks[item], flights[item]
        n = block.shape[2]
        half = n // 2 // LANE * LANE
        flight[0].wait_recv()
        left, right = (slice(None), slice(0, half)), (slice(None), slice(half, n))
        flight.append(send(item, 3, block.at[1, *left], block.at[3, *left], 4))
        flight.append(keep(item, 1, 2))
        flight[1].wait_recv()
        flight.append(send(item, 0, block.at[2, *right], block.at[3, *right], 2))
        flight.append(keep(item, 2, 4))

    def last(item):
        flight = flights[item]
        flight[3].wait_recv()
        flight[5].wait_recv()
        flight.append(keep(item, 3, 6))

    acts = {"columns": columns, "launch": launch, "forward": forward, "last": last}
    for act, which in program:
        acts[act](which)
    for flight in flights.values():
        for key in (2, 4, 6, 7):
            flight[key].wait_recv()
    for copy in stores:
        copy.wait()
    for copy in started:
        copy.wait_send()


def gather_all(shards, items, program, collective_id):
    count, nbatch = lax.axis_size("ctx"), lax.axis_size("batch")
    if nbatch != 8:
        found, out = [gather_columns(shard) for shard in shards], []
        for item in items:
            if not isinstance(item, tuple):
                out.append(gather_rows(item).reshape(nbatch, *item.shape))
                continue
            pieces, n, rows = item
            block = jnp.zeros((found[pieces[0][0]].shape[1], n), shards[pieces[0][0]].dtype)
            for part, place, lo, hi, at in pieces:
                block = block.at[:, at : at + hi - lo].set(found[part][place, :, lo:hi])
            out.append(gather_rows(block).reshape(nbatch, *block.shape) if rows else block)
        return out
    flat, kinds, shapes, blocks = list(shards), [], [], []
    for item in items:
        if isinstance(item, tuple):
            pieces, n, rows = item
            k, dtype = shards[pieces[0][0]].shape[0], shards[pieces[0][0]].dtype
        else:
            (k, n), pieces, rows, dtype = item.shape, (), True, item.dtype
            flat.append(item)
        kinds.append((pieces, rows))
        blocks.append(pltpu.VMEM((4 if rows else 1, k, n), dtype))
        shapes.append(jax.ShapeDtypeStruct((nbatch, k, n) if rows else (k, n), dtype))
    dma = pltpu.SemaphoreType.DMA
    hbm = pl.BlockSpec(memory_space=pl.ANY)
    return pl.pallas_call(
        functools.partial(gather_kernel, len(shards), tuple(kinds), program),
        in_specs=[hbm] * len(flat),
        out_specs=[hbm] * len(shapes),
        out_shape=shapes,
        scratch_shapes=[pltpu.VMEM((count,) + w.shape, w.dtype) for w in shards]
        + blocks
        + [dma((len(shards),)), dma((len(shards), count)), dma((len(shards), count))]
        + [dma((len(shapes), 8)), dma((len(shapes), 8)), dma((len(shapes), 5))],
        compiler_params=pltpu.CompilerParams(
            collective_id=collective_id, has_side_effects=True, vmem_limit_bytes=56 << 20
        ),
        name="gather_weights",
    )(*flat)


class Staged:
    def __init__(self, live):
        self.live = live
        self.fresh = list(live)
        self.stage = 0

    def fly(self, key, value):
        self.live[key] = value
        self.fresh.append(key)


def hold(staged, *values):
    flying = [[item.live[key] for key in item.fresh] for item in staged]
    flying, values = lax.optimization_barrier((flying, values))
    for item, arrived in zip(staged, flying):
        item.live.update(zip(item.fresh, arrived))
        item.fresh = []
    return values[0] if len(values) == 1 else values


class FromCtx(Staged):
    def __init__(self, value):
        super().__init__({0: value[None]})
        self.orders = [[0]]

    def step(self):
        bits = bits_of("ctx")[::-1]
        if self.stage < len(bits):
            bit = bits[self.stage]
            sent = list(self.live.values())
            sent = jnp.concatenate(sent, axis=0) if len(sent) > 1 else sent[0]
            self.orders.append([r ^ bit for order in self.orders for r in order])
            self.fly(self.stage + 1, permute_bit(sent, "ctx", bit))
        self.stage += 1

    def finish(self):
        while self.stage < len(bits_of("ctx")):
            self.step()
        return {
            r: self.live[i][j] for i, order in enumerate(self.orders) for j, r in enumerate(order)
        }


class ToCtx(Staged):
    def __init__(self, blocks):
        super().__init__({(r, 0): block for r, block in blocks.items()})

    def total(self, r):
        terms = [v.astype(F32) for key, v in self.live.items() if key[0] == r]
        return functools.reduce(jnp.add, terms)

    def step(self):
        bits = bits_of("ctx")
        if self.stage < len(bits):
            bit = bits[self.stage]
            which = sorted({key[0] for key in self.live if key[0] & bit})
            sent = jnp.stack([self.total(r).astype(BF16) for r in which])
            got = permute_bit(sent, "ctx", bit)
            self.live = {key: v for key, v in self.live.items() if not key[0] & bit}
            self.fresh = [key for key in self.fresh if key in self.live]
            for i, r in enumerate(which):
                self.fly((r ^ bit, self.stage + 1), got[i])
        self.stage += 1

    def result(self):
        while self.stage < len(bits_of("ctx")):
            self.step()
        return self.total(0)


def assemble_kernel(names, cuts, *refs):
    parts, wholes = refs[: len(names)], refs[len(names) : len(names) + len(cuts)]
    held, sems_in, sems_out, send_sems, recv_sems = refs[-5:]
    b = lax.axis_index("batch")
    other = {"batch": b ^ 1}
    ins = {}
    for i, (part, (r, lo)) in enumerate(zip(parts, names)):
        n = part.shape[1]
        slot = held.at[r // 2] if n == held.shape[2] else held.at[r // 2, :, lo : lo + n]
        ins.setdefault(r, []).append(pltpu.make_async_copy(part, slot, sems_in.at[i]))
        ins[r][-1].start()
    barrier = pltpu.get_barrier_semaphore()
    pl.semaphore_signal(barrier, inc=1, device_id=other, device_id_type=MESH)
    pl.semaphore_wait(barrier, 1)
    waits = []
    for r, copies in ins.items():
        for copy in copies:
            copy.wait()
        for i, (whole, (lo, hi)) in enumerate(zip(wholes, cuts)):
            slot = held.at[r // 2] if len(cuts) == 1 else held.at[r // 2, :, lo:hi]
            goes = pltpu.make_async_remote_copy(
                src_ref=slot,
                dst_ref=whole.at[b ^ r],
                send_sem=send_sems.at[i, r // 2],
                recv_sem=recv_sems.at[i, r // 2],
                device_id=other,
                device_id_type=MESH,
            )
            stays = pltpu.make_async_copy(slot, whole.at[b ^ r], sems_out.at[i, r // 2])
            goes.start()
            stays.start()
            waits += [goes, stays]
    for copy in waits:
        copy.wait()


def assemble(parts, widths, collective_id):
    names = tuple(parts)
    k, n = parts[(0, 0)].shape
    cuts = tuple((sum(widths[:i]), sum(widths[: i + 1])) for i in range(len(widths)))
    hbm = pl.BlockSpec(memory_space=pl.ANY)
    dma = pltpu.SemaphoreType.DMA
    wholes = pl.pallas_call(
        functools.partial(assemble_kernel, names, cuts),
        in_specs=[hbm] * len(names),
        out_specs=[hbm] * len(cuts),
        out_shape=[jax.ShapeDtypeStruct((8, k, width), BF16) for width in widths],
        scratch_shapes=[pltpu.VMEM((4, k, n), BF16), dma((len(names),)), dma((len(cuts), 4))]
        + [dma((len(cuts), 4)), dma((len(cuts), 4))],
        compiler_params=pltpu.CompilerParams(
            collective_id=collective_id, has_side_effects=True, vmem_limit_bytes=40 << 20
        ),
        cost_estimate=pl.CostEstimate(flops=0, bytes_accessed=32 * k * n, transcendentals=0),
        name="assemble",
    )(*[parts[name] for name in names])
    return [whole.reshape(8 * k, -1) for whole in wholes]


class Gather(Staged):
    def __init__(self, block, shard=None):
        self.block, self.shard = block, shard
        self.columns = None if shard is None else FromCtx(shard)
        super().__init__({(0, 0): block} if shard is None else self.columns.live)

    def step(self):
        if lax.axis_size("batch") != 8:
            return
        if self.columns:
            if self.columns.stage < len(bits_of("ctx")):
                self.columns.live, self.columns.fresh = self.live, []
                self.columns.step()
                self.live, self.fresh = self.columns.live, self.columns.fresh
                return
            self.columns.live = self.live
            self.live = {(0, 0): jnp.concatenate(from_ctx(self.columns.finish()), axis=1)}
            self.columns, self.fresh = None, []
        live, block = self.live, self.live[(0, 0)]
        if self.stage == 0:
            for bit in (2, 4):
                self.fly((bit, 0), permute_bit(block, "batch", bit))
        elif self.stage == 1:
            n = block.shape[1]
            half = n // 2 // LANE * LANE
            self.fly((6, 0), permute_bit(live[(2, 0)][:, :half], "batch", 4))
            self.fly((6, half), permute_bit(live[(4, 0)][:, half:], "batch", 2))
        self.stage += 1

    def whole(self, collective_id, *widths):
        if lax.axis_size("batch") == 8:
            return assemble(self.live, widths, collective_id)
        block = self.block
        if self.shard is not None:
            block = jnp.concatenate(list(gather_columns(self.shard)), axis=1)
        whole = gather_rows(block)
        return jnp.split(whole, [sum(widths[:i]) for i in range(1, len(widths))], axis=1)


def ctx_terms(own, columns):
    nctx, mine = lax.axis_size("ctx"), lax.axis_index("ctx")
    at, cuts = 0, []
    for n in columns:
        cuts.append([own[:, at + c * n : at + (c + 1) * n] for c in range(nctx)])
        at += nctx * n
    parts = [jnp.concatenate(cut, axis=1) if len(cut) > 1 else cut[0] for cut in zip(*cuts)]
    blocks = {}
    for r in range(nctx):
        blocks[r] = parts[0]
        for c in range(1, nctx):
            blocks[r] = jnp.where(mine ^ r == c, parts[c], blocks[r])
    return ToCtx(blocks)


class Scatter(Staged):
    def __init__(self, left, right, *columns, trim=None):
        count = lax.axis_size("batch")
        super().__init__({})
        self.columns, self.trim = columns, trim
        self.tall, self.right = left.T.reshape(count, -1, left.shape[0]), right
        self.arrived = {}
        self.spread = None

    def rows_of(self, which):
        mine = lax.axis_index("batch")
        return jnp.concatenate(
            [lax.dynamic_index_in_dim(self.tall, mine ^ r, 0, keepdims=False) for r in which], axis=0
        )

    def part(self, which, lo, hi):
        k = self.tall.shape[1]
        own = matmul(self.rows_of(which), self.right[:, lo:hi])
        for key, order in self.arrived.items():
            if key[0] in (lo, -1):
                off = lo if key[0] == -1 else 0
                pieces = [
                    self.live[key][
                        order.index(r) * k : (order.index(r) + 1) * k, off : off + hi - lo
                    ]
                    for r in which
                ]
                own = own + jnp.concatenate(pieces, axis=0).astype(F32)
        return own

    def step(self):
        stage = self.stage
        self.stage += 1
        count, bits = lax.axis_size("batch"), bits_of("batch")
        n = self.right.shape[1]
        cut = n // 2 // LANE * LANE
        halves = ((0, cut, bits[1:]), (cut, n, bits[:0:-1]))
        if self.stage > len(bits) + 1 and not self.spread:
            return
        if count != 8 and stage <= len(bits):
            self.stage = len(bits) + 1
            whole = matmul(self.tall.reshape(-1, self.tall.shape[2]), self.right).astype(BF16)
            own = lax.psum_scatter(whole, "batch", scatter_dimension=0, tiled=True)
            self.live = {"own": self.trim(own) if self.trim else own}
            if self.columns:
                self.to_ctx(self.live["own"])
        elif stage == 0:
            odd = [r for r in range(count) if r & 1]
            sent = matmul(self.rows_of(odd), self.right).astype(BF16)
            self.fly((-1, 0), permute_bit(sent, "batch", 1))
            self.arrived[(-1, 0)] = [r ^ 1 for r in odd]
        elif stage < len(bits):
            fresh = {}
            for lo, hi, order in halves:
                gone, bit = sum(order[: stage - 1]), order[stage - 1]
                which = [r for r in range(count) if not r & (gone | 1) and r & bit]
                fresh[(lo, stage)] = permute_bit(self.part(which, lo, hi).astype(BF16), "batch", bit)
                self.arrived[(lo, stage)] = [r ^ bit for r in which]
            for key, value in fresh.items():
                self.fly(key, value)
        elif stage == len(bits):
            own = jnp.concatenate([self.part([0], lo, hi) for lo, hi, _ in halves], axis=1)
            own = own.astype(BF16)
            self.live, self.fresh = {"own": self.trim(own) if self.trim else own}, []
            if self.columns:
                self.to_ctx(self.live["own"])
                self.step()
        elif self.spread:
            self.spread.live, self.spread.fresh = self.live, []
            self.spread.step()
            self.live, self.fresh = self.spread.live, self.spread.fresh

    def to_ctx(self, own):
        self.spread = ctx_terms(own, self.columns)
        self.live, self.fresh = self.spread.live, []

    def blocks(self, *columns):
        while self.stage <= len(bits_of("batch")):
            self.step()
        terms = ctx_terms(self.live["own"], columns).live
        return {key[0]: block for key, block in terms.items()}

    def result(self):
        while self.stage <= len(bits_of("batch")) or not self.spread:
            self.step()
        self.spread.live = self.live
        total, out = self.spread.result(), []
        for n in self.columns:
            at = sum(v.shape[1] for v in out)
            out.append(total[:, at : at + n])
        return out


def reduce_kernel(n_parts, n_late, items, program, *refs):
    n = len(items)
    plain = [i for i, pieces in enumerate(items) if not pieces]
    nctx = lax.axis_size("ctx")
    n_slots = n_parts + len(plain) + n_late
    terms, tile, refs = refs[:n], refs[n], refs[n + 1 :]
    lates, refs = refs[: n_late * nctx], refs[n_late * nctx :]
    outs, refs = refs[:n_slots], refs[n_slots:]
    tile_out, refs = refs[0], refs[1:]
    accs, refs = refs[:n], refs[n:]
    firsts, refs = refs[:n], refs[n:]
    seconds, refs = refs[:n], refs[n:]
    thirds, refs = refs[:n], refs[n:]
    parts, refs = refs[:n_parts], refs[n_parts:]
    lands, refs = refs[:n_slots], refs[n_slots:]
    load, b_send, b_recv, z_send, z_recv, held, came, m_send, m_recv = refs
    b, c = lax.axis_index("batch"), lax.axis_index("ctx")

    barrier = pltpu.get_barrier_semaphore()
    peers = [{"ctx": c ^ r} for r in range(1, nctx)] + [{"batch": b ^ bit} for bit in (1, 2, 4)]
    for device in peers:
        pl.semaphore_signal(barrier, inc=1, device_id=device, device_id_type=MESH)
    pl.semaphore_wait(barrier, len(peers))

    started = []

    def remote(source, target, send_sem, recv_sem, device):
        copy = pltpu.make_async_remote_copy(
            src_ref=source,
            dst_ref=target,
            send_sem=send_sem,
            recv_sem=recv_sem,
            device_id=device,
            device_id_type=MESH,
        )
        copy.start()
        started.append(copy)
        return copy

    def send(item, slot, source, target, bit):
        return remote(
            source, target, b_send.at[item, slot], b_recv.at[item, slot], {"batch": b ^ bit}
        )

    def halves(item):
        width = accs[item].shape[2]
        cut = width // 2 // LANE * LANE
        return (0, cut), (cut, width)

    def add(to, j, other, i, lo, hi):
        def rows(start, count):
            at = pl.ds(start, count)
            total = to[j, at, lo:hi].astype(F32) + other[i, at, lo:hi].astype(F32)
            to[j, at, lo:hi] = total.astype(BF16)

        copy_rows(to.shape[1], rows)

    flights, z_flights, owns = {}, {}, {}

    def begin(item):
        copies = []
        for j in range(4):
            own = pltpu.make_async_copy(terms[item].at[b ^ (2 * j)], accs[item].at[j], load.at[item, j])
            own.start()
            copies.append(own)
        for j in range(4):
            copies.append(send(item, j, terms[item].at[b ^ (2 * j + 1)], firsts[item].at[j], 1))
        flights[item] = copies

    def sub(ref, j, span):
        return ref.at[j, :, span[0] : span[1]]

    def first(item):
        acc, flight = accs[item], flights[item]
        left, right = halves(item)
        for j in (3, 1, 2, 0):
            flight[j].wait()
            flight[4 + j].wait_recv()
            add(acc, j, firsts[item], j, 0, acc.shape[2])
            if j == 1:
                after = [
                    send(item, 4, sub(acc, 1, left), sub(seconds[item], 0, left), 2),
                    send(item, 5, sub(acc, 3, left), sub(seconds[item], 1, left), 2),
                ]
            if j == 2:
                after += [
                    send(item, 6, sub(acc, 2, right), sub(seconds[item], 0, right), 4),
                    send(item, 7, sub(acc, 3, right), sub(seconds[item], 1, right), 4),
                ]
        flights[item] = after

    def second(item):
        acc, flight = accs[item], flights[item]
        left, right = halves(item)
        flight[1].wait_recv()
        add(acc, 2, seconds[item], 1, *left)
        after = [send(item, 8, sub(acc, 2, left), sub(thirds[item], 0, left), 4)]
        flight[3].wait_recv()
        add(acc, 1, seconds[item], 1, *right)
        after.append(send(item, 9, sub(acc, 1, right), sub(thirds[item], 0, right), 2))
        flight[0].wait_recv()
        flight[2].wait_recv()
        add(acc, 0, seconds[item], 0, 0, acc.shape[2])
        flights[item] = after

    def third(item):
        acc = accs[item]
        for copy in flights[item]:
            copy.wait_recv()
        add(acc, 0, thirds[item], 0, 0, acc.shape[2])
        if items[item]:

            def relay(start, count):
                at = pl.ds(start, count)
                for part, place, lo, hi, col in items[item]:
                    parts[part][place, at, lo:hi] = acc[0, at, col : col + hi - lo]

            copy_rows(acc.shape[1], relay)
        else:
            slot = n_parts + plain.index(item)
            land = lands[slot]

            def keep(start, count):
                land[c, pl.ds(start, count), :] = acc[0, pl.ds(start, count), :]

            copy_rows(acc.shape[1], keep)
            z_flights[slot] = [
                remote(
                    acc.at[0], land.at[c], z_send.at[slot, r], z_recv.at[slot, r], {"ctx": c ^ r}
                )
                for r in range(1, nctx)
            ]

    def spread(part):
        z_flights[part] = [
            remote(
                parts[part].at[c ^ r],
                lands[part].at[r],
                z_send.at[part, r],
                z_recv.at[part, r],
                {"ctx": c ^ r},
            )
            for r in range(1, nctx)
        ]

    def late(i):
        slot = n_slots - n_late + i
        own = pltpu.make_async_copy(lates[i * nctx], lands[slot].at[0], z_send.at[slot, 0])
        own.start()
        z_flights[slot] = [
            remote(
                lates[i * nctx + r],
                lands[slot].at[r],
                z_send.at[slot, r],
                z_recv.at[slot, r],
                {"ctx": c ^ r},
            )
            for r in range(1, nctx)
        ]
        owns[slot] = own

    def finish(slot):
        land, out = lands[slot], outs[slot]
        if slot in owns:
            owns[slot].wait()
        for copy in z_flights[slot]:
            copy.wait_recv()

        def rows(start, count):
            at = pl.ds(start, count)
            first = parts[slot][c, at, :] if slot < n_parts else land[0, at, :]
            total = first.astype(F32)
            for r in range(1, nctx):
                total = total + land[r, at, :].astype(F32)
            out[at, :] = total

        copy_rows(out.shape[0], rows)

    ways = [{"batch": b ^ bit} for bit in (1, 2, 4)] + [{"ctx": c ^ bit} for bit in bits_of("ctx")]
    swaps = []

    def swap(stage):
        if stage:
            swaps[-1].wait_recv()
            held[stage] = held[stage - 1] + came[stage - 1]
        else:
            held[0] = tile[...]
        if stage == len(ways):
            tile_out[...] = held[stage]
            return
        swaps.append(
            remote(held.at[stage], came.at[stage], m_send.at[stage], m_recv.at[stage], ways[stage])
        )

    acts = {"b": begin, "f": first, "s": second, "t": third, "p": spread, "e": finish, "m": swap, "l": late}
    for act, which in program:
        acts[act](which)
    for copy in started:
        copy.wait_send()


def reduce_all(terms, tile, lates, items, widths, program, collective_id):
    nctx, nbatch = lax.axis_size("ctx"), lax.axis_size("batch")
    plain = [i for i, pieces in enumerate(items) if not pieces]
    rows = {piece[0]: terms[i].shape[0] // nbatch for i, ps in enumerate(items) for piece in ps}
    if nbatch != 8:
        sums = [lax.psum_scatter(t, "batch", scatter_dimension=0, tiled=True) for t in terms]
        out = []
        for part, n in enumerate(widths):
            whole = jnp.zeros((rows[part], nctx, n), BF16)
            for i, pieces in enumerate(items):
                for at_part, place, lo, hi, col in pieces:
                    if at_part == part:
                        whole = whole.at[:, place, lo:hi].set(sums[i][:, col : col + hi - lo])
            out.append(lax.psum_scatter(whole, "ctx", scatter_dimension=1).astype(F32))
        out += [lax.psum(sums[i], "ctx").astype(F32) for i in plain]
        out += [ToCtx(blocks).result() for blocks in lates]
        return out + [lax.psum(tile, ("batch", "ctx"))]
    terms = [t.reshape(nbatch, -1, t.shape[1]) for t in terms]
    sizes = [t.shape[1:] for t in terms]
    shapes = [(rows[part], n) for part, n in enumerate(widths)] + [sizes[i] for i in plain]
    shapes += [blocks[0].shape for blocks in lates]
    late_blocks = [blocks[r] for blocks in lates for r in range(nctx)]
    hops = 3 + len(bits_of("ctx"))
    dma = pltpu.SemaphoreType.DMA
    return pl.pallas_call(
        functools.partial(reduce_kernel, len(widths), len(lates), tuple(items), program),
        in_specs=[pl.BlockSpec(memory_space=pl.ANY)] * len(terms)
        + [pl.BlockSpec(memory_space=pltpu.VMEM)]
        + [pl.BlockSpec(memory_space=pl.ANY)] * len(late_blocks),
        out_specs=[pl.BlockSpec(memory_space=pltpu.VMEM)] * (len(shapes) + 1),
        out_shape=[jax.ShapeDtypeStruct(shape, F32) for shape in shapes + [tile.shape]],
        scratch_shapes=[pltpu.VMEM((count,) + size, BF16) for count in (4, 4, 2, 1) for size in sizes]
        + [pltpu.VMEM((nctx,) + shape, BF16) for shape in shapes[: len(widths)]]
        + [pltpu.VMEM((nctx,) + shape, BF16) for shape in shapes]
        + [dma((len(terms), 4)), dma((len(terms), 10)), dma((len(terms), 10))]
        + [dma((len(shapes), nctx)), dma((len(shapes), nctx))]
        + [pltpu.VMEM((hops + 1,) + tile.shape, F32), pltpu.VMEM((hops,) + tile.shape, F32)]
        + [dma((hops,)), dma((hops,))],
        cost_estimate=pl.CostEstimate(flops=1, bytes_accessed=1, transcendentals=0),
        compiler_params=pltpu.CompilerParams(
            collective_id=collective_id, has_side_effects=True, vmem_limit_bytes=62 << 20
        ),
        name="reduce_gradients",
    )(*terms, tile, *late_blocks)


def pack_kernel(heights, n_rows, n_gains, *refs):
    blocks, refs = refs[: len(heights)], refs[len(heights) :]
    lines, gains, (out, few) = refs[:n_rows], refs[n_rows : n_rows + n_gains], refs[n_rows + n_gains :]
    owners, width = out.shape[0], few.shape[1]
    chan = width // owners
    out[...] = jnp.zeros_like(out)
    few[...] = jnp.zeros_like(few)
    for i, line in enumerate(lines):
        few[i : i + 1, :] = line[...]
    for i, gain in enumerate(gains):
        n = gain.shape[1] // owners
        for q in range(owners):
            few[n_rows + i : n_rows + i + 1, q * chan : q * chan + n] = gain[:, q * n : (q + 1) * n]
    at = 0
    for block in blocks + (few,):
        rows = block.shape[0]
        for q in range(owners):
            out[q, at : at + rows, :chan] = block[:, q * chan : (q + 1) * chan].astype(BF16)
        at += rows


def pack_small(blocks, lines, gains):
    nbatch = lax.axis_size("batch")
    heights = [block.shape[0] for block in blocks]
    total, chan = sum(heights) + 16, INNER // nbatch
    wide = -(-chan // (2 * LANE)) * 2 * LANE
    if nbatch != 8:
        own = D // nbatch
        gains = [
            jnp.pad(g.reshape(nbatch, own), ((0, 0), (0, chan - own))).reshape(1, INNER)
            for g in gains
        ]
        few = lines + gains
        few.append(jnp.zeros((16 - len(few), INNER), F32))
        packed = jnp.concatenate(blocks + few, axis=0).astype(BF16)
        packed = packed.reshape(total, nbatch, chan).transpose(1, 0, 2)
        packed = jnp.pad(packed, ((0, 0), (0, 0), (0, wide - chan)))
    else:
        vmem = pl.BlockSpec(memory_space=pltpu.VMEM)
        packed = pl.pallas_call(
            functools.partial(pack_kernel, tuple(heights), len(lines), len(gains)),
            in_specs=[vmem] * (len(blocks) + len(lines) + len(gains)),
            out_specs=vmem,
            out_shape=jax.ShapeDtypeStruct((nbatch, total, wide), BF16),
            scratch_shapes=[pltpu.VMEM((16, INNER), F32)],
            compiler_params=pltpu.CompilerParams(vmem_limit_bytes=40 << 20),
            name="pack_small",
        )(*blocks, *lines, *gains)
    return packed.reshape(nbatch * total, wide)


def wide(tile, width):
    return jnp.concatenate([tile] * (width // LANE), axis=1)


def fold(value):
    parts = [value[:, at : at + LANE] for at in range(0, value.shape[1], LANE)]
    return functools.reduce(jnp.add, parts)


SCAN_WIDTH = 640
SCAN_PART = 384
UNROLL = 16


def scan_parts(width):
    return [(lo, min(width, lo + SCAN_PART)) for lo in range(0, width, SCAN_PART)]


def scan_specs(seqs, span, chan):
    pos = pl.BlockSpec((1, span, SCAN_WIDTH), lambda s, e: (s, 0, e))
    coef = pl.BlockSpec((1, span, STATE, LANE), lambda s, e: (s, 0, 0, 0))
    dec = pl.BlockSpec((STATE, SCAN_WIDTH), lambda s, e: (0, e))
    state = pl.BlockSpec((1, STATE, SCAN_WIDTH), lambda s, e: (s, 0, e))
    return pos, coef, dec, state


def scan_params():
    return pltpu.CompilerParams(vmem_limit_bytes=56 << 20)


def scan_cost(seqs, span, chan, ops):
    return pl.CostEstimate(flops=ops, bytes_accessed=seqs * span * chan, transcendentals=0)


def final_kernel(step_ref, xc_ref, b_ref, dec_ref, fin_ref, drive):
    span, width = step_ref.shape[1:]
    drive[...] = step_ref[0] * xc_ref[0]
    for lo, hi in scan_parts(width):
        dec = dec_ref[:, lo:hi]

        def body(i, h):
            for j in range(UNROLL):
                t = i * UNROLL + j
                f = jnp.exp2(step_ref[0, pl.ds(t, 1), lo:hi] * dec)
                h = f * h + drive[pl.ds(t, 1), lo:hi] * wide(b_ref[0, t], hi - lo)
            return h

        fin_ref[0, :, lo:hi] = lax.fori_loop(
            0, span // UNROLL, body, jnp.zeros((STATE, hi - lo), F32)
        )


def scan_final(steps, xc, bb, dec):
    seqs, span, chan = steps.shape
    pos, coef, decs, state = scan_specs(seqs, span, chan)
    return pl.pallas_call(
        final_kernel,
        grid=(seqs, chan // SCAN_WIDTH),
        in_specs=[pos, pos, coef, decs],
        out_specs=state,
        out_shape=jax.ShapeDtypeStruct((seqs, STATE, chan), F32),
        scratch_shapes=[pltpu.VMEM((span, SCAN_WIDTH), F32)],
        compiler_params=scan_params(),
        cost_estimate=scan_cost(seqs, span, chan, 6),
        name="scan_final",
    )(steps, xc, bb, dec)


def out_kernel(step_ref, xc_ref, b_ref, c_ref, dec_ref, entry_ref, y_ref, drive):
    span, width = step_ref.shape[1:]
    drive[...] = step_ref[0] * xc_ref[0]
    for lo, hi in scan_parts(width):
        dec = dec_ref[:, lo:hi]

        def body(i, h):
            rows = []
            for j in range(UNROLL):
                t = i * UNROLL + j
                f = jnp.exp2(step_ref[0, pl.ds(t, 1), lo:hi] * dec)
                h = f * h + drive[pl.ds(t, 1), lo:hi] * wide(b_ref[0, t], hi - lo)
                rows.append(jnp.sum(h * wide(c_ref[0, t], hi - lo), axis=0, keepdims=True))
            at = pl.multiple_of(i * UNROLL, UNROLL)
            y_ref[0, pl.ds(at, UNROLL), lo:hi] = jnp.concatenate(rows, axis=0)
            return h

        lax.fori_loop(0, span // UNROLL, body, entry_ref[0, :, lo:hi])


def scan_out_of(steps, xc, bb, cc, dec, entry):
    seqs, span, chan = steps.shape
    pos, coef, decs, state = scan_specs(seqs, span, chan)
    return pl.pallas_call(
        out_kernel,
        grid=(seqs, chan // SCAN_WIDTH),
        in_specs=[pos, pos, coef, coef, decs, state],
        out_specs=pos,
        out_shape=jax.ShapeDtypeStruct((seqs, span, chan), F32),
        scratch_shapes=[pltpu.VMEM((span, SCAN_WIDTH), F32)],
        compiler_params=scan_params(),
        cost_estimate=scan_cost(seqs, span, chan, 10),
        name="scan_out",
    )(steps, xc, bb, cc, dec, entry)


def adjoint_kernel(step_ref, gy_ref, c_ref, dec_ref, out_ref):
    span, width = step_ref.shape[1:]
    for lo, hi in scan_parts(width):
        dec = dec_ref[:, lo:hi]

        def body(i, g):
            for j in range(UNROLL):
                t = span - 1 - (i * UNROLL + j)
                f = jnp.exp2(step_ref[0, pl.ds(t, 1), lo:hi] * dec)
                g = f * (g + gy_ref[0, pl.ds(t, 1), lo:hi] * wide(c_ref[0, t], hi - lo))
            return g

        out_ref[0, :, lo:hi] = lax.fori_loop(
            0, span // UNROLL, body, jnp.zeros((STATE, hi - lo), F32)
        )


def scan_adjoint(steps, gy, cc, dec):
    seqs, span, chan = steps.shape
    pos, coef, decs, state = scan_specs(seqs, span, chan)
    return pl.pallas_call(
        adjoint_kernel,
        grid=(seqs, chan // SCAN_WIDTH),
        in_specs=[pos, pos, coef, decs],
        out_specs=state,
        out_shape=jax.ShapeDtypeStruct((seqs, STATE, chan), F32),
        compiler_params=scan_params(),
        cost_estimate=scan_cost(seqs, span, chan, 6),
        name="scan_adjoint",
    )(steps, gy, cc, dec)


def back_kernel(
    step_ref, xc_ref, gy_ref, b_ref, c_ref, dec_ref, entry_ref, arrive_ref,
    dxc_ref, dstep_ref, db_ref, dc_ref, ddec_ref, drive, hs, fs,
):
    span, width = step_ref.shape[1:]
    drive[...] = step_ref[0] * xc_ref[0]

    @pl.when(pl.program_id(1) == 0)
    def _():
        db_ref[...] = jnp.zeros_like(db_ref)
        dc_ref[...] = jnp.zeros_like(dc_ref)

    for lo, hi in scan_parts(width):
        n = hi - lo
        dec = dec_ref[:, lo:hi]

        def ahead(i, h):
            for j in range(UNROLL):
                t = i * UNROLL + j
                f = jnp.exp2(step_ref[0, pl.ds(t, 1), lo:hi] * dec)
                hs[t, :, :n] = h
                fs[t, :, :n] = f
                h = f * h + drive[pl.ds(t, 1), lo:hi] * wide(b_ref[0, t], n)
            return h

        last = lax.fori_loop(0, span // UNROLL, ahead, entry_ref[0, :, lo:hi])

        def back(i, carry):
            g, h, ddec = carry
            weighted, along = [], []
            for j in range(UNROLL):
                t = span - 1 - (i * UNROLL + j)
                gy = gy_ref[0, pl.ds(t, 1), lo:hi]
                g = g + gy * wide(c_ref[0, t], n)
                dc_ref[0, t] += fold(gy * h)
                db_ref[0, t] += fold(g * drive[pl.ds(t, 1), lo:hi])
                weighted.append(jnp.sum(g * wide(b_ref[0, t], n), axis=0, keepdims=True))
                g = g * fs[t, :, :n]
                h = hs[t, :, :n]
                m = g * h
                along.append(jnp.sum(m * dec, axis=0, keepdims=True))
                ddec = ddec + m * step_ref[0, pl.ds(t, 1), lo:hi]
            at = pl.multiple_of(span - (i + 1) * UNROLL, UNROLL)
            w8 = jnp.concatenate(weighted[::-1], axis=0)
            m8 = jnp.concatenate(along[::-1], axis=0)
            dxc_ref[0, pl.ds(at, UNROLL), lo:hi] = w8 * step_ref[0, pl.ds(at, UNROLL), lo:hi]
            dstep_ref[0, pl.ds(at, UNROLL), lo:hi] = (
                m8 * LN2 + w8 * xc_ref[0, pl.ds(at, UNROLL), lo:hi]
            )
            return g, h, ddec

        start = (arrive_ref[0, :, lo:hi], last, jnp.zeros((STATE, n), F32))
        ddec_ref[0, :, lo:hi] = lax.fori_loop(0, span // UNROLL, back, start)[2]


def scan_back(steps, xc, gy, bb, cc, dec, entry, arrive):
    seqs, span, chan = steps.shape
    pos, coef, decs, state = scan_specs(seqs, span, chan)
    by_pos = jax.ShapeDtypeStruct((seqs, span, chan), F32)
    by_coef = jax.ShapeDtypeStruct((seqs, span, STATE, LANE), F32)
    return pl.pallas_call(
        back_kernel,
        grid=(seqs, chan // SCAN_WIDTH),
        in_specs=[pos, pos, pos, coef, coef, decs, state, state],
        out_specs=[pos, pos, coef, coef, state],
        out_shape=[by_pos, by_pos, by_coef, by_coef, jax.ShapeDtypeStruct((seqs, STATE, chan), F32)],
        scratch_shapes=[pltpu.VMEM((span, SCAN_WIDTH), F32)]
        + [pltpu.VMEM((span, STATE, SCAN_PART), F32)] * 2,
        compiler_params=scan_params(),
        cost_estimate=scan_cost(seqs, span, chan, 24),
        name="scan_back",
    )(steps, xc, gy, bb, cc, dec, entry, arrive)


def attend_mask(place_ref, mask):
    span = mask.shape[0]
    row = lax.broadcasted_iota(jnp.int32, (span, span), 0) + place_ref[0]
    col = lax.broadcasted_iota(jnp.int32, (span, span), 1)
    for at in range(mask.shape[1] // span):
        apart = row - (col + place_ref[at])
        allowed = (apart >= 0) & (apart < WINDOW)
        mask[:, at * span : (at + 1) * span] = jnp.where(allowed, 0.0, -1e30)


def first_step():
    return (pl.program_id(0) == 0) & (pl.program_id(1) == 0)


def scores_of(q, k):
    return lax.dot_general(q, k, (((1,), (1,)), ((), ())), preferred_element_type=F32)


QWIDE = -(-GROUP * HD // LANE) * LANE
KWIDE = -(-KV * HD // LANE) * LANE


def heads_in(k_refs, v_refs, k_all, v_all):
    span, at = v_refs[0].shape[2], 0
    for k_ref, v_ref in zip(k_refs, v_refs):
        for i in range(v_ref.shape[0]):
            v_all[at : at + span, :] = v_ref[i, 0]
            for h in range(KV):

                @pl.when(pl.program_id(1) == h)
                def _(k_ref=k_ref, i=i, at=at, h=h):
                    k_all[at : at + span, :] = k_ref[i, 0, :, h * HD : (h + 1) * HD]

            at += span


def attend_kernel(n, place_ref, q_ref, *refs):
    k_refs, v_refs, (out_ref, lse_ref, mask, k_all, v_all) = refs[:n], refs[n : 2 * n], refs[2 * n :]
    pl.when(first_step())(lambda: attend_mask(place_ref, mask))
    heads_in(k_refs, v_refs, k_all, v_all)
    for g in range(GROUP):
        s = scores_of(q_ref[0, :, g * HD : (g + 1) * HD], k_all[...]) + mask[...]
        peak = jnp.max(s, axis=-1, keepdims=True)
        e = jnp.exp(s - peak)
        total = jnp.sum(e, axis=-1, keepdims=True)
        lse_ref[0, :, g : g + 1] = peak + jnp.log(total)
        mixed = jnp.dot(e.astype(BF16), v_all[...], preferred_element_type=F32)
        out_ref[0, :, g * VHEAD : (g + 1) * VHEAD] = mixed / total


def attend_specs(span, kvs):
    q = pl.BlockSpec((1, span, QWIDE), lambda s, h: (s, 0, h))
    ks = [pl.BlockSpec((kv.shape[0], 1, span, KWIDE), lambda s, h: (0, s, 0, 0)) for kv in kvs]
    vs = [
        pl.BlockSpec((kv.shape[0], 1, span, VHEAD), lambda s, h: (0, s, 0, KWIDE // VHEAD + h))
        for kv in kvs
    ]
    out = pl.BlockSpec((1, span, GROUP * VHEAD), lambda s, h: (s, 0, h))
    lse = pl.BlockSpec((1, span, LANE), lambda s, h: (s, 0, h))
    length = span * sum(kv.shape[0] for kv in kvs)
    held = [
        pltpu.VMEM((span, length), F32),
        pltpu.VMEM((length, HD), BF16),
        pltpu.VMEM((length, VHEAD), BF16),
    ]
    return [pl.BlockSpec(memory_space=pltpu.SMEM), q] + ks + vs, q, out, lse, length, held


def attend(place_of, q, kvs):
    seqs, span, _ = q.shape
    ins, _, out, lse, length, held = attend_specs(span, kvs)
    cells = seqs * HEADS * span * length
    return pl.pallas_call(
        functools.partial(attend_kernel, len(kvs)),
        grid=(seqs, KV),
        in_specs=ins,
        out_specs=[out, lse],
        out_shape=[
            jax.ShapeDtypeStruct((seqs, span, INNER), F32),
            jax.ShapeDtypeStruct((seqs, span, KV * LANE), F32),
        ],
        scratch_shapes=held,
        compiler_params=pltpu.CompilerParams(vmem_limit_bytes=50 << 20),
        cost_estimate=pl.CostEstimate(flops=1, bytes_accessed=cells // 8, transcendentals=0),
        name="attend",
    )(place_of, q, *kvs, *kvs)


def attend_back_kernel(n, place_ref, q_ref, *refs):
    k_refs, v_refs, refs = refs[:n], refs[n : 2 * n], refs[2 * n :]
    lse_ref, o_ref, do_ref, dq_ref, dk_ref, dv_ref, mask, k_all, v_all, dk_sum, dv_sum = refs
    pl.when(first_step())(lambda: attend_mask(place_ref, mask))
    heads_in(k_refs, v_refs, k_all, v_all)
    k, v = k_all[...], v_all[...]
    for g in range(GROUP):
        q = q_ref[0, :, g * HD : (g + 1) * HD]
        do = do_ref[0, :, g * VHEAD : (g + 1) * VHEAD]
        o = o_ref[0, :, g * VHEAD : (g + 1) * VHEAD]
        s = scores_of(q, k) + mask[...]
        p = jnp.exp(s - lse_ref[0, :, g : g + 1])
        dp = scores_of(do, v)
        ds = (p * (dp - jnp.sum(do.astype(F32) * o, axis=-1, keepdims=True))).astype(BF16)
        dq = jnp.dot(ds, k, preferred_element_type=F32).astype(BF16)
        dq_ref[0, :, g * HD : (g + 1) * HD] = dq * jnp.asarray(HD**-0.5, BF16)
        dv = lax.dot_general(do, p.astype(BF16), (((0,), (0,)), ((), ())), preferred_element_type=F32)
        dk = lax.dot_general(q, ds, (((0,), (0,)), ((), ())), preferred_element_type=F32)
        if g == 0:
            dk_sum[...] = dk
            dv_sum[...] = dv
        else:
            dk_sum[...] += dk
            dv_sum[...] += dv
    if QWIDE > GROUP * HD:
        dq_ref[0, :, GROUP * HD :] = jnp.zeros((dq_ref.shape[1], QWIDE - GROUP * HD), BF16)
    dv_ref[0] = dv_sum[...].T.astype(BF16)
    dk = dk_sum[...].T.astype(BF16)

    @pl.when(pl.program_id(1) == 0)
    def _():
        dk_ref[...] = jnp.zeros_like(dk_ref)

    for h in range(KV):

        @pl.when(pl.program_id(1) == h)
        def _(h=h):
            dk_ref[0, :, h * HD : (h + 1) * HD] = dk


def attend_back(place_of, q, kvs, lse_in, o, do):
    seqs, span, _ = q.shape
    ins, qs, out, lse, length, held = attend_specs(span, kvs)
    cells = seqs * HEADS * span * length
    return pl.pallas_call(
        functools.partial(attend_back_kernel, len(kvs)),
        grid=(seqs, KV),
        in_specs=ins + [lse, out, out],
        out_specs=[
            qs,
            pl.BlockSpec((1, length, KWIDE), lambda s, h: (s, 0, 0)),
            pl.BlockSpec((1, length, VHEAD), lambda s, h: (s, 0, h)),
        ],
        out_shape=[
            jax.ShapeDtypeStruct(q.shape, BF16),
            jax.ShapeDtypeStruct((seqs, length, KWIDE), BF16),
            jax.ShapeDtypeStruct((seqs, length, KV * VHEAD), BF16),
        ],
        scratch_shapes=held + [pltpu.VMEM((HD, length), F32), pltpu.VMEM((VHEAD, length), F32)],
        compiler_params=pltpu.CompilerParams(vmem_limit_bytes=50 << 20),
        cost_estimate=pl.CostEstimate(flops=1, bytes_accessed=cells // 8, transcendentals=0),
        name="attend_back",
    )(place_of, q, *kvs, *kvs, lse_in, o, do)


def rms_scale(value):
    return lax.rsqrt(jnp.mean(value * value, axis=-1, keepdims=True) + EPS)


def norm_back(value, scale, upstream):
    return scale * upstream - value * scale**3 * jnp.mean(upstream * value, axis=-1, keepdims=True)


def silu_pair(value):
    sigma = jax.nn.sigmoid(value)
    return (value * sigma, sigma * (1.0 + value * (1.0 - sigma)))


def matmul(left, right):
    return jnp.dot(left, right, preferred_element_type=F32)


def matmul_back(left, right):
    return lax.dot_general(left, right, (((1,), (1,)), ((), ())), preferred_element_type=F32)


def outer_sum(left, right):
    return lax.dot_general(left, right, (((0,), (0,)), ((), ())), preferred_element_type=F32)


def carried(states, sums, dec, later):
    mine = lax.axis_index("ctx")
    total = jnp.zeros(states[0].shape, F32)
    for r in range(1, lax.axis_size("ctx")):
        far = mine ^ r
        passed = jnp.zeros(sums[0].shape, F32)
        for q in range(1, lax.axis_size("ctx")):
            at = mine ^ q
            between = (at > mine) & (at < far) if later else (at < mine) & (at > far)
            passed = passed + jnp.where(between, sums[q], 0.0)
        reaches = far > mine if later else far < mine
        total = total + jnp.where(reaches, jnp.exp2(dec * passed) * states[r].astype(F32), 0.0)
    return total


def per_device(
    tokens,
    teacher,
    cotangent,
    valid,
    w_query,
    w_key,
    w_value,
    w_mixer,
    w_output,
    w_gate,
    w_up,
    w_down,
    w_select,
    w_step,
    log_decay,
    conv_taps,
    conv_bias,
    step_bias,
    skip_gain,
    beta_attn,
    beta_ssm,
    gain_first,
    gain_second,
):
    seqs, span, width = tokens.shape
    nctx, nbatch = lax.axis_size("ctx"), lax.axis_size("batch")
    rows = seqs * span
    scale = 1.0 / math.sqrt(HD)
    all_tokens = rows * nbatch * nctx
    order = [0]
    for bit in bits_of("ctx")[::-1]:
        order += [r ^ bit for r in order]
    place_of = jnp.stack([(lax.axis_index("ctx") ^ r) * span for r in order]).astype(jnp.int32)

    lines = jnp.concatenate(
        [w_step, log_decay, conv_taps]
        + [v[None] for v in (conv_bias, step_bias, skip_gain, beta_attn, beta_ssm)]
        + [w_select.T],
        axis=0,
    )
    n_lines, chan = lines.shape
    gains = jnp.stack([gain_first, gain_second])
    packed = jnp.concatenate(
        [lines, jnp.pad(gains, ((0, 0), (0, chan - gains.shape[1])))], axis=0
    )
    packed = jnp.pad(packed, ((0, -packed.shape[0] % 16), (0, -chan % (2 * LANE))))
    n_q, n_k, n_v, n_mixer = [w.shape[1] for w in (w_query, w_key, w_value, w_mixer)]
    ff = nctx * w_gate.shape[1]
    every, half = range(nctx), nctx // 2
    here = jnp.full((8, LANE), jnp.sum(valid.astype(F32)))
    shards = [w_query, w_key, w_value, w_mixer, w_output, w_gate, w_up, here]
    in_kv = pieces_of(1, n_k, every) + pieces_of(2, n_v, every, KWIDE)
    items = [
        packed,
        (in_kv, KWIDE + KV * VHEAD, True),
        (pieces_of(0, n_q, every, 0, GROUP * HD, QWIDE), KV * QWIDE, True),
        (pieces_of(3, n_mixer, range(half)), INNER, True),
        (pieces_of(3, n_mixer, range(half, nctx)), INNER, True),
        (pieces_of(4, w_output.shape[1], every), D, False),
        (
            pieces_of(5, w_gate.shape[1], every) + pieces_of(6, w_up.shape[1], every, ff),
            2 * ff,
            False,
        ),
        (pieces_of(7, LANE, every), nctx * LANE, True),
    ]
    program = (
        "c1 c2 c0 c7 l0 c1 c2 l1 c0 c7 c3 l2 l7 c5 c3 f0 c6 l3 l4 f1 f2 f7 e0 c5 c4 f3 c6 e1 e2 "
        "e7 c4 l6 f4 l5 e3 e4"
    )
    acts = {"c": "columns", "l": "launch", "f": "forward", "e": "last"}
    program = tuple((acts[word[0]], int(word[1:])) for word in program.split())
    f_packed, f_kv, f_q, f_conv, f_z, row_output, row_gate_up, counts = gather_all(
        shards, items, program, 0
    )
    f_kv, f_q, f_conv, f_z = [v.reshape(-1, v.shape[2]) for v in (f_kv, f_q, f_conv, f_z)]
    count = jnp.sum(counts[:, 0, ::LANE])
    get_output, get_gate_up = Gather(row_output), Gather(row_gate_up)
    get_down = Gather(None, w_down)
    f_vectors = f_packed[:, :n_lines, :chan].transpose(1, 0, 2).reshape(n_lines, nbatch * chan)
    f_select = f_vectors[RANK + STATE + CONV + 5 :].T
    f_gains = f_packed[:, n_lines : n_lines + 2, : gains.shape[1]]
    f_gains = f_gains.transpose(1, 0, 2).reshape(2, -1)

    f_step = f_vectors[:RANK]
    f_decay = f_vectors[RANK : RANK + STATE].astype(F32)
    taps = f_vectors[RANK + STATE : RANK + STATE + CONV].astype(F32)
    f_conv_bias, f_step_bias, skip, beta_a, beta_s = [
        f_vectors[RANK + STATE + CONV + i].astype(F32) for i in range(5)
    ]
    gain_one, gain_two = f_gains[0].astype(F32), f_gains[1].astype(F32)
    decay = -jnp.exp(f_decay)
    dec = decay * LOG2E

    get_gate_up.step()
    x_flat = tokens.reshape(rows, D).astype(F32)
    scale1 = rms_scale(x_flat)
    normed1 = (x_flat * scale1 * gain_one).astype(BF16)
    conv_in = matmul(normed1, f_conv).astype(BF16).reshape(seqs, span, INNER)
    rim = shift(conv_in[:, span - (CONV - 1) :], "ctx", 1, False)
    conv_in, then1 = hold([], conv_in, normed1)
    kv_own = matmul(then1, f_kv).astype(BF16).reshape(seqs, span, KWIDE + KV * VHEAD)
    rim, kv_own, then1 = hold([], rim, kv_own, then1)
    get_kv = FromCtx(kv_own)
    get_kv.step()
    q_heads = (matmul(then1, f_q) * scale).astype(BF16).reshape(seqs, span, KV * QWIDE)
    gate_z = matmul(then1, f_z).reshape(seqs, span, INNER)
    extended = jnp.concatenate([rim, conv_in], axis=1).astype(F32)
    pre_conv = f_conv_bias + sum((taps[tap] * extended[:, tap : tap + span] for tap in range(CONV)))
    conv_out, conv_slope = silu_pair(pre_conv)

    conv_low = conv_out.reshape(rows, INNER).astype(BF16)
    projected = matmul(conv_low, f_select)
    rank_low = projected[:, :RANK].astype(BF16)
    coefs = projected[:, RANK:].reshape(seqs, span, 2, STATE, 1)
    bb = jnp.broadcast_to(coefs[:, :, 0], (seqs, span, STATE, LANE))
    cc = jnp.broadcast_to(coefs[:, :, 1], (seqs, span, STATE, LANE))
    step_pre = matmul(rank_low, f_step) + f_step_bias
    steps = jax.nn.softplus(step_pre).reshape(seqs, span, INNER)
    step_sums = jnp.sum(steps, axis=1, keepdims=True)
    steps, step_sums = hold([get_gate_up], steps, step_sums)
    get_gate_up.step()
    get_output.step()
    get_down.step()
    final = scan_final(steps, conv_out, bb, dec)
    final = hold([get_kv], final)
    get_kv.step()

    sums_high = step_sums.astype(BF16)
    sums_low = (step_sums - sums_high.astype(F32)).astype(BF16)
    get_state = FromCtx(jnp.concatenate([final.astype(BF16), sums_high, sums_low], axis=1))
    get_state.step()
    get_down.step()
    q_heads = hold([get_state, get_gate_up], q_heads)
    get_state.step()
    f_gate, f_up = hold([get_state, get_output, get_down], *get_gate_up.whole(2, ff, ff))
    get_output.step()
    get_down.step()

    states = get_state.finish()
    all_sums = {
        r: v[:, STATE : STATE + 1].astype(F32) + v[:, STATE + 1 :].astype(F32)
        for r, v in states.items()
    }
    entry = carried({r: v[:, :STATE] for r, v in states.items()}, all_sums, dec, False)
    scan_out = scan_out_of(steps, conv_out, bb, cc, dec, entry)
    scan_out = hold([get_kv, get_output, get_down], scan_out)
    get_down.step()
    get_kv.finish()
    kvs = list(get_kv.live.values())
    attn, lse = attend(place_of, q_heads, kvs)
    attn = attn.reshape(rows, INNER)
    attn = hold([get_down], attn)
    (f_output,) = get_output.whole(1, D)

    gate_act, gate_slope = silu_pair(gate_z)
    pre_gate = scan_out + skip * conv_out
    ssm_flat = (pre_gate * gate_act).reshape(rows, INNER)
    attn_scale = rms_scale(attn)
    attn_norm = attn * attn_scale
    ssm_scale = rms_scale(ssm_flat)
    ssm_norm = ssm_flat * ssm_scale
    merged = (0.5 * (attn_norm * beta_a + ssm_norm * beta_s)).astype(BF16)
    hidden1 = x_flat + matmul(merged, f_output)

    scale2 = rms_scale(hidden1)
    normed2 = (hidden1 * scale2 * gain_two).astype(BF16)
    gate_pre = matmul(normed2, f_gate)
    up_pre = matmul(normed2, f_up)
    gate_act2, gate_slope2 = silu_pair(gate_pre)
    inner_ff = (gate_act2 * up_pre).astype(BF16)
    (f_down,) = get_down.whole(3, D)
    hidden2 = hidden1 + matmul(inner_ff, f_down)
    output = hidden2.astype(BF16).reshape(seqs, span, D)
    weight_rows = valid.reshape(rows, 1).astype(F32)
    diff = hidden2 - teacher.reshape(rows, D).astype(F32)
    loss_local = jnp.sum(weight_rows * diff * diff)

    seed = cotangent.reshape(rows, D).astype(F32) + all_tokens / count * weight_rows * diff
    seed_low = seed.astype(BF16)
    put_down = Scatter(inner_ff, seed_low, w_down.shape[1])
    put_down.step()
    put_down.fresh.clear()
    d_inner = matmul_back(seed_low, f_down)
    d_gate = (d_inner * up_pre * gate_slope2).astype(BF16)
    d_up = (d_inner * gate_act2).astype(BF16)
    d_gate, d_up = hold([], d_gate, d_up)

    put_down.step()
    put_gate = Scatter(normed2, d_gate, w_gate.shape[1])
    put_gate.step()
    put_up = Scatter(normed2, d_up)
    put_up.step()
    d_norm2 = matmul_back(d_gate, f_gate) + matmul_back(d_up, f_up)
    g_gain_second = jnp.sum(d_norm2 * hidden1 * scale2, axis=0, keepdims=True)
    d_hidden1 = seed + norm_back(hidden1, scale2, d_norm2 * gain_two)
    d_hidden1 = hold([put_down, put_gate, put_up], d_hidden1)

    put_down.step()
    put_gate.step()
    d_branch = d_hidden1.astype(BF16)
    put_output = Scatter(merged, d_branch)
    put_output.step()
    d_merged = matmul_back(d_branch, f_output)
    g_beta_attn = jnp.sum(0.5 * d_merged * attn_norm, axis=0, keepdims=True)
    g_beta_ssm = jnp.sum(0.5 * d_merged * ssm_norm, axis=0, keepdims=True)
    d_attn = norm_back(attn, attn_scale, 0.5 * d_merged * beta_a).astype(BF16)
    d_ssm = norm_back(ssm_flat, ssm_scale, 0.5 * d_merged * beta_s).reshape(seqs, span, INNER)
    d_pre_gate = d_ssm * gate_act
    d_gate_z = (d_ssm * pre_gate * gate_slope).reshape(rows, INNER).astype(BF16)
    g_skip = jnp.sum(d_pre_gate * conv_out, axis=(0, 1))[None]
    adjoint = scan_adjoint(steps, d_pre_gate, cc, dec)
    d_attn, d_pre_gate, d_gate_z, adjoint = hold(
        [put_down, put_gate, put_output], d_attn, d_pre_gate, d_gate_z, adjoint
    )

    put_down.step()
    put_gate.step()
    put_up.step()
    get_adjoint = FromCtx(adjoint.astype(BF16))
    get_adjoint.step()
    dq, dk, dv = attend_back(
        place_of,
        q_heads,
        kvs,
        lse,
        attn.reshape(seqs, span, INNER),
        d_attn.reshape(seqs, span, INNER),
    )
    dq, dk, dv = hold([put_down, put_gate, put_up, get_adjoint], dq, dk, dv)
    get_adjoint.step()
    put_gate.step()
    put_up.step()
    put_output.step()
    dq = dq.reshape(rows, KV * QWIDE)
    g_q = outer_sum(normed1, dq).astype(BF16)
    g_z = outer_sum(normed1, d_gate_z).astype(BF16)
    d_norm1 = matmul_back(dq, f_q) + matmul_back(d_gate_z, f_z)
    put_down.fresh = list(put_down.live)
    d_norm1, g_q, g_z = hold([get_adjoint, put_up, put_output, put_down], d_norm1, g_q, g_z)

    d_kv = jnp.concatenate([dk, dv], axis=-1).reshape(seqs, nctx, span, KWIDE + KV * VHEAD)
    put_kv = ToCtx({r: d_kv[:, i] for i, r in enumerate(order)})
    put_kv.step()
    put_down.step()
    put_output.step()
    arrive = carried(get_adjoint.finish(), all_sums, dec, True)
    g_drive, g_steps, g_b, g_c, grad_decay = scan_back(
        steps, conv_out, d_pre_gate, bb, cc, dec, entry, arrive
    )
    g_drive, g_steps, g_b, g_c = hold(
        [put_down, put_gate, put_output, put_kv], g_drive, g_steps, g_b, g_c
    )

    put_kv.step()
    d_step_pre = g_steps.reshape(rows, INNER) * jax.nn.sigmoid(step_pre)
    g_step_bias = jnp.sum(d_step_pre, axis=0, keepdims=True)
    d_step_low = d_step_pre.astype(BF16)
    d_rank = matmul_back(d_step_low, f_step)
    d_projected = jnp.concatenate(
        [d_rank] + [jnp.sum(g, axis=-1).reshape(rows, STATE) for g in (g_b, g_c)], axis=1
    ).astype(BF16)
    d_conv = (
        g_drive
        + d_pre_gate * skip
        + matmul_back(d_projected, f_select).reshape(seqs, span, INNER)
    )
    d_pre_conv = d_conv * conv_slope
    g_conv_bias = jnp.sum(d_pre_conv, axis=(0, 1))[None]
    g_taps = [
        jnp.sum(d_pre_conv * extended[:, tap : tap + span], axis=(0, 1))[None]
        for tap in range(CONV)
    ]
    d_extended = sum(
        (
            jnp.pad(taps[tap] * d_pre_conv, ((0, 0), (tap, CONV - 1 - tap), (0, 0)))
            for tap in range(CONV)
        )
    )
    back_rim = shift(d_extended[:, : CONV - 1].astype(BF16), "ctx", -1, False)
    d_conv_in = d_extended[:, CONV - 1 :].at[:, span - (CONV - 1) :].add(back_rim.astype(F32))
    put_gate.fresh = list(put_gate.live)
    d_conv_in = hold([put_kv, put_gate], d_conv_in.reshape(rows, INNER).astype(BF16))
    put_gate.step()

    d_kv_own = put_kv.result().astype(BF16).reshape(rows, KWIDE + KV * VHEAD)
    d_norm1 = d_norm1 + matmul_back(d_kv_own, f_kv) + matmul_back(d_conv_in, f_conv)
    g_gain_first = jnp.sum(d_norm1 * x_flat * scale1, axis=0, keepdims=True)
    d_tokens = d_hidden1 + norm_back(x_flat, scale1, d_norm1 * gain_one)
    tokens_grad = d_tokens.astype(BF16).reshape(seqs, span, D)
    g_conv = outer_sum(normed1, d_conv_in).astype(BF16)
    g_kv = outer_sum(normed1, d_kv_own).astype(BF16)

    pad_rank, pad_sel = -RANK % 16, -(RANK + 2 * STATE) % 16
    g_step = outer_sum(jnp.pad(rank_low, ((0, 0), (0, pad_rank))), d_step_low)
    g_select = outer_sum(jnp.pad(d_projected, ((0, 0), (0, pad_sel))), conv_low)
    own_gain = D // nbatch
    at_sel = RANK + pad_rank
    at_dec = at_sel + RANK + 2 * STATE + pad_sel
    at_few = at_dec + STATE

    small = pack_small(
        [g_step, g_select, jnp.sum(grad_decay, axis=0) * decay],
        g_taps + [g_conv_bias, g_step_bias, g_skip, g_beta_attn, g_beta_ssm],
        [g_gain_first, g_gain_second],
    )
    small = hold([put_gate], small)
    lates = [put_output.blocks(w_output.shape[1]), put_up.blocks(w_up.shape[1])]
    terms = [g_conv, g_z, g_q, g_kv, small]
    items = [items[3][0], items[4][0], items[2][0], items[1][0], ()]
    program = "b4 b3 l0 l1 b2 b1 b0 m0 f4 f3 m1 f2 f1 s4 m2 f0 s3 t4 m3 s2 t3 p1 p2 m4 t2 p0 s1 e4 m5 t1 s0 "
    program += "t0 p3 e5 e6 e1 e2 e0 e3"
    program = tuple((word[0], int(word[1:])) for word in program.split())
    (r_down,), (r_gate,) = put_down.result(), put_gate.result()
    r_query, r_key, r_value, r_mixer, small, r_output, r_up, loss_sum = reduce_all(
        terms,
        jnp.full((8, LANE), loss_local),
        lates,
        items,
        (n_q, n_k, n_v, n_mixer),
        program,
        4,
    )
    loss_sum = loss_sum[0, 0]
    small = small[:, :chan]
    return (
        output,
        loss_sum / (count * D),
        tokens_grad,
        r_query,
        r_key,
        r_value,
        r_mixer,
        r_output,
        r_gate,
        r_up,
        r_down,
        small[at_sel : at_sel + RANK + 2 * STATE].T,
        small[:RANK],
        small[at_dec:at_few],
        small[at_few : at_few + CONV],
        *[small[at_few + CONV + i] for i in range(5)],
        *[small[at_few + CONV + 5 + i, :own_gain] for i in range(2)],
    )


def solution(mesh):
    by_pos = P("batch", "ctx", None)
    by_both = P("batch", "ctx")
    by_row, by_col, by_one = P("batch", None), P(None, "batch"), P("batch")
    weights = (by_both,) * 8 + (by_row,) + (by_col,) * 3 + (by_one,) * 7
    return jax.shard_map(
        per_device,
        mesh=mesh,
        in_specs=(by_pos, by_pos, by_pos, by_both) + weights,
        out_specs=(by_pos, P(), by_pos) + weights,
        check_vma=False,
    )
```
